32 devices in a mesh: groups: 2 (over x), ctx: 16 (over z, y, core).
Axes of the slice: x: 2, y: 2, z: 4, core: 2. Of those that a mesh axis runs over, the one named last changes fastest.
Arguments:
- key_cache: bfloat16 [4, 16384, 128], P(None, ('groups', 'ctx')), parts along dimension 1, may hold values from -16 to 16
- value_cache: bfloat16 [4, 16384, 128], P(None, ('groups', 'ctx')), parts along dimension 1, may hold values from -6 to 6
- init_centroids: bfloat16 [4, 1024, 128], replicated, may hold values from -6 to 6
- block_clusters: int32 [4, 128], P(None, 'groups'), parts along dimension 1, may hold values from 0 to 1023, as said below
- chosen_clusters: int32 [16, 4, 32], P('groups'), parts along dimension 0, may hold values from 0 to 1023, as said below
- request_positions: int32 [16], P('groups'), parts along dimension 0, may hold values from 1 to 8192, as said below
- queries: bfloat16 [16, 4, 8, 128], P('groups'), parts along dimension 0, may hold values from -640 to 640
Outputs:
- centroids: float32 [4, 2048, 128], P(None, ('groups', 'ctx')), parts along dimension 1
- attended: bfloat16 [16, 4, 8, 128], P('groups'), parts along dimension 0
The draws below stay inside these ranges and needn't reach their ends.
There are 2 independent parts, one for each index of `groups`. The reference program is written for one: setup_inputs(seed, part) draws one part's arguments, and reference() takes and returns one part's arrays. A program takes and returns all parts, laid end to end along the dimension named above; an argument that names none is the same for every part. Nothing has to cross between parts.
Inputs may be any that keep to these rules, and one draw needn't show every extreme that they name: `block_clusters`: the owner of cluster c is the ctx index c // 64. Over the 4 x 4 pairs (head, block) of one device's blocks, at most 2 pairs have clusters of one owner; 2 owners get exactly 2 pairs from every device. `chosen_clusters`: the 32 clusters of one request and head are distinct. `request_positions`: at least half of the requests see all 8192 tokens.
All inputs are finite; a program needn't handle non-finite values.
Results may differ from the reference program's by a relative error of at most 0.0078.
Values may be sent and summed in bfloat16 or wider, within the bound.
No kernel may reach another device: no remote copies, remote signals or barrier semaphores. Data moves between devices by JAX's collectives and lax.ppermute only.
A program may use at most 64 MiB of HBM per device.

```python
import math
import jax
import jax.numpy as jnp
from jax import lax

DH = 128
HEADS = 4
GROUP = 8
CLUSTERS = 1024
KSEL = 32
BLOCK = 128
REQUESTS = 8
TOK_DEV = 512
TOKENS = 8192
BLK_DEV = 4
NBLK = 64
PER_OWNER = 64
SLOTS = 2
HOT = 2


def shard_directions(key):
    shards = TOKENS // TOK_DEV
    direction = jax.random.normal(jax.random.fold_in(key, 32), (HEADS, shards, DH), jnp.float32)
    return direction / jnp.sqrt(jnp.sum(direction * direction, axis=2, keepdims=True))


def draw_key_cache(key, part):
    shards = TOKENS // TOK_DEV
    noise = jnp.clip(jax.random.normal(jax.random.fold_in(key, 31), (HEADS, TOKENS, DH), jnp.float32), -6.0, 6.0)
    direction = shard_directions(key)
    strength = jnp.ones((HEADS, shards, 1), jnp.float32) * 1.5
    common = jnp.repeat(direction * strength * math.sqrt(DH), TOK_DEV, axis=1)
    return jnp.clip(noise + common, -16.0, 16.0).astype(jnp.bfloat16)


def cluster_table(key):
    senders = NBLK // BLK_DEV
    entries = HEADS * BLK_DEV
    options = senders * SLOTS
    hot_order = jax.random.permutation(jax.random.fold_in(key, 11), senders)
    hot_rank = jnp.zeros((senders,), jnp.int32).at[hot_order].set(jnp.arange(senders, dtype=jnp.int32))
    is_hot = (hot_rank < HOT).astype(jnp.int32)
    slot_owner = jnp.arange(options, dtype=jnp.int32) // SLOTS

    def one_sender(sender):
        sender_key = jax.random.fold_in(jax.random.fold_in(key, 23), sender)
        noise = jax.random.randint(jax.random.fold_in(sender_key, 1), (options,), 0, 65536)
        ranking = is_hot[slot_owner] * 16777216 + noise * options + jnp.arange(options, dtype=jnp.int32)
        _, picked = lax.top_k(ranking, entries)
        shuffled = jax.random.permutation(jax.random.fold_in(sender_key, 2), picked)
        owners = slot_owner[shuffled]
        within = jax.random.randint(jax.random.fold_in(sender_key, 3), (entries,), 0, PER_OWNER)
        return (owners * PER_OWNER + within).reshape(HEADS, BLK_DEV)
    table = jax.vmap(one_sender)(jnp.arange(senders, dtype=jnp.int32))
    return jnp.transpose(table, (1, 0, 2)).reshape(HEADS, NBLK).astype(jnp.int32)


def draw_block_clusters(key, part):
    return cluster_table(key)


def request_plan(key):
    shards = TOKENS // TOK_DEV
    order = jax.random.permutation(jax.random.fold_in(key, 41), REQUESTS)
    ranks = jnp.zeros((REQUESTS,), jnp.int32).at[order].set(jnp.arange(REQUESTS, dtype=jnp.int32))
    full = ranks < REQUESTS // 2
    shard_order = jax.random.permutation(jax.random.fold_in(key, 42), shards).astype(jnp.int32)
    place = ranks[:, None, None] * (HEADS * GROUP) + jnp.arange(HEADS, dtype=jnp.int32)[None, :, None] * GROUP + jnp.arange(GROUP, dtype=jnp.int32)[None, None, :]
    target_shard = shard_order[place % shards]
    target_block = target_shard * BLK_DEV + jax.random.randint(jax.random.fold_in(key, 43), (REQUESTS, HEADS, GROUP), 0, BLK_DEV)
    return (ranks, full, target_shard, target_block.astype(jnp.int32))


def draw_request_positions(key, part):
    ranks, full, target_shard, target_block = request_plan(key)
    drawn = jax.random.randint(jax.random.fold_in(key, 44), (REQUESTS,), 1, TOKENS + 1)
    return jnp.where(full, TOKENS, drawn).astype(jnp.int32)


def draw_chosen_clusters(key, part):
    ranks, full, target_shard, target_block = request_plan(key)
    table = cluster_table(key)
    head_ids = jnp.arange(HEADS, dtype=jnp.int32)
    target_clusters = table[head_ids[None, :, None], target_block]
    cluster_ids = jnp.arange(CLUSTERS, dtype=jnp.int32)
    marked = jnp.any(target_clusters[..., None] == cluster_ids[None, None, None, :], axis=2) & full[:, None, None]
    extra = (ranks == REQUESTS // 2)[:, None, None] & (head_ids == 0)[None, :, None] & ((cluster_ids == 0) | (cluster_ids == CLUSTERS - 1))[None, None, :]
    marked = marked | extra
    noise = jax.random.randint(jax.random.fold_in(key, 45), (REQUESTS, HEADS, CLUSTERS), 0, 1024)
    ranking = marked.astype(jnp.int32) * 4194304 + noise * CLUSTERS + cluster_ids[None, None, :]
    _, picked = lax.top_k(ranking, KSEL)
    return picked.astype(jnp.int32)


def draw_queries(key, part):
    shape = (REQUESTS, HEADS, GROUP, DH)
    ranks, full, target_shard, target_block = request_plan(key)
    direction = shard_directions(key)
    head_ids = jnp.arange(HEADS, dtype=jnp.int32)
    aim = direction[head_ids[None, :, None], target_shard]
    reach = jax.random.uniform(jax.random.fold_in(key, 8), (REQUESTS, HEADS, GROUP, 1), minval=1.5, maxval=3.0)
    aligned = jnp.where(full[:, None, None, None], reach * math.sqrt(DH) * aim, 0.0)
    values_drawn = jnp.clip(jax.random.normal(jax.random.fold_in(key, 5), shape, jnp.float32), -6.0, 6.0)
    values_drawn = jnp.clip(values_drawn + aligned, -8.0, 8.0)
    order = jax.random.permutation(jax.random.fold_in(key, 6), REQUESTS)
    strong_rank = jnp.zeros((REQUESTS,), jnp.int32).at[order].set(jnp.arange(REQUESTS, dtype=jnp.int32))
    strong = (strong_rank < max(1, REQUESTS // 4)).reshape(REQUESTS, 1, 1, 1)
    factor = jnp.exp(jax.random.uniform(jax.random.fold_in(key, 7), (REQUESTS, 1, 1, 1), minval=math.log(40.0), maxval=math.log(80.0)))
    values_drawn = values_drawn * jnp.where(strong, factor, 1.0)
    return values_drawn.astype(jnp.bfloat16)


def shard_levels(own_key, extent, split, low, high):
    loudness, own = 1.0, jax.random.fold_in(own_key, 6)
    for dim, blocks in split:
        steps = jnp.exp(jax.random.uniform(jax.random.fold_in(own, dim), (blocks,), jnp.float32, low / len(split), high / len(split)))
        loudness = loudness * jnp.repeat(steps, extent[dim] // blocks).reshape([-1 if axis == dim else 1 for axis in range(len(extent))])
    return loudness


def normal_values(key, extent, scale, most, split=(), held_as=jnp.bfloat16):
    level = shard_levels(key, extent, split, -0.22, 0.18) if split else 1.0
    values = jax.random.normal(key, extent, jnp.float32) * scale * level
    return jnp.minimum(jnp.maximum(values, -most), most).astype(held_as)


def setup_inputs(seed: int = 0, part: int = 0) -> dict:
    streams_of = jax.random.split(jax.random.key(seed), 8)
    part_splits = jax.random.split(jax.random.fold_in(streams_of[7], part), 8)
    key_cache = draw_key_cache(jax.random.fold_in(jax.random.fold_in(streams_of[7], part), 71), part)
    value_cache = normal_values(part_splits[1], (HEADS, TOKENS, DH), 1.0, 6.0, ((1, 16),))
    init_centroids = normal_values(streams_of[2], (HEADS, CLUSTERS, DH), 1.0, 6.0)
    block_clusters = draw_block_clusters(jax.random.fold_in(jax.random.fold_in(streams_of[7], part), 71), part)
    chosen_clusters = draw_chosen_clusters(jax.random.fold_in(jax.random.fold_in(streams_of[7], part), 71), part)
    request_positions = draw_request_positions(jax.random.fold_in(jax.random.fold_in(streams_of[7], part), 71), part)
    queries = draw_queries(jax.random.fold_in(jax.random.fold_in(streams_of[7], part), 71), part)
    return dict(key_cache=key_cache, value_cache=value_cache, init_centroids=init_centroids, block_clusters=block_clusters, chosen_clusters=chosen_clusters, request_positions=request_positions, queries=queries)


SHARPNESS = 16.0
EPSILON = 1e-06
NEGATIVE = -1e+30

def to_unit(vectors):
    vectors = vectors.astype(jnp.float32)
    return vectors * lax.rsqrt(lax.optimization_barrier(jnp.mean(vectors * vectors, axis=-1, keepdims=True)) + EPSILON) * vectors.shape[-1] ** (-0.5)

def head_sums(keys_head, values_head, cents_head, with_values):
    token_count = keys_head.shape[0]
    block_rows = math.gcd(8192, token_count)
    turn_count = token_count // block_rows
    cluster_count = cents_head.shape[0]
    head_dim = keys_head.shape[1]

    def advance(running, turn_index):
        key_block = lax.dynamic_slice_in_dim(keys_head, turn_index * block_rows, block_rows, 0)
        unit_keys = to_unit(key_block).astype(jnp.bfloat16)
        cosine = jnp.dot(unit_keys, cents_head.T, preferred_element_type=jnp.float32)
        raised = jnp.exp(SHARPNESS * (cosine - 1.0))
        weights = (raised / lax.optimization_barrier(jnp.sum(raised, axis=1, keepdims=True))).astype(jnp.bfloat16)
        key_sums = running[0] + jnp.dot(weights.T, key_block, preferred_element_type=jnp.float32)
        if with_values:
            value_block = lax.dynamic_slice_in_dim(values_head, turn_index * block_rows, block_rows, 0)
            masses = running[1] + lax.optimization_barrier(jnp.sum(weights.astype(jnp.float32), axis=0))
            value_sums = running[2] + jnp.dot(weights.T, value_block, preferred_element_type=jnp.float32)
            return ((key_sums, masses, value_sums), None)
        return ((key_sums,), None)
    start = (jnp.zeros((cluster_count, head_dim), jnp.float32),)
    if with_values:
        start = (start[0], jnp.zeros((cluster_count,), jnp.float32), jnp.zeros((cluster_count, head_dim), jnp.float32))
    running, _ = lax.scan(advance, start, jnp.arange(turn_count, dtype=jnp.int32))
    return running

def decode_head(head, key_cache, value_cache, block_clusters, chosen_clusters, request_positions, queries, mean_keys, mean_values, log_mass):
    requests, group_size, head_dim = (queries.shape[0], queries.shape[2], queries.shape[3])
    token_count = key_cache.shape[1]
    cluster_count = mean_keys.shape[1]
    score_scale = head_dim ** (-0.5)
    flat_queries = queries[:, head].reshape(requests * group_size, head_dim)
    exact = jnp.dot(flat_queries, key_cache[head].T, preferred_element_type=jnp.float32).reshape(requests, group_size, token_count) * score_scale
    block_pick = jnp.any(chosen_clusters[:, head, :, None] == block_clusters[head][None, None, :], axis=1)
    token_pick = jnp.repeat(block_pick, BLOCK, axis=1) & (jnp.arange(token_count, dtype=jnp.int32)[None, :] < request_positions[:, None])
    summary = jnp.dot(flat_queries, mean_keys[head].T, preferred_element_type=jnp.float32).reshape(requests, group_size, cluster_count) * score_scale
    summary = summary + log_mass[head][None, None, :]
    summary_pick = jnp.logical_not(jnp.any(chosen_clusters[:, head, :, None] == jnp.arange(cluster_count, dtype=jnp.int32)[None, None, :], axis=1))
    exact_usable = token_pick[:, None, :]
    summary_usable = summary_pick[:, None, :]
    peak = jnp.maximum(lax.optimization_barrier(jnp.max(jnp.where(exact_usable, exact, NEGATIVE), axis=2)), lax.optimization_barrier(jnp.max(jnp.where(summary_usable, summary, NEGATIVE), axis=2)))
    exact_prob = jnp.where(exact_usable, jnp.exp(exact - peak[..., None]), 0.0).astype(jnp.bfloat16)
    summary_prob = jnp.where(summary_usable, jnp.exp(summary - peak[..., None]), 0.0).astype(jnp.bfloat16)
    weight_sum = lax.optimization_barrier(jnp.sum(exact_prob.astype(jnp.float32), axis=2)) + lax.optimization_barrier(jnp.sum(summary_prob.astype(jnp.float32), axis=2))
    weighted = jnp.dot(exact_prob.reshape(requests * group_size, token_count), value_cache[head], preferred_element_type=jnp.float32)
    weighted = weighted + jnp.dot(summary_prob.reshape(requests * group_size, cluster_count), mean_values[head], preferred_element_type=jnp.float32)
    weighted = weighted.reshape(requests, group_size, head_dim)
    return (weighted / weight_sum[..., None]).astype(jnp.bfloat16)

def reference(key_cache, value_cache, init_centroids, block_clusters, chosen_clusters, request_positions, queries):
    head_count = key_cache.shape[0]
    current = to_unit(init_centroids).astype(jnp.bfloat16)
    first_pass = jnp.stack([head_sums(key_cache[head], value_cache[head], current[head], False)[0] for head in range(head_count)])
    current = to_unit(first_pass).astype(jnp.bfloat16)
    second_pass = [head_sums(key_cache[head], value_cache[head], current[head], True) for head in range(head_count)]
    key_sums = jnp.stack([entry[0] for entry in second_pass])
    masses = jnp.stack([entry[1] for entry in second_pass])
    value_sums = jnp.stack([entry[2] for entry in second_pass])
    centroids = to_unit(key_sums)
    mean_keys = (key_sums / masses[..., None]).astype(jnp.bfloat16)
    mean_values = (value_sums / masses[..., None]).astype(jnp.bfloat16)
    log_mass = jnp.log(masses)
    attended = jnp.stack([decode_head(head, key_cache, value_cache, block_clusters, chosen_clusters, request_positions, queries, mean_keys, mean_values, log_mass) for head in range(head_count)], axis=1)
    return (centroids, attended)
```

```python
import functools
import math

import jax
import jax.numpy as jnp
from jax import lax
from jax.experimental import pallas as pl
from jax.experimental.pallas import tpu as pltpu
from jax.sharding import PartitionSpec as P

BLOCK = 128
SHARPNESS = 16.0
EPSILON = 1e-06
NEGATIVE = -1e30
F32 = jnp.float32
BF16 = jnp.bfloat16
VMEM_BYTES = 48 * 1024 * 1024
TILE = 256


def to_unit(vectors):
    vectors = vectors.astype(F32)
    return (
        vectors
        * lax.rsqrt(jnp.mean(vectors * vectors, axis=-1, keepdims=True) + EPSILON)
        * vectors.shape[-1] ** (-0.5)
    )


def dot_nt(left, right):
    return lax.dot_general(left, right, (((1,), (1,)), ((), ())), preferred_element_type=F32)


def call(kernel, outs, args, scratch=(), flops=0, scalars=0):
    in_specs = [pl.BlockSpec(memory_space=pltpu.SMEM)] * scalars
    in_specs += [pl.BlockSpec(memory_space=pltpu.VMEM)] * (len(args) - scalars)
    touched = sum(a.size * a.dtype.itemsize for a in (*args, *outs))
    return pl.pallas_call(
        kernel,
        out_shape=tuple(outs),
        in_specs=in_specs,
        out_specs=tuple(pl.BlockSpec(memory_space=pltpu.VMEM) for _ in outs),
        scratch_shapes=list(scratch),
        compiler_params=pltpu.CompilerParams(vmem_limit_bytes=VMEM_BYTES),
        cost_estimate=pl.CostEstimate(flops=flops, bytes_accessed=touched, transcendentals=0),
    )(*args)


def shape(dims, dtype):
    return jax.ShapeDtypeStruct(dims, dtype)


def fill_weights(unit_keys, pieces, raised_ref, weight_ref, first, mass_ref):
    tokens = unit_keys.shape[0]
    factor = SHARPNESS * math.log2(math.e)
    total = jnp.zeros((1, tokens), F32)
    row = 0
    tiles = []
    for piece in pieces:
        tile = min(TILE, piece.shape[0])
        for at in range(0, piece.shape[0], tile):
            raised = jnp.exp2(dot_nt(piece[at : at + tile, :], unit_keys) * factor)
            raised_ref[row : row + tile, :tokens] = raised
            total = total + jnp.sum(raised, axis=0, keepdims=True)
            tiles.append((row, tile))
            row += tile
    inverse = 1.0 / total
    for row, tile in tiles:
        weights = raised_ref[row : row + tile, :tokens] * inverse
        weight_ref[row : row + tile, first : first + tokens] = weights.astype(BF16)
        if mass_ref is not None:
            part = weights[:, :128]
            for at in range(128, tokens, 128):
                part = part + weights[:, at : at + 128]
            if first == 0:
                mass_ref[row : row + tile, :] = part
            else:
                mass_ref[row : row + tile, :] += part


def first_kernel(key_ref, cent_ref, sums_ref, unit_ref, raised_ref, weight_ref):
    unit_ref[...] = to_unit(cent_ref[...]).astype(BF16)
    keys = key_ref[...]
    fill_weights(to_unit(keys).astype(BF16), (unit_ref,), raised_ref, weight_ref, 0, None)
    rows = sums_ref.shape[0]
    tile = min(TILE, rows)
    for row in range(0, rows, tile):
        sums_ref[row : row + tile, :] = jnp.dot(
            weight_ref[row : row + tile, :], keys, preferred_element_type=F32
        )


def rest_kernel(count, *refs):
    key_refs, (unit_ref, sums_ref, keep_ref, send_ref, raised_ref, weight_ref) = (
        refs[:count],
        refs[count:],
    )
    first = 0
    for key_ref in key_refs:
        unit_keys = to_unit(key_ref[...]).astype(BF16)
        fill_weights(unit_keys, (unit_ref,), raised_ref, weight_ref, first, None)
        first += unit_keys.shape[0]
    keys = jnp.concatenate([key_ref[...] for key_ref in key_refs], axis=0)
    half = keep_ref.shape[0]
    tile = min(TILE, half)
    for row in range(0, half, tile):
        keep_ref[row : row + tile, :] = sums_ref[row : row + tile, :] + jnp.dot(
            weight_ref[row : row + tile, :], keys, preferred_element_type=F32
        )
    for row in range(half, 2 * half, tile):
        send_ref[row - half : row - half + tile, :] = (
            sums_ref[row : row + tile, :]
            + jnp.dot(weight_ref[row : row + tile, :], keys, preferred_element_type=F32)
        ).astype(BF16)


def packed_masses(row, lanes):
    count = row.shape[1]
    high = row.astype(BF16).astype(F32)
    low = row - high
    rows = []
    for part in (high, low):
        if count < lanes:
            rows.append(jnp.concatenate([part, jnp.zeros((1, lanes - count), F32)], axis=1))
        else:
            rows += [part[:, at : at + lanes] for at in range(0, count, lanes)]
    rows.append(jnp.zeros((16 - len(rows), lanes), F32))
    return jnp.concatenate(rows, axis=0).astype(BF16)


def unpacked_masses(block, count):
    block = block.astype(F32)
    lanes = block.shape[1]
    if count < lanes:
        return block[0:1, :count] + block[1:2, :count]
    rows = count // lanes
    return jnp.concatenate(
        [block[i : i + 1, :] + block[rows + i : rows + i + 1, :] for i in range(rows)], axis=1
    )


def second_kernel(count, *refs):
    key_refs, value_refs = refs[:count], refs[count : 2 * count]
    own_ref, other_ref, keep_ref, keep_mass_ref, send_ref, raised_ref, weight_ref, mass_ref = refs[
        2 * count :
    ]
    first = 0
    for key_ref in key_refs:
        unit_keys = to_unit(key_ref[...]).astype(BF16)
        fill_weights(unit_keys, (own_ref, other_ref), raised_ref, weight_ref, first, mass_ref)
        first += unit_keys.shape[0]
    pairs = jnp.concatenate(
        [jnp.concatenate([k[...], v[...]], axis=1) for k, v in zip(key_refs, value_refs)], axis=0
    )
    half, lanes = keep_ref.shape
    tile = min(TILE, half)
    for row in range(half, 2 * half, tile):
        send_ref[row - half : row - half + tile, :] = jnp.dot(
            weight_ref[row : row + tile, :], pairs, preferred_element_type=F32
        ).astype(BF16)
    for row in range(0, half, tile):
        keep_ref[row : row + tile, :] = jnp.dot(
            weight_ref[row : row + tile, :], pairs, preferred_element_type=F32
        )
    masses = jnp.sum(mass_ref[...].T, axis=0, keepdims=True)
    keep_mass_ref[...] = jnp.broadcast_to(masses[:, :half], keep_mass_ref.shape)
    send_ref[half:, :] = packed_masses(masses[:, half:], lanes)


def halve_kernel(keep_ref, mass_ref, recv_ref, keep_out_ref, mass_out_ref, send_ref):
    count, lanes = keep_ref.shape
    half = count // 2
    masses = mass_ref[0:1, :] + unpacked_masses(recv_ref[count:, :], count)
    keep_out_ref[...] = keep_ref[:half, :] + recv_ref[:half, :].astype(F32)
    mass_out_ref[...] = jnp.broadcast_to(masses[:, :half], mass_out_ref.shape)
    send_ref[:half, :] = (keep_ref[half:, :] + recv_ref[half:count, :].astype(F32)).astype(BF16)
    send_ref[half:, :] = packed_masses(masses[:, half:], lanes)


def packed_state(peak, weight_sum, weighted):
    rows, dim = weighted.shape
    lane = lax.broadcasted_iota(jnp.int32, (rows, dim), 1)
    return jnp.concatenate([weighted, jnp.where(lane < dim // 2, peak, weight_sum)], axis=1)


def softmax_part(scores, usable, values):
    peak = jnp.max(jnp.where(usable, scores, NEGATIVE), axis=1, keepdims=True)
    probability = jnp.where(usable, jnp.exp(scores - peak), 0.0).astype(BF16)
    weight_sum = jnp.sum(probability.astype(F32), axis=1, keepdims=True)
    return peak, weight_sum, jnp.dot(probability, values, preferred_element_type=F32)


def joined(former, latter):
    peak = jnp.maximum(former[0], latter[0])
    left, right = jnp.exp(former[0] - peak), jnp.exp(latter[0] - peak)
    return (
        peak,
        former[1] * left + latter[1] * right,
        former[2] * left + latter[2] * right,
    )


def unpacked_state(state):
    dim = state.shape[1] // 2
    return state[:, dim : dim + 1], state[:, dim + dim // 2 : dim + dim // 2 + 1], state[:, :dim]


def exact_kernel(count, *refs):
    key_refs, value_refs = refs[:count], refs[count : 2 * count]
    query_ref, limit_ref, out_ref = refs[2 * count :]
    queries = query_ref[...]
    rows, dim = queries.shape
    keys = jnp.concatenate([k[...] for k in key_refs], axis=0)
    values = jnp.concatenate([v[...] for v in value_refs], axis=0)
    scores = dot_nt(queries, keys) * dim ** (-0.5)
    lane = lax.broadcasted_iota(jnp.int32, (rows, BLOCK), 1)
    usable = jnp.concatenate(
        [
            jnp.where(lane < limit_ref[:, i : i + 1], 1.0, 0.0)
            for i in range(keys.shape[0] // BLOCK)
        ],
        axis=1,
    )
    out_ref[...] = packed_state(*softmax_part(scores, usable > 0.5, values))


def summary_kernel(
    keep_ref, mass_ref, recv_ref, query_ref, usable_ref, exact_ref, state_ref, cent_ref
):
    count, lanes = keep_ref.shape
    dim = lanes // 2
    masses = mass_ref[0:1, :] + unpacked_masses(recv_ref[count:, :], count)
    sums = keep_ref[...] + recv_ref[:count, :].astype(F32)
    cent_ref[...] = to_unit(sums[:, :dim])
    column = jnp.broadcast_to(masses, (dim, count)).T
    mean_keys = (sums[:, :dim] / column).astype(BF16)
    mean_values = (sums[:, dim:] / column).astype(BF16)
    scores = dot_nt(query_ref[...], mean_keys) * dim ** (-0.5) + jnp.log(masses)
    state = softmax_part(scores, usable_ref[...] > 0.5, mean_values)
    state_ref[...] = packed_state(*joined(unpacked_state(exact_ref[...]), state))


def in_order(flip, own_ref, recv_ref):
    own, recv = own_ref[...], recv_ref[...]
    return jnp.where(flip, recv, own), jnp.where(flip, own, recv)


def merge_kernel(flip_ref, own_ref, recv_ref, out_ref):
    former, latter = in_order(flip_ref[0] != 0, own_ref, recv_ref)
    out_ref[...] = packed_state(*joined(unpacked_state(former), unpacked_state(latter)))


def last_merge_kernel(scalar_ref, own_ref, recv_ref, cent_ref, *pack_refs):
    former, latter = in_order(scalar_ref[0] != 0, own_ref, recv_ref)
    _, weight_sum, weighted = joined(unpacked_state(former), unpacked_state(latter))
    attended = weighted / weight_sum
    own = scalar_ref[1]
    per_owner = cent_ref.shape[1]
    for step, pack_ref in enumerate(pack_refs):
        pack_ref[:per_owner, :] = cent_ref[own ^ step]
        pack_ref[per_owner:, :] = attended


def spread_kernel(scalar_ref, *refs):
    pack_refs, (cent_ref, out_ref) = refs[:-2], refs[-2:]
    own = scalar_ref[0]
    per_owner = cent_ref.shape[1]
    requests, _, group, dim = out_ref.shape
    for step, pack_ref in enumerate(pack_refs):
        cent_ref[own ^ step] = pack_ref[:per_owner, :]
        for r in range(requests):
            at = per_owner + r * group
            out_ref[r, own ^ step] = pack_ref[at : at + group, :].astype(BF16)


def body(
    key_cache,
    value_cache,
    init_centroids,
    block_clusters,
    chosen_clusters,
    request_positions,
    queries,
):
    devices = lax.axis_size("ctx")
    index = lax.axis_index("ctx").astype(jnp.int32)
    heads, tok_dev, dim = key_cache.shape
    clusters = init_centroids.shape[1]
    requests, _, group, _ = queries.shape
    per_owner = clusters // devices
    blk_dev = tok_dev // BLOCK
    spread = devices // heads
    levels = spread.bit_length() - 1
    if heads * spread != devices or 1 << levels != spread or heads & (heads - 1) or levels < 2:
        raise ValueError("unsupported mesh")
    head, rank = index // spread, index % spread
    half = clusters // 2
    rows = requests * group
    owned = heads * per_owner

    def over(array, bit):
        return lax.ppermute(array, "ctx", [(i, i ^ bit) for i in range(devices)])

    def pick(array, at, axis=0):
        return lax.dynamic_index_in_dim(array, at, axis, keepdims=False)

    keys = [pick(key_cache, head)]
    keys += [over(pick(key_cache, head ^ s), s * spread) for s in range(1, heads)]

    by_rank = pick(init_centroids, head).reshape(heads, spread, per_owner, dim)
    reverse = [int(format(r, f"0{levels}b")[::-1], 2) for r in range(spread)]
    cents = jnp.stack([pick(by_rank, rank ^ r, 1) for r in reverse]).reshape(clusters, dim)

    pass_flops = 4 * tok_dev * clusters * dim
    sums, unit_cents = call(
        first_kernel,
        [shape((clusters, dim), F32), shape((clusters, dim), BF16)],
        [keys[0], cents],
        [pltpu.VMEM((clusters, tok_dev), F32), pltpu.VMEM((clusters, tok_dev), BF16)],
        pass_flops,
    )
    keep, send = call(
        functools.partial(rest_kernel, heads - 1),
        [shape((half, dim), F32), shape((half, dim), BF16)],
        [*keys[1:], unit_cents, sums],
        [
            pltpu.VMEM((clusters, tok_dev), F32),
            pltpu.VMEM((clusters, (heads - 1) * tok_dev), BF16),
        ],
        pass_flops * (heads - 1),
    )

    arrived = lax.optimization_barrier((value_cache, *keys[1:]))
    later_values = arrived[0]
    values = [pick(value_cache, head)]
    values += [over(pick(later_values, head ^ s), s * spread) for s in range(1, heads)]

    for level in range(levels - 1):
        total = keep + over(send, 1 << level).astype(F32)
        if level < levels - 2:
            cut = total.shape[0] // 2
            keep, send = total[:cut], total[cut:].astype(BF16)
    rounded = total.astype(BF16)
    recv = over(rounded, 1 << (levels - 1))
    cut = rounded.shape[0] // 2
    recv = jnp.concatenate([recv[cut:], recv[:cut]])
    own_cents = to_unit(rounded.astype(F32) + recv.astype(F32)).astype(BF16)
    for level in range(levels - 2, 0, -1):
        own_cents = jnp.concatenate([own_cents, over(own_cents, 1 << level)])
    other_cents = over(own_cents, 1)

    keep, keep_mass, send = call(
        functools.partial(second_kernel, heads),
        [
            shape((half, 2 * dim), F32),
            shape((8, half), F32),
            shape((half + 16, 2 * dim), BF16),
        ],
        [*keys, *values, own_cents, other_cents],
        [
            pltpu.VMEM((clusters, tok_dev), F32),
            pltpu.VMEM((clusters, heads * tok_dev), BF16),
            pltpu.VMEM((clusters, 128), F32),
        ],
        pass_flops * heads * 3 // 2,
    )

    own_queries = pick(queries, head, 1).reshape(rows, dim)
    own_chosen = pick(chosen_clusters, head, 1)
    places = jnp.stack([head ^ s for s in range(heads)])[:, None] * spread + rank
    block_ids = (places * blk_dev + jnp.arange(blk_dev, dtype=jnp.int32)).reshape(-1)
    held = pick(pick(block_clusters, head).reshape(heads, spread, blk_dev), rank, 1)
    held = jnp.stack([pick(held, head ^ s) for s in range(heads)]).reshape(-1)
    picked = jnp.any(own_chosen[:, :, None] == held, axis=1)
    limits = jnp.where(
        picked, jnp.clip(request_positions[:, None] - block_ids * BLOCK, 0, BLOCK), 0
    )
    limits = jnp.repeat(limits, group, axis=0)
    owners = jnp.arange(heads, dtype=jnp.int32)[:, None] * spread + rank
    owned_ids = (owners * per_owner + jnp.arange(per_owner, dtype=jnp.int32)).reshape(-1)
    usable = jnp.all(own_chosen[:, :, None] != owned_ids, axis=1).astype(F32)
    usable = jnp.repeat(usable, group, axis=0)

    (exact,) = call(
        functools.partial(exact_kernel, heads),
        [shape((rows, 2 * dim), F32)],
        [*keys, *values, own_queries, limits],
        (),
        4 * rows * heads * tok_dev * dim,
    )

    for level in range(levels - 1):
        recv = over(send, 1 << level)
        count = keep.shape[0] // 2
        keep, keep_mass, send = call(
            halve_kernel,
            [
                shape((count, 2 * dim), F32),
                shape((8, count), F32),
                shape((count + 16, 2 * dim), BF16),
            ],
            [keep, keep_mass, recv],
        )
    recv = over(send, 1 << (levels - 1))
    state, centroids = call(
        summary_kernel,
        [shape((rows, 2 * dim), F32), shape((owned, dim), F32)],
        [keep, keep_mass, recv, own_queries, usable, exact],
        (),
        4 * rows * owned * dim,
    )
    for level in range(levels - 1):
        flip = ((index >> level) & 1).reshape(1)
        (state,) = call(
            merge_kernel,
            [shape((rows, 2 * dim), F32)],
            [flip, state, over(state, 1 << level)],
            scalars=1,
        )
    scalars = jnp.stack([(index >> (levels - 1)) & 1, head])
    packs = call(
        last_merge_kernel,
        [shape((per_owner + rows, dim), F32)] * heads,
        [
            scalars,
            state,
            over(state, 1 << (levels - 1)),
            centroids.reshape(heads, per_owner, dim),
        ],
        scalars=1,
    )
    packs = [packs[0]] + [over(packs[s], s * spread) for s in range(1, heads)]
    return call(
        spread_kernel,
        [shape((heads, per_owner, dim), F32), shape(queries.shape, BF16)],
        [head.reshape(1), *packs],
        scalars=1,
    )


def solution(mesh):
    placed = (
        P(None, ("groups", "ctx"), None),
        P(None, ("groups", "ctx"), None),
        P(),
        P(None, "groups"),
        P("groups", None, None),
        P("groups"),
        P("groups", None, None, None),
    )
    return jax.shard_map(
        body,
        mesh=mesh,
        in_specs=placed,
        out_specs=(P(None, ("groups", "ctx"), None), P("groups", None, None, None)),
        check_vma=False,
    )
```

```python
import functools
import math

import jax
import jax.numpy as jnp
from jax import lax
from jax.experimental import pallas as pl
from jax.experimental.pallas import tpu as pltpu
from jax.sharding import PartitionSpec as P

BLOCK = 128
SHARPNESS = 16.0
EPSILON = 1e-06
NEGATIVE = -1e30
F32 = jnp.float32
BF16 = jnp.bfloat16
VMEM_BYTES = 48 * 1024 * 1024
TILE = 256


def to_unit(vectors):
    vectors = vectors.astype(F32)
    return (
        vectors
        * lax.rsqrt(jnp.mean(vectors * vectors, axis=-1, keepdims=True) + EPSILON)
        * vectors.shape[-1] ** (-0.5)
    )


def dot_nt(left, right):
    return lax.dot_general(left, right, (((1,), (1,)), ((), ())), preferred_element_type=F32)


def call(kernel, outs, args, scratch=(), flops=0, scalars=0):
    in_specs = [pl.BlockSpec(memory_space=pltpu.SMEM)] * scalars
    in_specs += [pl.BlockSpec(memory_space=pltpu.VMEM)] * (len(args) - scalars)
    touched = sum(a.size * a.dtype.itemsize for a in (*args, *outs))
    return pl.pallas_call(
        kernel,
        out_shape=tuple(outs),
        in_specs=in_specs,
        out_specs=tuple(pl.BlockSpec(memory_space=pltpu.VMEM) for _ in outs),
        scratch_shapes=list(scratch),
        compiler_params=pltpu.CompilerParams(vmem_limit_bytes=VMEM_BYTES),
        cost_estimate=pl.CostEstimate(flops=flops, bytes_accessed=touched, transcendentals=0),
    )(*args)


def shape(dims, dtype):
    return jax.ShapeDtypeStruct(dims, dtype)


def fill_weights(unit_keys, pieces, raised_ref, weight_ref, first, mass_ref):
    tokens = unit_keys.shape[0]
    factor = SHARPNESS * math.log2(math.e)
    total = jnp.zeros((1, tokens), F32)
    row = 0
    tiles = []
    for piece in pieces:
        tile = min(TILE, piece.shape[0])
        for at in range(0, piece.shape[0], tile):
            raised = jnp.exp2(dot_nt(piece[at : at + tile, :], unit_keys) * factor)
            raised_ref[row : row + tile, :tokens] = raised
            total = total + jnp.sum(raised, axis=0, keepdims=True)
            tiles.append((row, tile))
            row += tile
    inverse = 1.0 / total
    for row, tile in tiles:
        weights = raised_ref[row : row + tile, :tokens] * inverse
        weight_ref[row : row + tile, first : first + tokens] = weights.astype(BF16)
        if mass_ref is not None:
            part = weights[:, :128]
            for at in range(128, tokens, 128):
                part = part + weights[:, at : at + 128]
            if first == 0:
                mass_ref[row : row + tile, :] = part
            else:
                mass_ref[row : row + tile, :] += part


def first_kernel(key_ref, cent_ref, sums_ref, unit_ref, raised_ref, weight_ref):
    unit_ref[...] = to_unit(cent_ref[...]).astype(BF16)
    keys = key_ref[...]
    fill_weights(to_unit(keys).astype(BF16), (unit_ref,), raised_ref, weight_ref, 0, None)
    rows = sums_ref.shape[0]
    tile = min(TILE, rows)
    for row in range(0, rows, tile):
        sums_ref[row : row + tile, :] = jnp.dot(
            weight_ref[row : row + tile, :], keys, preferred_element_type=F32
        )


def rest_kernel(count, *refs):
    key_refs, (unit_ref, sums_ref, keep_ref, send_ref, raised_ref, weight_ref) = (
        refs[:count],
        refs[count:],
    )
    first = 0
    for key_ref in key_refs:
        unit_keys = to_unit(key_ref[...]).astype(BF16)
        fill_weights(unit_keys, (unit_ref,), raised_ref, weight_ref, first, None)
        first += unit_keys.shape[0]
    keys = jnp.concatenate([key_ref[...] for key_ref in key_refs], axis=0)
    half = keep_ref.shape[0]
    tile = min(TILE, half)
    for row in range(0, half, tile):
        keep_ref[row : row + tile, :] = sums_ref[row : row + tile, :] + jnp.dot(
            weight_ref[row : row + tile, :], keys, preferred_element_type=F32
        )
    for row in range(half, 2 * half, tile):
        send_ref[row - half : row - half + tile, :] = (
            sums_ref[row : row + tile, :]
            + jnp.dot(weight_ref[row : row + tile, :], keys, preferred_element_type=F32)
        ).astype(BF16)


def packed_masses(row, lanes):
    count = row.shape[1]
    high = row.astype(BF16).astype(F32)
    low = row - high
    rows = []
    for part in (high, low):
        if count < lanes:
            rows.append(jnp.concatenate([part, jnp.zeros((1, lanes - count), F32)], axis=1))
        else:
            rows += [part[:, at : at + lanes] for at in range(0, count, lanes)]
    rows.append(jnp.zeros((16 - len(rows), lanes), F32))
    return jnp.concatenate(rows, axis=0).astype(BF16)


def unpacked_masses(block, count):
    block = block.astype(F32)
    lanes = block.shape[1]
    if count < lanes:
        return block[0:1, :count] + block[1:2, :count]
    rows = count // lanes
    return jnp.concatenate(
        [block[i : i + 1, :] + block[rows + i : rows + i + 1, :] for i in range(rows)], axis=1
    )


def second_kernel(count, *refs):
    key_refs, value_refs = refs[:count], refs[count : 2 * count]
    own_ref, other_ref, keep_ref, keep_mass_ref, send_ref, raised_ref, weight_ref, mass_ref = refs[
        2 * count :
    ]
    first = 0
    for key_ref in key_refs:
        unit_keys = to_unit(key_ref[...]).astype(BF16)
        fill_weights(unit_keys, (own_ref, other_ref), raised_ref, weight_ref, first, mass_ref)
        first += unit_keys.shape[0]
    pairs = jnp.concatenate(
        [jnp.concatenate([k[...], v[...]], axis=1) for k, v in zip(key_refs, value_refs)], axis=0
    )
    half, lanes = keep_ref.shape
    tile = min(TILE, half)
    for row in range(half, 2 * half, tile):
        send_ref[row - half : row - half + tile, :] = jnp.dot(
            weight_ref[row : row + tile, :], pairs, preferred_element_type=F32
        ).astype(BF16)
    for row in range(0, half, tile):
        keep_ref[row : row + tile, :] = jnp.dot(
            weight_ref[row : row + tile, :], pairs, preferred_element_type=F32
        )
    masses = jnp.sum(mass_ref[...].T, axis=0, keepdims=True)
    keep_mass_ref[...] = jnp.broadcast_to(masses[:, :half], keep_mass_ref.shape)
    send_ref[half:, :] = packed_masses(masses[:, half:], lanes)


def halve_kernel(keep_ref, mass_ref, recv_ref, keep_out_ref, mass_out_ref, send_ref):
    count, lanes = keep_ref.shape
    half = count // 2
    masses = mass_ref[0:1, :] + unpacked_masses(recv_ref[count:, :], count)
    keep_out_ref[...] = keep_ref[:half, :] + recv_ref[:half, :].astype(F32)
    mass_out_ref[...] = jnp.broadcast_to(masses[:, :half], mass_out_ref.shape)
    send_ref[:half, :] = (keep_ref[half:, :] + recv_ref[half:count, :].astype(F32)).astype(BF16)
    send_ref[half:, :] = packed_masses(masses[:, half:], lanes)


def packed_state(peak, weight_sum, weighted):
    rows, dim = weighted.shape
    lane = lax.broadcasted_iota(jnp.int32, (rows, dim), 1)
    return jnp.concatenate([weighted, jnp.where(lane < dim // 2, peak, weight_sum)], axis=1)


def softmax_part(scores, usable, values):
    peak = jnp.max(jnp.where(usable, scores, NEGATIVE), axis=1, keepdims=True)
    probability = jnp.where(usable, jnp.exp(scores - peak), 0.0).astype(BF16)
    weight_sum = jnp.sum(probability.astype(F32), axis=1, keepdims=True)
    return peak, weight_sum, jnp.dot(probability, values, preferred_element_type=F32)


def joined(former, latter):
    peak = jnp.maximum(former[0], latter[0])
    left, right = jnp.exp(former[0] - peak), jnp.exp(latter[0] - peak)
    return (
        peak,
        former[1] * left + latter[1] * right,
        former[2] * left + latter[2] * right,
    )


def unpacked_state(state):
    dim = state.shape[1] // 2
    return state[:, dim : dim + 1], state[:, dim + dim // 2 : dim + dim // 2 + 1], state[:, :dim]


def exact_kernel(count, *refs):
    key_refs, value_refs = refs[:count], refs[count : 2 * count]
    query_ref, limit_ref, out_ref = refs[2 * count :]
    queries = query_ref[...]
    rows, dim = queries.shape
    keys = jnp.concatenate([k[...] for k in key_refs], axis=0)
    values = jnp.concatenate([v[...] for v in value_refs], axis=0)
    scores = dot_nt(queries, keys) * dim ** (-0.5)
    lane = lax.broadcasted_iota(jnp.int32, (rows, BLOCK), 1)
    usable = jnp.concatenate(
        [
            jnp.where(lane < limit_ref[:, i : i + 1], 1.0, 0.0)
            for i in range(keys.shape[0] // BLOCK)
        ],
        axis=1,
    )
    out_ref[...] = packed_state(*softmax_part(scores, usable > 0.5, values))


def summary_kernel(
    keep_ref, mass_ref, recv_ref, query_ref, usable_ref, exact_ref, state_ref, cent_ref
):
    count, lanes = keep_ref.shape
    dim = lanes // 2
    masses = mass_ref[0:1, :] + unpacked_masses(recv_ref[count:, :], count)
    sums = keep_ref[...] + recv_ref[:count, :].astype(F32)
    cent_ref[...] = to_unit(sums[:, :dim])
    column = jnp.broadcast_to(masses, (dim, count)).T
    mean_keys = (sums[:, :dim] / column).astype(BF16)
    mean_values = (sums[:, dim:] / column).astype(BF16)
    scores = dot_nt(query_ref[...], mean_keys) * dim ** (-0.5) + jnp.log(masses)
    state = softmax_part(scores, usable_ref[...] > 0.5, mean_values)
    state_ref[...] = packed_state(*joined(unpacked_state(exact_ref[...]), state))


def in_order(flip, own_ref, recv_ref):
    own, recv = own_ref[...], recv_ref[...]
    return jnp.where(flip, recv, own), jnp.where(flip, own, recv)


def merge_kernel(flip_ref, own_ref, recv_ref, out_ref):
    former, latter = in_order(flip_ref[0] != 0, own_ref, recv_ref)
    out_ref[...] = packed_state(*joined(unpacked_state(former), unpacked_state(latter)))


def last_merge_kernel(scalar_ref, own_ref, recv_ref, cent_ref, *pack_refs):
    former, latter = in_order(scalar_ref[0] != 0, own_ref, recv_ref)
    _, weight_sum, weighted = joined(unpacked_state(former), unpacked_state(latter))
    attended = weighted / weight_sum
    own = scalar_ref[1]
    per_owner = cent_ref.shape[1]
    for step, pack_ref in enumerate(pack_refs):
        pack_ref[:per_owner, :] = cent_ref[own ^ step]
        pack_ref[per_owner:, :] = attended


def spread_kernel(scalar_ref, *refs):
    pack_refs, (cent_ref, out_ref) = refs[:-2], refs[-2:]
    own = scalar_ref[0]
    per_owner = cent_ref.shape[1]
    requests, _, group, dim = out_ref.shape
    for step, pack_ref in enumerate(pack_refs):
        cent_ref[own ^ step] = pack_ref[:per_owner, :]
        for r in range(requests):
            at = per_owner + r * group
            out_ref[r, own ^ step] = pack_ref[at : at + group, :].astype(BF16)


def body(
    key_cache,
    value_cache,
    init_centroids,
    block_clusters,
    chosen_clusters,
    request_positions,
    queries,
):
    devices = lax.axis_size("ctx")
    index = lax.axis_index("ctx").astype(jnp.int32)
    heads, tok_dev, dim = key_cache.shape
    clusters = init_centroids.shape[1]
    requests, _, group, _ = queries.shape
    per_owner = clusters // devices
    blk_dev = tok_dev // BLOCK
    spread = devices // heads
    levels = spread.bit_length() - 1
    if heads * spread != devices or 1 << levels != spread or heads & (heads - 1) or levels < 2:
        raise ValueError("unsupported mesh")
    bits = heads.bit_length() - 1
    head_masks = [s << 1 for s in range(heads)]
    rank_masks = [1] + [1 << (bits + level) for level in range(1, levels)]
    rank_masks[1] |= heads
    far = index // (2 * heads)
    head = (index // 2) % heads ^ (far % 2) * (heads // 2)
    rank = far * 2 + index % 2
    half = clusters // 2
    rows = requests * group
    owned = heads * per_owner

    def over(array, bit):
        return lax.ppermute(array, "ctx", [(i, i ^ bit) for i in range(devices)])

    def pick(array, at, axis=0):
        return lax.dynamic_index_in_dim(array, at, axis, keepdims=False)

    keys = [pick(key_cache, head)]
    keys += [over(pick(key_cache, head ^ s), head_masks[s]) for s in range(1, heads)]

    blocks = pick(init_centroids, head).reshape(spread // 4, 2, heads, 2, per_owner, dim)
    blocks = jnp.stack([blocks[:, 0], jnp.roll(blocks[:, 1], heads // 2, axis=1)], axis=1)
    by_rank = jnp.moveaxis(blocks.reshape(spread // 2, heads, 2, per_owner, dim), 2, 1)
    by_rank = by_rank.reshape(spread, heads, per_owner, dim)
    reverse = [int(format(r, f"0{levels}b")[::-1], 2) for r in range(spread)]
    cents = jnp.stack([pick(by_rank, rank ^ r) for r in reverse]).reshape(clusters, dim)

    pass_flops = 4 * tok_dev * clusters * dim
    sums, unit_cents = call(
        first_kernel,
        [shape((clusters, dim), F32), shape((clusters, dim), BF16)],
        [keys[0], cents],
        [pltpu.VMEM((clusters, tok_dev), F32), pltpu.VMEM((clusters, tok_dev), BF16)],
        pass_flops,
    )
    keep, send = call(
        functools.partial(rest_kernel, heads - 1),
        [shape((half, dim), F32), shape((half, dim), BF16)],
        [*keys[1:], unit_cents, sums],
        [
            pltpu.VMEM((clusters, tok_dev), F32),
            pltpu.VMEM((clusters, (heads - 1) * tok_dev), BF16),
        ],
        pass_flops * (heads - 1),
    )

    arrived = lax.optimization_barrier((value_cache, *keys[1:]))
    later_values = arrived[0]
    values = [pick(value_cache, head)]
    values += [over(pick(later_values, head ^ s), head_masks[s]) for s in range(1, heads)]

    for level in range(levels - 1):
        total = keep + over(send, rank_masks[level]).astype(F32)
        if level < levels - 2:
            cut = total.shape[0] // 2
            keep, send = total[:cut], total[cut:].astype(BF16)
    rounded = total.astype(BF16)
    recv = over(rounded, rank_masks[levels - 1])
    cut = rounded.shape[0] // 2
    recv = jnp.concatenate([recv[cut:], recv[:cut]])
    own_cents = to_unit(rounded.astype(F32) + recv.astype(F32)).astype(BF16)
    for level in range(levels - 2, 0, -1):
        own_cents = jnp.concatenate([own_cents, over(own_cents, rank_masks[level])])
    other_cents = over(own_cents, 1)

    keep, keep_mass, send = call(
        functools.partial(second_kernel, heads),
        [
            shape((half, 2 * dim), F32),
            shape((8, half), F32),
            shape((half + 16, 2 * dim), BF16),
        ],
        [*keys, *values, own_cents, other_cents],
        [
            pltpu.VMEM((clusters, tok_dev), F32),
            pltpu.VMEM((clusters, heads * tok_dev), BF16),
            pltpu.VMEM((clusters, 128), F32),
        ],
        pass_flops * heads * 3 // 2,
    )

    own_queries = pick(queries, head, 1).reshape(rows, dim)
    own_chosen = pick(chosen_clusters, head, 1)
    places = jnp.stack([index ^ mask for mask in head_masks])[:, None]
    block_ids = (places * blk_dev + jnp.arange(blk_dev, dtype=jnp.int32)).reshape(-1)
    held = pick(block_clusters, head).reshape(devices, blk_dev)
    held = jnp.stack([pick(held, index ^ mask) for mask in head_masks]).reshape(-1)
    picked = jnp.any(own_chosen[:, :, None] == held, axis=1)
    limits = jnp.where(
        picked, jnp.clip(request_positions[:, None] - block_ids * BLOCK, 0, BLOCK), 0
    )
    limits = jnp.repeat(limits, group, axis=0)
    owners = jnp.arange(heads, dtype=jnp.int32)[:, None] ^ (far % 2) * (heads // 2)
    owners = (far * heads + owners) * 2 + index % 2
    owned_ids = (owners * per_owner + jnp.arange(per_owner, dtype=jnp.int32)).reshape(-1)
    usable = jnp.all(own_chosen[:, :, None] != owned_ids, axis=1).astype(F32)
    usable = jnp.repeat(usable, group, axis=0)

    (exact,) = call(
        functools.partial(exact_kernel, heads),
        [shape((rows, 2 * dim), F32)],
        [*keys, *values, own_queries, limits],
        (),
        4 * rows * heads * tok_dev * dim,
    )

    for level in range(levels - 1):
        recv = over(send, rank_masks[level])
        count = keep.shape[0] // 2
        keep, keep_mass, send = call(
            halve_kernel,
            [
                shape((count, 2 * dim), F32),
                shape((8, count), F32),
                shape((count + 16, 2 * dim), BF16),
            ],
            [keep, keep_mass, recv],
        )
    recv = over(send, rank_masks[levels - 1])
    state, centroids = call(
        summary_kernel,
        [shape((rows, 2 * dim), F32), shape((owned, dim), F32)],
        [keep, keep_mass, recv, own_queries, usable, exact],
        (),
        4 * rows * owned * dim,
    )
    for level in range(levels - 1):
        flip = ((rank >> level) & 1).reshape(1)
        (state,) = call(
            merge_kernel,
            [shape((rows, 2 * dim), F32)],
            [flip, state, over(state, rank_masks[level])],
            scalars=1,
        )
    scalars = jnp.stack([(rank >> (levels - 1)) & 1, head])
    packs = call(
        last_merge_kernel,
        [shape((per_owner + rows, dim), F32)] * heads,
        [
            scalars,
            state,
            over(state, rank_masks[levels - 1]),
            centroids.reshape(heads, per_owner, dim),
        ],
        scalars=1,
    )
    packs = [packs[0]] + [over(packs[s], head_masks[s]) for s in range(1, heads)]
    return call(
        spread_kernel,
        [shape((heads, per_owner, dim), F32), shape(queries.shape, BF16)],
        [head.reshape(1), *packs],
        scalars=1,
    )


def solution(mesh):
    placed = (
        P(None, ("groups", "ctx"), None),
        P(None, ("groups", "ctx"), None),
        P(),
        P(None, "groups"),
        P("groups", None, None),
        P("groups"),
        P("groups", None, None, None),
    )
    return jax.shard_map(
        body,
        mesh=mesh,
        in_specs=placed,
        out_specs=(P(None, ("groups", "ctx"), None), P("groups", None, None, None)),
        check_vma=False,
    )
```

```python
import functools
import math

import jax
import jax.numpy as jnp
from jax import lax
from jax.experimental import pallas as pl
from jax.experimental.pallas import tpu as pltpu
from jax.sharding import PartitionSpec as P

BLOCK = 128
SHARPNESS = 16.0
EPSILON = 1e-06
NEGATIVE = -1e30
F32 = jnp.float32
BF16 = jnp.bfloat16
VMEM_BYTES = 48 * 1024 * 1024
TILE = 256


def to_unit(vectors):
    vectors = vectors.astype(F32)
    return (
        vectors
        * lax.rsqrt(jnp.mean(vectors * vectors, axis=-1, keepdims=True) + EPSILON)
        * vectors.shape[-1] ** (-0.5)
    )


def dot_nt(left, right):
    return lax.dot_general(left, right, (((1,), (1,)), ((), ())), preferred_element_type=F32)


def spanned(basis, number):
    return functools.reduce(lambda a, b: a ^ b, [m for j, m in enumerate(basis) if number >> j & 1], 0)


def duals(head_basis, rank_basis, devices):
    basis = [*head_basis, *rank_basis]
    found = [
        next(
            f
            for f in range(devices)
            if all((f & m).bit_count() % 2 == (j == k) for j, m in enumerate(basis))
        )
        for k in range(len(basis))
    ]
    return found[: len(head_basis)], found[len(head_basis) :]


def coordinates(number, masks):
    result = 0
    for place, mask in enumerate(masks):
        for bit in range(mask.bit_length()):
            if mask >> bit & 1:
                result = result ^ ((number >> bit & 1) << place)
    return result


def call(kernel, outs, args, scratch=(), flops=0, scalars=0):
    in_specs = [pl.BlockSpec(memory_space=pltpu.SMEM)] * scalars
    in_specs += [pl.BlockSpec(memory_space=pltpu.VMEM)] * (len(args) - scalars)
    touched = sum(a.size * a.dtype.itemsize for a in (*args, *outs))
    return pl.pallas_call(
        kernel,
        out_shape=tuple(outs),
        in_specs=in_specs,
        out_specs=tuple(pl.BlockSpec(memory_space=pltpu.VMEM) for _ in outs),
        scratch_shapes=list(scratch),
        compiler_params=pltpu.CompilerParams(vmem_limit_bytes=VMEM_BYTES),
        cost_estimate=pl.CostEstimate(flops=flops, bytes_accessed=touched, transcendentals=0),
    )(*args)


def shape(dims, dtype):
    return jax.ShapeDtypeStruct(dims, dtype)


def fill_weights(unit_keys, pieces, raised_ref, weight_ref, first, mass_ref):
    tokens = unit_keys.shape[0]
    factor = SHARPNESS * math.log2(math.e)
    total = jnp.zeros((1, tokens), F32)
    row = 0
    tiles = []
    for piece in pieces:
        tile = min(TILE, piece.shape[0])
        for at in range(0, piece.shape[0], tile):
            raised = jnp.exp2(dot_nt(piece[at : at + tile, :], unit_keys) * factor)
            raised_ref[row : row + tile, :tokens] = raised
            total = total + jnp.sum(raised, axis=0, keepdims=True)
            tiles.append((row, tile))
            row += tile
    inverse = 1.0 / total
    for row, tile in tiles:
        weights = raised_ref[row : row + tile, :tokens] * inverse
        weight_ref[row : row + tile, first : first + tokens] = weights.astype(BF16)
        if mass_ref is not None:
            part = weights[:, :128]
            for at in range(128, tokens, 128):
                part = part + weights[:, at : at + 128]
            if first == 0:
                mass_ref[row : row + tile, :] = part
            else:
                mass_ref[row : row + tile, :] += part


def first_kernel(
    order_ref, key_ref, cent_ref, sums_ref, unit_ref, cents_ref, raised_ref, weight_ref
):
    owners, per_owner, _ = cent_ref.shape
    for at in range(owners):
        cents_ref[at * per_owner : (at + 1) * per_owner, :] = cent_ref[order_ref[at]].astype(F32)
    unit_ref[...] = to_unit(cents_ref[...]).astype(BF16)
    keys = key_ref[...]
    fill_weights(to_unit(keys).astype(BF16), (unit_ref,), raised_ref, weight_ref, 0, None)
    rows = sums_ref.shape[0]
    tile = min(TILE, rows)
    for row in range(0, rows, tile):
        sums_ref[row : row + tile, :] = jnp.dot(
            weight_ref[row : row + tile, :], keys, preferred_element_type=F32
        )


def rest_kernel(count, *refs):
    key_refs, (unit_ref, sums_ref, keep_ref, send_ref, raised_ref, weight_ref) = (
        refs[:count],
        refs[count:],
    )
    first = 0
    for key_ref in key_refs:
        unit_keys = to_unit(key_ref[...]).astype(BF16)
        fill_weights(unit_keys, (unit_ref,), raised_ref, weight_ref, first, None)
        first += unit_keys.shape[0]
    keys = jnp.concatenate([key_ref[...] for key_ref in key_refs], axis=0)
    half = keep_ref.shape[0]
    tile = min(TILE, half)
    for row in range(0, half, tile):
        keep_ref[row : row + tile, :] = sums_ref[row : row + tile, :] + jnp.dot(
            weight_ref[row : row + tile, :], keys, preferred_element_type=F32
        )
    for row in range(half, 2 * half, tile):
        send_ref[row - half : row - half + tile, :] = (
            sums_ref[row : row + tile, :]
            + jnp.dot(weight_ref[row : row + tile, :], keys, preferred_element_type=F32)
        ).astype(BF16)


def packed_masses(row, lanes):
    count = row.shape[1]
    high = row.astype(BF16).astype(F32)
    low = row - high
    rows = []
    for part in (high, low):
        if count < lanes:
            rows.append(jnp.concatenate([part, jnp.zeros((1, lanes - count), F32)], axis=1))
        else:
            rows += [part[:, at : at + lanes] for at in range(0, count, lanes)]
    rows.append(jnp.zeros((16 - len(rows), lanes), F32))
    return jnp.concatenate(rows, axis=0).astype(BF16)


def unpacked_masses(block, count):
    block = block.astype(F32)
    lanes = block.shape[1]
    if count < lanes:
        return block[0:1, :count] + block[1:2, :count]
    rows = count // lanes
    return jnp.concatenate(
        [block[i : i + 1, :] + block[rows + i : rows + i + 1, :] for i in range(rows)], axis=1
    )


def second_kernel(count, *refs):
    key_refs, value_refs = refs[:count], refs[count : 2 * count]
    own_ref, other_ref, keep_ref, keep_mass_ref, send_ref, raised_ref, weight_ref, mass_ref = refs[
        2 * count :
    ]
    first = 0
    for key_ref in key_refs:
        unit_keys = to_unit(key_ref[...]).astype(BF16)
        fill_weights(unit_keys, (own_ref, other_ref), raised_ref, weight_ref, first, mass_ref)
        first += unit_keys.shape[0]
    pairs = jnp.concatenate(
        [jnp.concatenate([k[...], v[...]], axis=1) for k, v in zip(key_refs, value_refs)], axis=0
    )
    half, lanes = keep_ref.shape
    tile = min(TILE, half)
    for row in range(half, 2 * half, tile):
        send_ref[row - half : row - half + tile, :] = jnp.dot(
            weight_ref[row : row + tile, :], pairs, preferred_element_type=F32
        ).astype(BF16)
    for row in range(0, half, tile):
        keep_ref[row : row + tile, :] = jnp.dot(
            weight_ref[row : row + tile, :], pairs, preferred_element_type=F32
        )
    masses = jnp.sum(mass_ref[...].T, axis=0, keepdims=True)
    keep_mass_ref[...] = jnp.broadcast_to(masses[:, :half], keep_mass_ref.shape)
    send_ref[half:, :] = packed_masses(masses[:, half:], lanes)


def halve_kernel(keep_ref, mass_ref, recv_ref, keep_out_ref, mass_out_ref, send_ref):
    count, lanes = keep_ref.shape
    half = count // 2
    masses = mass_ref[0:1, :] + unpacked_masses(recv_ref[count:, :], count)
    keep_out_ref[...] = keep_ref[:half, :] + recv_ref[:half, :].astype(F32)
    mass_out_ref[...] = jnp.broadcast_to(masses[:, :half], mass_out_ref.shape)
    send_ref[:half, :] = (keep_ref[half:, :] + recv_ref[half:count, :].astype(F32)).astype(BF16)
    send_ref[half:, :] = packed_masses(masses[:, half:], lanes)


def packed_state(peak, weight_sum, weighted):
    rows, dim = weighted.shape
    lane = lax.broadcasted_iota(jnp.int32, (rows, dim), 1)
    return jnp.concatenate([weighted, jnp.where(lane < dim // 2, peak, weight_sum)], axis=1)


def softmax_part(scores, usable, values):
    peak = jnp.max(jnp.where(usable, scores, NEGATIVE), axis=1, keepdims=True)
    probability = jnp.where(usable, jnp.exp(scores - peak), 0.0).astype(BF16)
    weight_sum = jnp.sum(probability.astype(F32), axis=1, keepdims=True)
    return peak, weight_sum, jnp.dot(probability, values, preferred_element_type=F32)


def joined(former, latter):
    peak = jnp.maximum(former[0], latter[0])
    left, right = jnp.exp(former[0] - peak), jnp.exp(latter[0] - peak)
    return (
        peak,
        former[1] * left + latter[1] * right,
        former[2] * left + latter[2] * right,
    )


def unpacked_state(state):
    dim = state.shape[1] // 2
    return state[:, dim : dim + 1], state[:, dim + dim // 2 : dim + dim // 2 + 1], state[:, :dim]


def exact_kernel(count, *refs):
    key_refs, value_refs = refs[:count], refs[count : 2 * count]
    query_ref, limit_ref, out_ref = refs[2 * count :]
    queries = query_ref[...]
    rows, dim = queries.shape
    keys = jnp.concatenate([k[...] for k in key_refs], axis=0)
    values = jnp.concatenate([v[...] for v in value_refs], axis=0)
    scores = dot_nt(queries, keys) * dim ** (-0.5)
    lane = lax.broadcasted_iota(jnp.int32, (rows, BLOCK), 1)
    usable = jnp.concatenate(
        [
            jnp.where(lane < limit_ref[:, i : i + 1], 1.0, 0.0)
            for i in range(keys.shape[0] // BLOCK)
        ],
        axis=1,
    )
    out_ref[...] = packed_state(*softmax_part(scores, usable > 0.5, values))


def summary_kernel(
    keep_ref, mass_ref, recv_ref, query_ref, usable_ref, exact_ref, state_ref, cent_ref
):
    count, lanes = keep_ref.shape
    dim = lanes // 2
    masses = mass_ref[0:1, :] + unpacked_masses(recv_ref[count:, :], count)
    sums = keep_ref[...] + recv_ref[:count, :].astype(F32)
    cent_ref[...] = to_unit(sums[:, :dim])
    column = jnp.broadcast_to(masses, (dim, count)).T
    mean_keys = (sums[:, :dim] / column).astype(BF16)
    mean_values = (sums[:, dim:] / column).astype(BF16)
    scores = dot_nt(query_ref[...], mean_keys) * dim ** (-0.5) + jnp.log(masses)
    state = softmax_part(scores, usable_ref[...] > 0.5, mean_values)
    state_ref[...] = packed_state(*joined(unpacked_state(exact_ref[...]), state))


def in_order(flip, own_ref, recv_ref):
    own, recv = own_ref[...], recv_ref[...]
    return jnp.where(flip, recv, own), jnp.where(flip, own, recv)


def merge_kernel(flip_ref, own_ref, recv_ref, out_ref):
    former, latter = in_order(flip_ref[0] != 0, own_ref, recv_ref)
    out_ref[...] = packed_state(*joined(unpacked_state(former), unpacked_state(latter)))


def last_merge_kernel(scalar_ref, own_ref, recv_ref, cent_ref, *pack_refs):
    former, latter = in_order(scalar_ref[0] != 0, own_ref, recv_ref)
    _, weight_sum, weighted = joined(unpacked_state(former), unpacked_state(latter))
    attended = weighted / weight_sum
    own = scalar_ref[1]
    per_owner = cent_ref.shape[1]
    for step, pack_ref in enumerate(pack_refs):
        pack_ref[:per_owner, :] = cent_ref[own ^ step]
        pack_ref[per_owner:, :] = attended


def spread_kernel(scalar_ref, *refs):
    pack_refs, (cent_ref, out_ref) = refs[:-2], refs[-2:]
    own = scalar_ref[0]
    per_owner = cent_ref.shape[1]
    requests, _, group, dim = out_ref.shape
    for step, pack_ref in enumerate(pack_refs):
        cent_ref[own ^ step] = pack_ref[:per_owner, :]
        for r in range(requests):
            at = per_owner + r * group
            out_ref[r, own ^ step] = pack_ref[at : at + group, :].astype(BF16)


def body(
    key_cache,
    value_cache,
    init_centroids,
    block_clusters,
    chosen_clusters,
    request_positions,
    queries,
):
    devices = lax.axis_size("ctx")
    index = lax.axis_index("ctx").astype(jnp.int32)
    heads, tok_dev, dim = key_cache.shape
    clusters = init_centroids.shape[1]
    requests, _, group, _ = queries.shape
    per_owner = clusters // devices
    blk_dev = tok_dev // BLOCK
    spread = devices // heads
    levels = spread.bit_length() - 1
    if heads * spread != devices or 1 << levels != spread or heads & (heads - 1) or levels < 2:
        raise ValueError("unsupported mesh")
    bits = devices.bit_length() - 1
    head_bits = heads.bit_length() - 1
    head_basis = [2 << bit for bit in range(head_bits)]
    rank_basis = [1] + [1 << bit for bit in range(head_bits + 1, bits)]
    rank_basis[1] |= heads
    head_masks = [spanned(head_basis, s) for s in range(heads)]
    rank_masks = [spanned(rank_basis, s) for s in range(spread)]
    head_duals, rank_duals = duals(head_basis, rank_basis, devices)
    head, rank = coordinates(index, head_duals), coordinates(index, rank_duals)
    base = coordinates(rank, [sum(1 << j for j in range(levels) if rank_basis[j] >> bit & 1) for bit in range(bits)])
    half = clusters // 2
    rows = requests * group
    owned = heads * per_owner

    def over(array, bit):
        return lax.ppermute(array, "ctx", [(i, i ^ bit) for i in range(devices)])

    def pick(array, at, axis=0):
        return lax.dynamic_index_in_dim(array, at, axis, keepdims=False)

    keys = [pick(key_cache, head)]
    keys += [over(pick(key_cache, head ^ s), head_masks[s]) for s in range(1, heads)]

    blocks = pick(init_centroids, head).reshape(devices, per_owner, dim)
    turned = [int(format(r, f"0{levels}b")[::-1], 2) for r in range(spread)]
    order = jnp.stack([base ^ rank_masks[r] ^ mask for r in turned for mask in head_masks])

    pass_flops = 4 * tok_dev * clusters * dim
    sums, unit_cents = call(
        first_kernel,
        [shape((clusters, dim), F32), shape((clusters, dim), BF16)],
        [order, keys[0], blocks],
        [
            pltpu.VMEM((clusters, dim), F32),
            pltpu.VMEM((clusters, tok_dev), F32),
            pltpu.VMEM((clusters, tok_dev), BF16),
        ],
        pass_flops,
        scalars=1,
    )
    keep, send = call(
        functools.partial(rest_kernel, heads - 1),
        [shape((half, dim), F32), shape((half, dim), BF16)],
        [*keys[1:], unit_cents, sums],
        [
            pltpu.VMEM((clusters, tok_dev), F32),
            pltpu.VMEM((clusters, (heads - 1) * tok_dev), BF16),
        ],
        pass_flops * (heads - 1),
    )

    values = [pick(value_cache, head)]
    values += [over(pick(value_cache, head ^ s), head_masks[s]) for s in range(1, heads)]

    for level in range(levels - 1):
        total = keep + over(send, rank_basis[level]).astype(F32)
        if level < levels - 2:
            cut = total.shape[0] // 2
            keep, send = total[:cut], total[cut:].astype(BF16)
    rounded = total.astype(BF16)
    recv = over(rounded, rank_basis[levels - 1])
    cut = rounded.shape[0] // 2
    recv = jnp.concatenate([recv[cut:], recv[:cut]])
    own_cents = to_unit(rounded.astype(F32) + recv.astype(F32)).astype(BF16)
    for level in range(levels - 2, 0, -1):
        own_cents = jnp.concatenate([own_cents, over(own_cents, rank_basis[level])])
    other_cents = over(own_cents, 1)

    keep, keep_mass, send = call(
        functools.partial(second_kernel, heads),
        [
            shape((half, 2 * dim), F32),
            shape((8, half), F32),
            shape((half + 16, 2 * dim), BF16),
        ],
        [*keys, *values, own_cents, other_cents],
        [
            pltpu.VMEM((clusters, tok_dev), F32),
            pltpu.VMEM((clusters, heads * tok_dev), BF16),
            pltpu.VMEM((clusters, 128), F32),
        ],
        pass_flops * heads * 3 // 2,
    )

    own_queries = pick(queries, head, 1).reshape(rows, dim)
    own_chosen = pick(chosen_clusters, head, 1)
    held_by = jnp.stack([index ^ mask for mask in head_masks])
    block_ids = (held_by[:, None] * blk_dev + jnp.arange(blk_dev, dtype=jnp.int32)).reshape(-1)
    held = pick(block_clusters, head).reshape(devices, blk_dev)
    held = jnp.stack([pick(held, index ^ mask) for mask in head_masks]).reshape(-1)
    picked = jnp.any(own_chosen[:, :, None] == held, axis=1)
    limits = jnp.where(
        picked, jnp.clip(request_positions[:, None] - block_ids * BLOCK, 0, BLOCK), 0
    )
    limits = jnp.repeat(limits, group, axis=0)
    owners = (base ^ jnp.array(head_masks, jnp.int32))[:, None]
    owned_ids = (owners * per_owner + jnp.arange(per_owner, dtype=jnp.int32)).reshape(-1)
    usable = jnp.all(own_chosen[:, :, None] != owned_ids, axis=1).astype(F32)
    usable = jnp.repeat(usable, group, axis=0)

    (exact,) = call(
        functools.partial(exact_kernel, heads),
        [shape((rows, 2 * dim), F32)],
        [*keys, *values, own_queries, limits],
        (),
        4 * rows * heads * tok_dev * dim,
    )

    for level in range(levels - 1):
        recv = over(send, rank_basis[level])
        count = keep.shape[0] // 2
        keep, keep_mass, send = call(
            halve_kernel,
            [
                shape((count, 2 * dim), F32),
                shape((8, count), F32),
                shape((count + 16, 2 * dim), BF16),
            ],
            [keep, keep_mass, recv],
        )
    recv = over(send, rank_basis[levels - 1])
    state, centroids = call(
        summary_kernel,
        [shape((rows, 2 * dim), F32), shape((owned, dim), F32)],
        [keep, keep_mass, recv, own_queries, usable, exact],
        (),
        4 * rows * owned * dim,
    )
    for level in range(levels - 1):
        flip = ((rank >> level) & 1).reshape(1)
        (state,) = call(
            merge_kernel,
            [shape((rows, 2 * dim), F32)],
            [flip, state, over(state, rank_basis[level])],
            scalars=1,
        )
    scalars = jnp.stack([(rank >> (levels - 1)) & 1, head])
    packs = call(
        last_merge_kernel,
        [shape((per_owner + rows, dim), F32)] * heads,
        [
            scalars,
            state,
            over(state, rank_basis[levels - 1]),
            centroids.reshape(heads, per_owner, dim),
        ],
        scalars=1,
    )
    packs = [packs[0]] + [over(packs[s], head_masks[s]) for s in range(1, heads)]
    return call(
        spread_kernel,
        [shape((heads, per_owner, dim), F32), shape(queries.shape, BF16)],
        [head.reshape(1), *packs],
        scalars=1,
    )


def solution(mesh):
    placed = (
        P(None, ("groups", "ctx"), None),
        P(None, ("groups", "ctx"), None),
        P(),
        P(None, "groups"),
        P("groups", None, None),
        P("groups"),
        P("groups", None, None, None),
    )
    return jax.shard_map(
        body,
        mesh=mesh,
        in_specs=placed,
        out_specs=(P(None, ("groups", "ctx"), None), P("groups", None, None, None)),
        check_vma=False,
    )
```

```python
import functools
import math

import jax
import jax.numpy as jnp
from jax import lax
from jax.experimental import pallas as pl
from jax.experimental.pallas import tpu as pltpu
from jax.sharding import PartitionSpec as P

BLOCK = 128
SHARPNESS = 16.0
EPSILON = 1e-06
NEGATIVE = -1e30
F32 = jnp.float32
BF16 = jnp.bfloat16
VMEM_BYTES = 48 * 1024 * 1024
TILE = 256


def to_unit(vectors):
    vectors = vectors.astype(F32)
    return (
        vectors
        * lax.rsqrt(jnp.mean(vectors * vectors, axis=-1, keepdims=True) + EPSILON)
        * vectors.shape[-1] ** (-0.5)
    )


def dot_nt(left, right):
    return lax.dot_general(left, right, (((1,), (1,)), ((), ())), preferred_element_type=F32)


def spanned(basis, number):
    return functools.reduce(lambda a, b: a ^ b, [m for j, m in enumerate(basis) if number >> j & 1], 0)


def duals(head_basis, rank_basis, devices):
    basis = [*head_basis, *rank_basis]
    found = [
        next(
            f
            for f in range(devices)
            if all((f & m).bit_count() % 2 == (j == k) for j, m in enumerate(basis))
        )
        for k in range(len(basis))
    ]
    return found[: len(head_basis)], found[len(head_basis) :]


def coordinates(number, masks):
    result = 0
    for place, mask in enumerate(masks):
        for bit in range(mask.bit_length()):
            if mask >> bit & 1:
                result = result ^ ((number >> bit & 1) << place)
    return result


def call(kernel, outs, args, scratch=(), flops=0, scalars=0):
    in_specs = [pl.BlockSpec(memory_space=pltpu.SMEM)] * scalars
    in_specs += [pl.BlockSpec(memory_space=pltpu.VMEM)] * (len(args) - scalars)
    touched = sum(a.size * a.dtype.itemsize for a in (*args, *outs))
    return pl.pallas_call(
        kernel,
        out_shape=tuple(outs),
        in_specs=in_specs,
        out_specs=tuple(pl.BlockSpec(memory_space=pltpu.VMEM) for _ in outs),
        scratch_shapes=list(scratch),
        compiler_params=pltpu.CompilerParams(vmem_limit_bytes=VMEM_BYTES),
        cost_estimate=pl.CostEstimate(flops=flops, bytes_accessed=touched, transcendentals=0),
    )(*args)


def shape(dims, dtype):
    return jax.ShapeDtypeStruct(dims, dtype)


def fill_raised(piece, unit_keys, raised_ref, row, first):
    tokens = unit_keys.shape[0]
    factor = SHARPNESS * math.log2(math.e)
    total = jnp.zeros((1, tokens), F32)
    tile = min(TILE, piece.shape[0])
    for at in range(0, piece.shape[0], tile):
        raised = jnp.exp2(dot_nt(piece[at : at + tile, :], unit_keys) * factor)
        raised_ref[row + at : row + at + tile, first : first + tokens] = raised.astype(
            raised_ref.dtype
        )
        total = total + jnp.sum(raised, axis=0, keepdims=True)
    return total


def fill_weights(raised_ref, inverse, weight_ref, rows, from_row, first, raised_first, mass_ref):
    tokens = inverse.shape[1]
    tile = min(TILE, rows)
    for at in range(0, rows, tile):
        raised = raised_ref[
            from_row + at : from_row + at + tile, raised_first : raised_first + tokens
        ]
        weights = raised.astype(F32) * inverse
        weight_ref[at : at + tile, first : first + tokens] = weights.astype(BF16)
        if mass_ref is not None:
            part = weights[:, :128]
            for lane in range(128, tokens, 128):
                part = part + weights[:, lane : lane + 128]
            if first == 0:
                mass_ref[at : at + tile, :] = part
            else:
                mass_ref[at : at + tile, :] += part


def product(out_ref, weight_ref, values, sums_ref=None, row=0):
    rows = weight_ref.shape[0]
    tile = min(TILE, rows)
    for at in range(0, rows, tile):
        sums = jnp.dot(weight_ref[at : at + tile, :], values, preferred_element_type=F32)
        if sums_ref is not None:
            sums = sums + sums_ref[row + at : row + at + tile, :]
        out_ref[at : at + tile, :] = sums.astype(out_ref.dtype)


def first_kernel(
    base_ref, order, key_ref, cent_ref, sums_ref, unit_ref, cents_ref, raised_ref, weight_ref
):
    per_owner = cent_ref.shape[1]
    for at, mask in enumerate(order):
        cents_ref[at * per_owner : (at + 1) * per_owner, :] = cent_ref[base_ref[0] ^ mask].astype(
            F32
        )
    unit_ref[...] = to_unit(cents_ref[...]).astype(BF16)
    keys = key_ref[...]
    inverse = 1.0 / fill_raised(unit_ref, to_unit(keys).astype(BF16), raised_ref, 0, 0)
    fill_weights(raised_ref, inverse, weight_ref, weight_ref.shape[0], 0, 0, 0, None)
    product(sums_ref, weight_ref, keys)


def rest_kernel(count, *refs):
    key_refs, (unit_ref, sums_ref, send_ref, keep_weight_ref, raised_ref, weight_ref) = (
        refs[:count],
        refs[count:],
    )
    half = send_ref.shape[0]
    first = 0
    for key_ref in key_refs:
        unit_keys = to_unit(key_ref[...]).astype(BF16)
        inverse = 1.0 / fill_raised(unit_ref, unit_keys, raised_ref, 0, 0)
        fill_weights(raised_ref, inverse, weight_ref, half, half, first, 0, None)
        fill_weights(raised_ref, inverse, keep_weight_ref, half, 0, first, 0, None)
        first += unit_keys.shape[0]
    product(send_ref, weight_ref, joined_rows(key_refs), sums_ref, half)


def keep_kernel(count, *refs):
    key_refs, (sums_ref, weight_ref, keep_ref) = refs[:count], refs[count:]
    product(keep_ref, weight_ref, joined_rows(key_refs), sums_ref, 0)


def joined_rows(refs):
    return jnp.concatenate([ref[...] for ref in refs], axis=0)


def joined_pairs(key_refs, value_refs):
    return jnp.concatenate(
        [jnp.concatenate([k[...], v[...]], axis=1) for k, v in zip(key_refs, value_refs)], axis=0
    )


def packed_masses(row, lanes):
    count = row.shape[1]
    high = row.astype(BF16).astype(F32)
    low = row - high
    rows = []
    for part in (high, low):
        if count < lanes:
            rows.append(jnp.concatenate([part, jnp.zeros((1, lanes - count), F32)], axis=1))
        else:
            rows += [part[:, at : at + lanes] for at in range(0, count, lanes)]
    rows.append(jnp.zeros((16 - len(rows), lanes), F32))
    return jnp.concatenate(rows, axis=0).astype(BF16)


def unpacked_masses(block, count):
    block = block.astype(F32)
    lanes = block.shape[1]
    if count < lanes:
        return block[0:1, :count] + block[1:2, :count]
    rows = count // lanes
    return jnp.concatenate(
        [block[i : i + 1, :] + block[rows + i : rows + i + 1, :] for i in range(rows)], axis=1
    )


def own_half_kernel(count, *refs):
    key_refs, (cent_ref, unit_ref, raised_ref, total_ref) = refs[:count], refs[count:]
    first = 0
    for key_ref in key_refs:
        unit_keys = to_unit(key_ref[...]).astype(BF16)
        tokens = unit_keys.shape[0]
        unit_ref[first : first + tokens, :] = unit_keys
        total = fill_raised(cent_ref, unit_keys, raised_ref, 0, first)
        total_ref[:, first : first + tokens] = jnp.broadcast_to(total, (8, tokens))
        first += tokens


def other_half_kernel(count, *refs):
    key_refs, value_refs = refs[:count], refs[count : 2 * count]
    unit_ref, cent_ref, total_ref, send_ref, inverse_ref, raised_ref, weight_ref, mass_ref = refs[
        2 * count :
    ]
    half, lanes = cent_ref.shape[0], send_ref.shape[1]
    first = 0
    for key_ref in key_refs:
        tokens = key_ref.shape[0]
        chunk = slice(first, first + tokens)
        total = fill_raised(cent_ref, unit_ref[chunk, :], raised_ref, 0, 0)
        inverse = 1.0 / (total_ref[0:1, chunk] + total)
        inverse_ref[:, chunk] = jnp.broadcast_to(inverse, (8, tokens))
        fill_weights(raised_ref, inverse, weight_ref, half, 0, first, 0, mass_ref)
        first += tokens
    masses = jnp.sum(mass_ref[...].T, axis=0, keepdims=True)
    send_ref[half:, :] = packed_masses(masses, lanes)
    product(send_ref, weight_ref, joined_pairs(key_refs, value_refs))


def keep_half_kernel(count, *refs):
    key_refs, value_refs = refs[:count], refs[count : 2 * count]
    raised_ref, inverse_ref, keep_ref, keep_mass_ref, weight_ref, mass_ref = refs[2 * count :]
    half = keep_ref.shape[0]
    first = 0
    for key_ref in key_refs:
        tokens = key_ref.shape[0]
        inverse = inverse_ref[0:1, first : first + tokens]
        fill_weights(raised_ref, inverse, weight_ref, half, 0, first, first, mass_ref)
        first += tokens
    masses = jnp.sum(mass_ref[...].T, axis=0, keepdims=True)
    keep_mass_ref[...] = jnp.broadcast_to(masses, keep_mass_ref.shape)
    product(keep_ref, weight_ref, joined_pairs(key_refs, value_refs))


def halve_kernel(keep_ref, mass_ref, recv_ref, keep_out_ref, mass_out_ref, send_ref):
    count, lanes = keep_ref.shape
    half = count // 2
    masses = mass_ref[0:1, :] + unpacked_masses(recv_ref[count:, :], count)
    keep_out_ref[...] = keep_ref[:half, :] + recv_ref[:half, :].astype(F32)
    mass_out_ref[...] = jnp.broadcast_to(masses[:, :half], mass_out_ref.shape)
    send_ref[:half, :] = (keep_ref[half:, :] + recv_ref[half:count, :].astype(F32)).astype(BF16)
    send_ref[half:, :] = packed_masses(masses[:, half:], lanes)


def packed_state(peak, weight_sum, weighted):
    rows, dim = weighted.shape
    lane = lax.broadcasted_iota(jnp.int32, (rows, dim), 1)
    return jnp.concatenate([weighted, jnp.where(lane < dim // 2, peak, weight_sum)], axis=1)


def softmax_part(scores, usable, values):
    peak = jnp.max(jnp.where(usable, scores, NEGATIVE), axis=1, keepdims=True)
    probability = jnp.where(usable, jnp.exp(scores - peak), 0.0).astype(BF16)
    weight_sum = jnp.sum(probability.astype(F32), axis=1, keepdims=True)
    return peak, weight_sum, jnp.dot(probability, values, preferred_element_type=F32)


def joined(former, latter):
    peak = jnp.maximum(former[0], latter[0])
    left, right = jnp.exp(former[0] - peak), jnp.exp(latter[0] - peak)
    return (
        peak,
        former[1] * left + latter[1] * right,
        former[2] * left + latter[2] * right,
    )


def unpacked_state(state):
    dim = state.shape[1] // 2
    return state[:, dim : dim + 1], state[:, dim + dim // 2 : dim + dim // 2 + 1], state[:, :dim]


def exact_kernel(count, head_masks, owned_by, per_owner, *refs):
    scalar_refs, key_refs, value_refs = (
        refs[:5],
        refs[5 : 5 + count],
        refs[5 + count : 5 + 2 * count],
    )
    head_ref, index_ref, base_ref, position_ref, cluster_ref = scalar_refs
    query_ref, chosen_ref, out_ref, own_query_ref, usable_ref = refs[5 + 2 * count :]
    head, index, base = head_ref[0], index_ref[0], base_ref[0]
    requests, _, group, dim = query_ref.shape
    rows = requests * group
    for r in range(requests):
        own_query_ref[r * group : (r + 1) * group, :] = query_ref[r, head].astype(F32)
    queries = own_query_ref[...].astype(BF16)
    ksel = chosen_ref.shape[2]
    chosen = jnp.concatenate(
        [
            jnp.broadcast_to(chosen_ref[r, pl.ds(head, 1), :], (group, ksel))
            for r in range(requests)
        ],
        axis=0,
    )
    positions = jnp.concatenate(
        [jnp.full((group, 1), position_ref[r], jnp.int32) for r in range(requests)], axis=0
    )
    lane = lax.broadcasted_iota(jnp.int32, (rows, BLOCK), 1)
    blocks = key_refs[0].shape[0] // BLOCK
    parts = []
    for mask in head_masks:
        for block in range(blocks):
            at = (index ^ mask) * blocks + block
            picked = jnp.max(
                jnp.where(chosen == cluster_ref[head, at], 1, 0).astype(F32), axis=1, keepdims=True
            )
            limit = jnp.where(picked > 0.5, positions - at * BLOCK, 0)
            parts.append(jnp.where(lane < limit, 1.0, 0.0))
    scores = dot_nt(queries, joined_rows(key_refs)) * dim ** (-0.5)
    usable = jnp.concatenate(parts, axis=1) > 0.5
    out_ref[...] = packed_state(*softmax_part(scores, usable, joined_rows(value_refs)))
    owned = usable_ref.shape[1]
    place = lax.broadcasted_iota(jnp.int32, (rows, owned), 1)
    ids = place
    for part, mask in enumerate(owned_by):
        shift = (base ^ mask) * per_owner - part * per_owner
        ids = jnp.where((place >= part * per_owner) & (place < (part + 1) * per_owner), place + shift, ids)
    free = jnp.ones((rows, owned), F32)
    for k in range(ksel):
        free = jnp.where(chosen[:, k : k + 1] == ids, 0.0, free)
    usable_ref[...] = free


def summary_kernel(
    keep_ref, mass_ref, recv_ref, query_ref, usable_ref, exact_ref, state_ref, cent_ref
):
    count, lanes = keep_ref.shape
    dim = lanes // 2
    masses = mass_ref[0:1, :] + unpacked_masses(recv_ref[count:, :], count)
    sums = keep_ref[...] + recv_ref[:count, :].astype(F32)
    cent_ref[...] = to_unit(sums[:, :dim])
    column = jnp.broadcast_to(masses, (dim, count)).T
    mean_keys = (sums[:, :dim] / column).astype(BF16)
    mean_values = (sums[:, dim:] / column).astype(BF16)
    queries = query_ref[...].astype(BF16)
    scores = dot_nt(queries, mean_keys) * dim ** (-0.5) + jnp.log(masses)
    state = softmax_part(scores, usable_ref[...] > 0.5, mean_values)
    state_ref[...] = packed_state(*joined(unpacked_state(exact_ref[...]), state))


def in_order(flip, own_ref, recv_ref):
    own, recv = own_ref[...], recv_ref[...]
    return jnp.where(flip, recv, own), jnp.where(flip, own, recv)


def merge_kernel(flip_ref, own_ref, recv_ref, out_ref):
    former, latter = in_order(flip_ref[0] != 0, own_ref, recv_ref)
    out_ref[...] = packed_state(*joined(unpacked_state(former), unpacked_state(latter)))


def last_merge_kernel(flip_ref, head_ref, own_ref, recv_ref, cent_ref, *pack_refs):
    former, latter = in_order(flip_ref[0] != 0, own_ref, recv_ref)
    _, weight_sum, weighted = joined(unpacked_state(former), unpacked_state(latter))
    attended = weighted / weight_sum
    own = head_ref[0]
    per_owner = cent_ref.shape[1]
    for step, pack_ref in enumerate(pack_refs):
        pack_ref[:per_owner, :] = cent_ref[own ^ step]
        pack_ref[per_owner:, :] = attended


def spread_kernel(scalar_ref, *refs):
    pack_refs, (cent_ref, out_ref) = refs[:-2], refs[-2:]
    own = scalar_ref[0]
    per_owner = cent_ref.shape[1]
    requests, _, group, dim = out_ref.shape
    for step, pack_ref in enumerate(pack_refs):
        cent_ref[own ^ step] = pack_ref[:per_owner, :]
        for r in range(requests):
            at = per_owner + r * group
            out_ref[r, own ^ step] = pack_ref[at : at + group, :].astype(BF16)


def body(
    key_cache,
    value_cache,
    init_centroids,
    block_clusters,
    chosen_clusters,
    request_positions,
    queries,
):
    devices = lax.axis_size("ctx")
    index = lax.axis_index("ctx").astype(jnp.int32)
    heads, tok_dev, dim = key_cache.shape
    clusters = init_centroids.shape[1]
    requests, _, group, _ = queries.shape
    per_owner = clusters // devices
    spread = devices // heads
    levels = spread.bit_length() - 1
    if heads * spread != devices or 1 << levels != spread or heads & (heads - 1) or levels < 2:
        raise ValueError("unsupported mesh")
    bits = devices.bit_length() - 1
    head_bits = heads.bit_length() - 1
    head_basis = [2 << bit for bit in range(head_bits)]
    rank_basis = [1] + [1 << bit for bit in range(head_bits + 1, bits)]
    rank_basis[1] |= heads
    head_masks = [spanned(head_basis, s) for s in range(heads)]
    rank_masks = [spanned(rank_basis, s) for s in range(spread)]
    head_duals, rank_duals = duals(head_basis, rank_basis, devices)
    head, rank = coordinates(index, head_duals), coordinates(index, rank_duals)
    base = coordinates(rank, [sum(1 << j for j in range(levels) if rank_basis[j] >> bit & 1) for bit in range(bits)])
    half = clusters // 2
    rows = requests * group
    owned = heads * per_owner

    def over(array, bit):
        return lax.ppermute(array, "ctx", [(i, i ^ bit) for i in range(devices)])

    def pick(array, at, axis=0):
        return lax.dynamic_index_in_dim(array, at, axis, keepdims=False)

    keys = [pick(key_cache, head)]
    keys += [over(pick(key_cache, head ^ s), head_masks[s]) for s in range(1, heads)]

    blocks = pick(init_centroids, head).reshape(devices, per_owner, dim)
    turned = [int(format(r, f"0{levels}b")[::-1], 2) for r in range(spread)]
    order = [rank_masks[r] ^ mask for r in turned for mask in head_masks]
    scalar_base = base.reshape(1)

    pass_flops = 4 * tok_dev * clusters * dim
    sums, unit_cents = call(
        lambda base_ref, *refs: first_kernel(base_ref, order, *refs),
        [shape((clusters, dim), F32), shape((clusters, dim), BF16)],
        [scalar_base, keys[0], blocks],
        [
            pltpu.VMEM((clusters, dim), F32),
            pltpu.VMEM((clusters, tok_dev), F32),
            pltpu.VMEM((clusters, tok_dev), BF16),
        ],
        pass_flops,
        scalars=1,
    )
    values = [pick(value_cache, head)]
    values += [over(pick(value_cache, head ^ s), head_masks[s]) for s in range(1, heads)]

    send, keep_weights = call(
        functools.partial(rest_kernel, heads - 1),
        [shape((half, dim), BF16), shape((half, (heads - 1) * tok_dev), BF16)],
        [*keys[1:], unit_cents, sums],
        [
            pltpu.VMEM((clusters, tok_dev), F32),
            pltpu.VMEM((half, (heads - 1) * tok_dev), BF16),
        ],
        pass_flops * (heads - 1),
    )
    (keep,) = call(
        functools.partial(keep_kernel, heads - 1),
        [shape((half, dim), F32)],
        [*keys[1:], sums, keep_weights],
        (),
        pass_flops * (heads - 1) // 4,
    )

    keep, values[1], values[2], values[3] = lax.optimization_barrier((keep, values[1], values[2], values[3]))
    for level in range(levels - 1):
        total = keep + over(send, rank_basis[level]).astype(F32)
        if level < levels - 2:
            cut = total.shape[0] // 2
            keep, send = total[:cut], total[cut:].astype(BF16)
    rounded = total.astype(BF16)
    recv = over(rounded, rank_basis[levels - 1])
    cut = rounded.shape[0] // 2
    recv = jnp.concatenate([recv[cut:], recv[:cut]])
    own_cents = to_unit(rounded.astype(F32) + recv.astype(F32)).astype(BF16)
    for level in range(levels - 2, 0, -1):
        own_cents = jnp.concatenate([own_cents, over(own_cents, rank_basis[level])])
    other_cents = over(own_cents, 1)

    tokens = heads * tok_dev
    unit_keys, raised, total = call(
        functools.partial(own_half_kernel, heads),
        [shape((tokens, dim), BF16), shape((half, tokens), BF16), shape((8, tokens), F32)],
        [*keys, own_cents],
        (),
        pass_flops * heads // 4,
    )
    half_scratch = [pltpu.VMEM((half, tokens), BF16), pltpu.VMEM((half, 128), F32)]
    send, inverse = call(
        functools.partial(other_half_kernel, heads),
        [shape((half + 16, 2 * dim), BF16), shape((8, tokens), F32)],
        [*keys, *values, unit_keys, other_cents, total],
        [pltpu.VMEM((half, tok_dev), F32), *half_scratch],
        pass_flops * heads * 3 // 4,
    )
    keep, keep_mass = call(
        functools.partial(keep_half_kernel, heads),
        [shape((half, 2 * dim), F32), shape((8, half), F32)],
        [*keys, *values, raised, inverse],
        half_scratch,
        pass_flops * heads // 2,
    )

    exact, own_queries, usable = call(
        functools.partial(exact_kernel, heads, head_masks, head_masks, per_owner),
        [shape((rows, 2 * dim), F32), shape((rows, dim), F32), shape((rows, owned), F32)],
        [
            head.reshape(1),
            index.reshape(1),
            scalar_base,
            request_positions,
            block_clusters,
            *keys,
            *values,
            queries,
            chosen_clusters,
        ],
        (),
        4 * rows * heads * tok_dev * dim,
        scalars=5,
    )

    for level in range(levels - 1):
        recv = over(send, rank_basis[level])
        count = keep.shape[0] // 2
        keep, keep_mass, send = call(
            halve_kernel,
            [
                shape((count, 2 * dim), F32),
                shape((8, count), F32),
                shape((count + 16, 2 * dim), BF16),
            ],
            [keep, keep_mass, recv],
        )
    recv = over(send, rank_basis[levels - 1])
    state, centroids = call(
        summary_kernel,
        [shape((rows, 2 * dim), F32), shape((owned, dim), F32)],
        [keep, keep_mass, recv, own_queries, usable, exact],
        (),
        4 * rows * owned * dim,
    )
    for level in range(levels - 1):
        flip = ((rank >> level) & 1).reshape(1)
        (state,) = call(
            merge_kernel,
            [shape((rows, 2 * dim), F32)],
            [flip, state, over(state, rank_basis[level])],
            scalars=1,
        )
    flip = ((rank >> (levels - 1)) & 1).reshape(1)
    packs = call(
        last_merge_kernel,
        [shape((per_owner + rows, dim), F32)] * heads,
        [
            flip,
            head.reshape(1),
            state,
            over(state, rank_basis[levels - 1]),
            centroids.reshape(heads, per_owner, dim),
        ],
        scalars=2,
    )
    packs = [packs[0]] + [over(packs[s], head_masks[s]) for s in range(1, heads)]
    return call(
        spread_kernel,
        [shape((heads, per_owner, dim), F32), shape(queries.shape, BF16)],
        [head.reshape(1), *packs],
        scalars=1,
    )


def solution(mesh):
    placed = (
        P(None, ("groups", "ctx"), None),
        P(None, ("groups", "ctx"), None),
        P(),
        P(None, "groups"),
        P("groups", None, None),
        P("groups"),
        P("groups", None, None, None),
    )
    return jax.shard_map(
        body,
        mesh=mesh,
        in_specs=placed,
        out_specs=(P(None, ("groups", "ctx"), None), P("groups", None, None, None)),
        check_vma=False,
    )
```

```python
import functools
import math

import jax
import jax.numpy as jnp
from jax import lax
from jax.experimental import pallas as pl
from jax.experimental.pallas import tpu as pltpu
from jax.sharding import PartitionSpec as P

BLOCK = 128
SHARPNESS = 16.0
EPSILON = 1e-06
NEGATIVE = -1e30
F32 = jnp.float32
BF16 = jnp.bfloat16
VMEM_BYTES = 48 * 1024 * 1024
TILE = 256


def to_unit(vectors):
    vectors = vectors.astype(F32)
    return (
        vectors
        * lax.rsqrt(jnp.mean(vectors * vectors, axis=-1, keepdims=True) + EPSILON)
        * vectors.shape[-1] ** (-0.5)
    )


def dot_nt(left, right):
    return lax.dot_general(left, right, (((1,), (1,)), ((), ())), preferred_element_type=F32)


def spanned(basis, number):
    return functools.reduce(lambda a, b: a ^ b, [m for j, m in enumerate(basis) if number >> j & 1], 0)


def duals(head_basis, rank_basis, devices):
    basis = [*head_basis, *rank_basis]
    found = [
        next(
            f
            for f in range(devices)
            if all((f & m).bit_count() % 2 == (j == k) for j, m in enumerate(basis))
        )
        for k in range(len(basis))
    ]
    return found[: len(head_basis)], found[len(head_basis) :]


def coordinates(number, masks):
    result = 0
    for place, mask in enumerate(masks):
        for bit in range(mask.bit_length()):
            if mask >> bit & 1:
                result = result ^ ((number >> bit & 1) << place)
    return result


def call(kernel, outs, args, scratch=(), flops=0, scalars=0):
    in_specs = [pl.BlockSpec(memory_space=pltpu.SMEM)] * scalars
    in_specs += [pl.BlockSpec(memory_space=pltpu.VMEM)] * (len(args) - scalars)
    touched = sum(a.size * a.dtype.itemsize for a in (*args, *outs))
    return pl.pallas_call(
        kernel,
        out_shape=tuple(outs),
        in_specs=in_specs,
        out_specs=tuple(pl.BlockSpec(memory_space=pltpu.VMEM) for _ in outs),
        scratch_shapes=list(scratch),
        compiler_params=pltpu.CompilerParams(vmem_limit_bytes=VMEM_BYTES),
        cost_estimate=pl.CostEstimate(flops=flops, bytes_accessed=touched, transcendentals=0),
    )(*args)


def shape(dims, dtype):
    return jax.ShapeDtypeStruct(dims, dtype)


def fill_raised(piece, unit_keys, raised_ref, row, first):
    tokens = unit_keys.shape[0]
    factor = SHARPNESS * math.log2(math.e)
    total = jnp.zeros((1, tokens), F32)
    tile = min(TILE, piece.shape[0])
    for at in range(0, piece.shape[0], tile):
        raised = jnp.exp2(dot_nt(piece[at : at + tile, :], unit_keys) * factor)
        raised_ref[row + at : row + at + tile, first : first + tokens] = raised.astype(
            raised_ref.dtype
        )
        total = total + jnp.sum(raised, axis=0, keepdims=True)
    return total


def fill_weights(raised_ref, inverse, weight_ref, rows, from_row, first, raised_first, mass_ref):
    tokens = inverse.shape[1]
    tile = min(TILE, rows)
    for at in range(0, rows, tile):
        raised = raised_ref[
            from_row + at : from_row + at + tile, raised_first : raised_first + tokens
        ]
        weights = raised.astype(F32) * inverse
        weight_ref[at : at + tile, first : first + tokens] = weights.astype(BF16)
        if mass_ref is not None:
            part = weights[:, :128]
            for lane in range(128, tokens, 128):
                part = part + weights[:, lane : lane + 128]
            if first == 0:
                mass_ref[at : at + tile, :] = part
            else:
                mass_ref[at : at + tile, :] += part


def product(out_ref, weight_ref, values, sums_ref=None, row=0):
    rows = weight_ref.shape[0]
    tile = min(TILE, rows)
    for at in range(0, rows, tile):
        sums = jnp.dot(weight_ref[at : at + tile, :], values, preferred_element_type=F32)
        if sums_ref is not None:
            sums = sums + sums_ref[row + at : row + at + tile, :]
        out_ref[at : at + tile, :] = sums.astype(out_ref.dtype)


def first_kernel(
    base_ref,
    order,
    key_ref,
    cent_ref,
    sums_ref,
    keep_weight_ref,
    unit_ref,
    cents_ref,
    raised_ref,
    weight_ref,
):
    per_owner = cent_ref.shape[1]
    for at, mask in enumerate(order):
        cents_ref[at * per_owner : (at + 1) * per_owner, :] = cent_ref[base_ref[0] ^ mask].astype(
            F32
        )
    unit_ref[...] = to_unit(cents_ref[...]).astype(BF16)
    pass_chunk(key_ref, unit_ref, None, sums_ref, keep_weight_ref, raised_ref, weight_ref)


def pass_chunk(key_ref, unit_ref, before_ref, sums_ref, keep_weight_ref, raised_ref, weight_ref):
    keys = key_ref[...]
    half = sums_ref.shape[0]
    inverse = 1.0 / fill_raised(unit_ref, to_unit(keys).astype(BF16), raised_ref, 0, 0)
    fill_weights(raised_ref, inverse, weight_ref, half, half, 0, 0, None)
    fill_weights(raised_ref, inverse, keep_weight_ref, half, 0, 0, 0, None)
    product(sums_ref, weight_ref, keys, before_ref)


def keep_kernel(count, *refs):
    key_refs, weight_refs, keep_ref = refs[:count], refs[count : 2 * count], refs[-1]
    weights = jnp.concatenate([ref[...] for ref in weight_refs], axis=1)
    keep_ref[...] = jnp.dot(weights, joined_rows(key_refs), preferred_element_type=F32)


def joined_rows(refs):
    return jnp.concatenate([ref[...] for ref in refs], axis=0)


def joined_pairs(key_refs, value_refs):
    return jnp.concatenate(
        [jnp.concatenate([k[...], v[...]], axis=1) for k, v in zip(key_refs, value_refs)], axis=0
    )


def packed_masses(row, lanes):
    count = row.shape[1]
    high = row.astype(BF16).astype(F32)
    low = row - high
    rows = []
    for part in (high, low):
        if count < lanes:
            rows.append(jnp.concatenate([part, jnp.zeros((1, lanes - count), F32)], axis=1))
        else:
            rows += [part[:, at : at + lanes] for at in range(0, count, lanes)]
    rows.append(jnp.zeros((16 - len(rows), lanes), F32))
    return jnp.concatenate(rows, axis=0).astype(BF16)


def unpacked_masses(block, count):
    block = block.astype(F32)
    lanes = block.shape[1]
    if count < lanes:
        return block[0:1, :count] + block[1:2, :count]
    rows = count // lanes
    return jnp.concatenate(
        [block[i : i + 1, :] + block[rows + i : rows + i + 1, :] for i in range(rows)], axis=1
    )


def own_half_kernel(count, *refs):
    key_refs, (cent_ref, unit_ref, raised_ref, total_ref) = refs[:count], refs[count:]
    first = 0
    for key_ref in key_refs:
        unit_keys = to_unit(key_ref[...]).astype(BF16)
        tokens = unit_keys.shape[0]
        unit_ref[first : first + tokens, :] = unit_keys
        total = fill_raised(cent_ref, unit_keys, raised_ref, 0, first)
        total_ref[:, first : first + tokens] = jnp.broadcast_to(total, (8, tokens))
        first += tokens


def other_half_kernel(count, *refs):
    key_refs, value_refs = refs[:count], refs[count : 2 * count]
    unit_ref, cent_ref, total_ref, send_ref, inverse_ref, raised_ref, weight_ref, mass_ref = refs[
        2 * count :
    ]
    half, lanes = cent_ref.shape[0], send_ref.shape[1]
    first = 0
    for key_ref in key_refs:
        tokens = key_ref.shape[0]
        chunk = slice(first, first + tokens)
        total = fill_raised(cent_ref, unit_ref[chunk, :], raised_ref, 0, 0)
        inverse = 1.0 / (total_ref[0:1, chunk] + total)
        inverse_ref[:, chunk] = jnp.broadcast_to(inverse, (8, tokens))
        fill_weights(raised_ref, inverse, weight_ref, half, 0, first, 0, mass_ref)
        first += tokens
    masses = jnp.sum(mass_ref[...].T, axis=0, keepdims=True)
    send_ref[half:, :] = packed_masses(masses, lanes)
    product(send_ref, weight_ref, joined_pairs(key_refs, value_refs))


def keep_half_kernel(count, *refs):
    key_refs, value_refs = refs[:count], refs[count : 2 * count]
    raised_ref, inverse_ref, keep_ref, keep_mass_ref, weight_ref, mass_ref = refs[2 * count :]
    half = keep_ref.shape[0]
    first = 0
    for key_ref in key_refs:
        tokens = key_ref.shape[0]
        inverse = inverse_ref[0:1, first : first + tokens]
        fill_weights(raised_ref, inverse, weight_ref, half, 0, first, first, mass_ref)
        first += tokens
    masses = jnp.sum(mass_ref[...].T, axis=0, keepdims=True)
    keep_mass_ref[...] = jnp.broadcast_to(masses, keep_mass_ref.shape)
    product(keep_ref, weight_ref, joined_pairs(key_refs, value_refs))


def halve_kernel(keep_ref, mass_ref, recv_ref, keep_out_ref, mass_out_ref, send_ref):
    count, lanes = keep_ref.shape
    half = count // 2
    masses = mass_ref[0:1, :] + unpacked_masses(recv_ref[count:, :], count)
    keep_out_ref[...] = keep_ref[:half, :] + recv_ref[:half, :].astype(F32)
    mass_out_ref[...] = jnp.broadcast_to(masses[:, :half], mass_out_ref.shape)
    send_ref[:half, :] = (keep_ref[half:, :] + recv_ref[half:count, :].astype(F32)).astype(BF16)
    send_ref[half:, :] = packed_masses(masses[:, half:], lanes)


def packed_state(peak, weight_sum, weighted):
    rows, dim = weighted.shape
    lines = [
        jnp.concatenate(
            [jnp.broadcast_to(column, (rows, dim)), jnp.zeros((dim - rows, dim), F32)], axis=0
        ).T[0:1, :]
        for column in (peak, weight_sum)
    ]
    return jnp.concatenate([weighted, *lines, jnp.zeros((6, dim), F32)], axis=0)


def softmax_part(scores, usable, values):
    peak = jnp.max(jnp.where(usable, scores, NEGATIVE), axis=1, keepdims=True)
    probability = jnp.where(usable, jnp.exp(scores - peak), 0.0).astype(BF16)
    weight_sum = jnp.sum(probability.astype(F32), axis=1, keepdims=True)
    return peak, weight_sum, jnp.dot(probability, values, preferred_element_type=F32)


def joined(former, latter):
    peak = jnp.maximum(former[0], latter[0])
    left, right = jnp.exp(former[0] - peak), jnp.exp(latter[0] - peak)
    return (
        peak,
        former[1] * left + latter[1] * right,
        former[2] * left + latter[2] * right,
    )


def unpacked_state(state):
    dim = state.shape[1]
    rows = state.shape[0] - 8
    columns = [
        jnp.broadcast_to(state[rows + at : rows + at + 1, :], (dim, dim)).T[:rows, :]
        for at in range(2)
    ]
    return columns[0], columns[1], state[:rows, :]


def exact_kernel(count, head_masks, owned_by, per_owner, *refs):
    scalar_refs, key_refs, value_refs = (
        refs[:5],
        refs[5 : 5 + count],
        refs[5 + count : 5 + 2 * count],
    )
    head_ref, index_ref, base_ref, position_ref, cluster_ref = scalar_refs
    query_ref, chosen_ref, out_ref, own_query_ref, usable_ref = refs[5 + 2 * count :]
    head, index, base = head_ref[0], index_ref[0], base_ref[0]
    requests, _, group, dim = query_ref.shape
    rows = requests * group
    for r in range(requests):
        own_query_ref[r * group : (r + 1) * group, :] = query_ref[r, head].astype(F32)
    queries = own_query_ref[...].astype(BF16)
    ksel = chosen_ref.shape[2]
    chosen = jnp.concatenate(
        [
            jnp.broadcast_to(chosen_ref[r, pl.ds(head, 1), :], (group, ksel))
            for r in range(requests)
        ],
        axis=0,
    )
    positions = jnp.concatenate(
        [jnp.full((group, 1), position_ref[r], jnp.int32) for r in range(requests)], axis=0
    )
    lane = lax.broadcasted_iota(jnp.int32, (rows, BLOCK), 1)
    blocks = key_refs[0].shape[0] // BLOCK
    parts = []
    for mask in head_masks:
        for block in range(blocks):
            at = (index ^ mask) * blocks + block
            picked = jnp.max(
                jnp.where(chosen == cluster_ref[head, at], 1, 0).astype(F32), axis=1, keepdims=True
            )
            limit = jnp.where(picked > 0.5, positions - at * BLOCK, 0)
            parts.append(jnp.where(lane < limit, 1.0, 0.0))
    scores = dot_nt(queries, joined_rows(key_refs)) * dim ** (-0.5)
    usable = jnp.concatenate(parts, axis=1) > 0.5
    out_ref[...] = packed_state(*softmax_part(scores, usable, joined_rows(value_refs)))
    owned = usable_ref.shape[1]
    place = lax.broadcasted_iota(jnp.int32, (rows, owned), 1)
    ids = place
    for part, mask in enumerate(owned_by):
        shift = (base ^ mask) * per_owner - part * per_owner
        ids = jnp.where((place >= part * per_owner) & (place < (part + 1) * per_owner), place + shift, ids)
    free = jnp.ones((rows, owned), F32)
    for k in range(ksel):
        free = jnp.where(chosen[:, k : k + 1] == ids, 0.0, free)
    usable_ref[...] = free


def summary_kernel(
    keep_ref, mass_ref, recv_ref, query_ref, usable_ref, exact_ref, state_ref, cent_ref
):
    count, lanes = keep_ref.shape
    dim = lanes // 2
    masses = mass_ref[0:1, :] + unpacked_masses(recv_ref[count:, :], count)
    sums = keep_ref[...] + recv_ref[:count, :].astype(F32)
    cent_ref[...] = to_unit(sums[:, :dim])
    column = jnp.broadcast_to(masses, (dim, count)).T
    mean_keys = (sums[:, :dim] / column).astype(BF16)
    mean_values = (sums[:, dim:] / column).astype(BF16)
    queries = query_ref[...].astype(BF16)
    scores = dot_nt(queries, mean_keys) * dim ** (-0.5) + jnp.log(masses)
    state = softmax_part(scores, usable_ref[...] > 0.5, mean_values)
    state_ref[...] = packed_state(*joined(unpacked_state(exact_ref[...]), state))


def in_order(flip, own_ref, recv_ref):
    own, recv = own_ref[...], recv_ref[...]
    return jnp.where(flip, recv, own), jnp.where(flip, own, recv)


def merge_kernel(flip_ref, own_ref, recv_ref, out_ref):
    former, latter = in_order(flip_ref[0] != 0, own_ref, recv_ref)
    out_ref[...] = packed_state(*joined(unpacked_state(former), unpacked_state(latter)))


def last_merge_kernel(flip_ref, head_ref, own_ref, recv_ref, cent_ref, attended_ref, *pack_refs):
    former, latter = in_order(flip_ref[0] != 0, own_ref, recv_ref)
    _, weight_sum, weighted = joined(unpacked_state(former), unpacked_state(latter))
    attended = (weighted / weight_sum).astype(BF16)
    attended_ref[...] = attended
    rows = attended.shape[0]
    for step, pack_ref in enumerate(pack_refs, 1):
        pack_ref[:rows, :] = attended
        pack_ref[rows:, :] = cent_ref[head_ref[0] ^ step].astype(BF16)


def spread_kernel(head_ref, own_cent_ref, attended_ref, *refs):
    pack_refs, (cent_ref, out_ref) = refs[:-2], refs[-2:]
    own = head_ref[0]
    requests, _, group, _ = out_ref.shape
    rows = requests * group
    cent_ref[own] = own_cent_ref[own]
    for step, pack_ref in enumerate((attended_ref, *pack_refs)):
        attended = pack_ref[:rows, :].astype(F32)
        if step:
            cent_ref[own ^ step] = pack_ref[rows:, :].astype(F32)
        for r in range(requests):
            out_ref[r, own ^ step] = attended[r * group : (r + 1) * group, :].astype(BF16)


def body(
    key_cache,
    value_cache,
    init_centroids,
    block_clusters,
    chosen_clusters,
    request_positions,
    queries,
):
    devices = lax.axis_size("ctx")
    index = lax.axis_index("ctx").astype(jnp.int32)
    heads, tok_dev, dim = key_cache.shape
    clusters = init_centroids.shape[1]
    requests, _, group, _ = queries.shape
    per_owner = clusters // devices
    spread = devices // heads
    levels = spread.bit_length() - 1
    if heads * spread != devices or 1 << levels != spread or heads & (heads - 1) or levels < 2:
        raise ValueError("unsupported mesh")
    bits = devices.bit_length() - 1
    head_bits = heads.bit_length() - 1
    head_basis = [2 << bit for bit in range(head_bits)]
    rank_basis = [1] + [1 << bit for bit in range(head_bits + 1, bits)]
    rank_basis[1] |= heads
    head_masks = [spanned(head_basis, s) for s in range(heads)]
    rank_masks = [spanned(rank_basis, s) for s in range(spread)]
    head_duals, rank_duals = duals(head_basis, rank_basis, devices)
    head, rank = coordinates(index, head_duals), coordinates(index, rank_duals)
    base = coordinates(rank, [sum(1 << j for j in range(levels) if rank_basis[j] >> bit & 1) for bit in range(bits)])
    half = clusters // 2
    rows = requests * group
    owned = heads * per_owner

    def over(array, bit):
        return lax.ppermute(array, "ctx", [(i, i ^ bit) for i in range(devices)])

    def pick(array, at, axis=0):
        return lax.dynamic_index_in_dim(array, at, axis, keepdims=False)

    keys = [pick(key_cache, head)]
    keys += [over(pick(key_cache, head ^ s), head_masks[s]) for s in range(1, heads)]

    blocks = pick(init_centroids, head).reshape(devices, per_owner, dim)
    turned = [int(format(r, f"0{levels}b")[::-1], 2) for r in range(spread)]
    order = [rank_masks[r] ^ mask for r in turned for mask in head_masks]
    scalar_base = base.reshape(1)

    pass_flops = 4 * tok_dev * clusters * dim
    chunk_scratch = [pltpu.VMEM((clusters, tok_dev), F32), pltpu.VMEM((half, tok_dev), BF16)]
    sums, keep_weights, unit_cents = call(
        lambda base_ref, *refs: first_kernel(base_ref, order, *refs),
        [
            shape((half, dim), F32),
            shape((half, tok_dev), BF16),
            shape((clusters, dim), BF16),
        ],
        [scalar_base, keys[0], blocks],
        [pltpu.VMEM((clusters, dim), F32), *chunk_scratch],
        pass_flops,
        scalars=1,
    )
    values = [pick(value_cache, head)]
    values += [over(pick(value_cache, head ^ s), head_masks[s]) for s in range(1, heads)]

    keep_weights = [keep_weights]
    for step in range(1, heads):
        sums, kept = call(
            pass_chunk,
            [shape((half, dim), F32 if step < heads - 1 else BF16), shape((half, tok_dev), BF16)],
            [keys[step], unit_cents, sums],
            chunk_scratch,
            pass_flops,
        )
        keep_weights.append(kept)
    send = sums
    (keep,) = call(
        functools.partial(keep_kernel, heads),
        [shape((half, dim), F32)],
        [*keys, *keep_weights],
        (),
        pass_flops * heads // 4,
    )
    keep, values[1], values[2] = lax.optimization_barrier((keep, values[1], values[2]))
    for level in range(levels - 1):
        total = keep + over(send, rank_basis[level]).astype(F32)
        if level < levels - 2:
            cut = total.shape[0] // 2
            keep, send = total[:cut], total[cut:].astype(BF16)
    rounded = total.astype(BF16)
    recv = over(rounded, rank_basis[levels - 1])
    cut = rounded.shape[0] // 2
    recv = jnp.concatenate([recv[cut:], recv[:cut]])
    own_cents = to_unit(rounded.astype(F32) + recv.astype(F32)).astype(BF16)
    for level in range(levels - 2, 0, -1):
        own_cents = jnp.concatenate([own_cents, over(own_cents, rank_basis[level])])
    other_cents = over(own_cents, 1)

    tokens = heads * tok_dev
    unit_keys, raised, total = call(
        functools.partial(own_half_kernel, heads),
        [shape((tokens, dim), BF16), shape((half, tokens), BF16), shape((8, tokens), F32)],
        [*keys, own_cents],
        (),
        pass_flops * heads // 4,
    )
    half_scratch = [pltpu.VMEM((half, tokens), BF16), pltpu.VMEM((half, 128), F32)]
    send, inverse = call(
        functools.partial(other_half_kernel, heads),
        [shape((half + 16, 2 * dim), BF16), shape((8, tokens), F32)],
        [*keys, *values, unit_keys, other_cents, total],
        [pltpu.VMEM((half, tok_dev), F32), *half_scratch],
        pass_flops * heads * 3 // 4,
    )
    keep, keep_mass = call(
        functools.partial(keep_half_kernel, heads),
        [shape((half, 2 * dim), F32), shape((8, half), F32)],
        [*keys, *values, raised, inverse],
        half_scratch,
        pass_flops * heads // 2,
    )

    exact, own_queries, usable = call(
        functools.partial(exact_kernel, heads, head_masks, head_masks, per_owner),
        [shape((rows + 8, dim), F32), shape((rows, dim), F32), shape((rows, owned), F32)],
        [
            head.reshape(1),
            index.reshape(1),
            scalar_base,
            request_positions,
            block_clusters,
            *keys,
            *values,
            queries,
            chosen_clusters,
        ],
        (),
        4 * rows * heads * tok_dev * dim,
        scalars=5,
    )

    for level in range(levels - 1):
        recv = over(send, rank_basis[level])
        count = keep.shape[0] // 2
        keep, keep_mass, send = call(
            halve_kernel,
            [
                shape((count, 2 * dim), F32),
                shape((8, count), F32),
                shape((count + 16, 2 * dim), BF16),
            ],
            [keep, keep_mass, recv],
        )
    recv = over(send, rank_basis[levels - 1])
    state, centroids = call(
        summary_kernel,
        [shape((rows + 8, dim), F32), shape((owned, dim), F32)],
        [keep, keep_mass, recv, own_queries, usable, exact],
        (),
        4 * rows * owned * dim,
    )
    for level in range(levels - 1):
        flip = ((rank >> level) & 1).reshape(1)
        (state,) = call(
            merge_kernel,
            [shape((rows + 8, dim), F32)],
            [flip, state, over(state, rank_basis[level])],
            scalars=1,
        )
    flip = ((rank >> (levels - 1)) & 1).reshape(1)
    centroids = centroids.reshape(heads, per_owner, dim)
    attended, *packs = call(
        last_merge_kernel,
        [shape((rows, dim), BF16)] + [shape((rows + per_owner, dim), BF16)] * (heads - 1),
        [flip, head.reshape(1), state, over(state, rank_basis[levels - 1]), centroids],
        scalars=2,
    )
    packs = [over(pack, head_masks[step]) for step, pack in enumerate(packs, 1)]
    return call(
        spread_kernel,
        [shape((heads, per_owner, dim), F32), shape(queries.shape, BF16)],
        [head.reshape(1), centroids, attended, *packs],
        scalars=1,
    )


def solution(mesh):
    placed = (
        P(None, ("groups", "ctx"), None),
        P(None, ("groups", "ctx"), None),
        P(),
        P(None, "groups"),
        P("groups", None, None),
        P("groups"),
        P("groups", None, None, None),
    )
    return jax.shard_map(
        body,
        mesh=mesh,
        in_specs=placed,
        out_specs=(P(None, ("groups", "ctx"), None), P("groups", None, None, None)),
        check_vma=False,
    )
```

```python
import functools
import math

import jax
import jax.numpy as jnp
from jax import lax
from jax.experimental import pallas as pl
from jax.experimental.pallas import tpu as pltpu
from jax.sharding import PartitionSpec as P

BLOCK = 128
SHARPNESS = 16.0
EPSILON = 1e-06
NEGATIVE = -1e30
F32 = jnp.float32
BF16 = jnp.bfloat16
VMEM_BYTES = 48 * 1024 * 1024
TILE = 256


def to_unit(vectors):
    vectors = vectors.astype(F32)
    return (
        vectors
        * lax.rsqrt(jnp.mean(vectors * vectors, axis=-1, keepdims=True) + EPSILON)
        * vectors.shape[-1] ** (-0.5)
    )


def dot_nt(left, right):
    return lax.dot_general(left, right, (((1,), (1,)), ((), ())), preferred_element_type=F32)


def spanned(basis, number):
    return functools.reduce(lambda a, b: a ^ b, [m for j, m in enumerate(basis) if number >> j & 1], 0)


def duals(head_basis, rank_basis, devices):
    basis = [*head_basis, *rank_basis]
    found = [
        next(
            f
            for f in range(devices)
            if all((f & m).bit_count() % 2 == (j == k) for j, m in enumerate(basis))
        )
        for k in range(len(basis))
    ]
    return found[: len(head_basis)], found[len(head_basis) :]


def coordinates(number, masks):
    result = 0
    for place, mask in enumerate(masks):
        for bit in range(mask.bit_length()):
            if mask >> bit & 1:
                result = result ^ ((number >> bit & 1) << place)
    return result


def call(kernel, outs, args, scratch=(), flops=0, scalars=0):
    in_specs = [pl.BlockSpec(memory_space=pltpu.SMEM)] * scalars
    in_specs += [pl.BlockSpec(memory_space=pltpu.VMEM)] * (len(args) - scalars)
    touched = sum(a.size * a.dtype.itemsize for a in (*args, *outs))
    return pl.pallas_call(
        kernel,
        out_shape=tuple(outs),
        in_specs=in_specs,
        out_specs=tuple(pl.BlockSpec(memory_space=pltpu.VMEM) for _ in outs),
        scratch_shapes=list(scratch),
        compiler_params=pltpu.CompilerParams(vmem_limit_bytes=VMEM_BYTES),
        cost_estimate=pl.CostEstimate(flops=flops, bytes_accessed=touched, transcendentals=0),
    )(*args)


def shape(dims, dtype):
    return jax.ShapeDtypeStruct(dims, dtype)


def fill_raised(piece, unit_keys, raised_ref, row, first):
    tokens = unit_keys.shape[0]
    factor = SHARPNESS * math.log2(math.e)
    total = jnp.zeros((1, tokens), F32)
    tile = min(TILE, piece.shape[0])
    for at in range(0, piece.shape[0], tile):
        raised = jnp.exp2(dot_nt(piece[at : at + tile, :], unit_keys) * factor)
        raised_ref[row + at : row + at + tile, first : first + tokens] = raised.astype(
            raised_ref.dtype
        )
        total = total + jnp.sum(raised, axis=0, keepdims=True)
    return total


def fill_weights(raised_ref, inverse, weight_ref, rows, from_row, first, raised_first, mass_ref):
    tokens = inverse.shape[1]
    tile = min(TILE, rows)
    for at in range(0, rows, tile):
        raised = raised_ref[
            from_row + at : from_row + at + tile, raised_first : raised_first + tokens
        ]
        weights = raised.astype(F32) * inverse
        weight_ref[at : at + tile, first : first + tokens] = weights.astype(BF16)
        if mass_ref is not None:
            part = weights[:, :128]
            for lane in range(128, tokens, 128):
                part = part + weights[:, lane : lane + 128]
            if first == 0:
                mass_ref[at : at + tile, :] = part
            else:
                mass_ref[at : at + tile, :] += part


def product(out_ref, weight_ref, values, sums_ref=None, row=0):
    rows = weight_ref.shape[0]
    tile = min(TILE, rows)
    for at in range(0, rows, tile):
        sums = jnp.dot(weight_ref[at : at + tile, :], values, preferred_element_type=F32)
        if sums_ref is not None:
            sums = sums + sums_ref[row + at : row + at + tile, :]
        out_ref[at : at + tile, :] = sums.astype(out_ref.dtype)


def first_kernel(
    base_ref,
    order,
    key_ref,
    cent_ref,
    sums_ref,
    keep_weight_ref,
    unit_ref,
    cents_ref,
    raised_ref,
    weight_ref,
):
    per_owner = cent_ref.shape[1]
    for at, mask in enumerate(order):
        cents_ref[at * per_owner : (at + 1) * per_owner, :] = cent_ref[base_ref[0] ^ mask].astype(
            F32
        )
    unit_ref[...] = to_unit(cents_ref[...]).astype(BF16)
    pass_chunk(key_ref, unit_ref, None, sums_ref, keep_weight_ref, raised_ref, weight_ref)


def pass_chunk(key_ref, unit_ref, before_ref, sums_ref, keep_weight_ref, raised_ref, weight_ref):
    keys = key_ref[...]
    half = sums_ref.shape[0]
    inverse = 1.0 / fill_raised(unit_ref, to_unit(keys).astype(BF16), raised_ref, 0, 0)
    fill_weights(raised_ref, inverse, weight_ref, half, half, 0, 0, None)
    fill_weights(raised_ref, inverse, keep_weight_ref, half, 0, 0, 0, None)
    product(sums_ref, weight_ref, keys, before_ref)


def keep_kernel(count, *refs):
    key_refs, weight_refs, keep_ref = refs[:count], refs[count : 2 * count], refs[-1]
    weights = jnp.concatenate([ref[...] for ref in weight_refs], axis=1)
    keep_ref[...] = jnp.dot(weights, joined_rows(key_refs), preferred_element_type=F32)


def joined_rows(refs):
    return jnp.concatenate([ref[...] for ref in refs], axis=0)


def joined_pairs(key_refs, value_refs):
    return jnp.concatenate(
        [jnp.concatenate([k[...], v[...]], axis=1) for k, v in zip(key_refs, value_refs)], axis=0
    )


def packed_masses(row, lanes):
    count = row.shape[1]
    high = row.astype(BF16).astype(F32)
    low = row - high
    rows = []
    for part in (high, low):
        if count < lanes:
            rows.append(jnp.concatenate([part, jnp.zeros((1, lanes - count), F32)], axis=1))
        else:
            rows += [part[:, at : at + lanes] for at in range(0, count, lanes)]
    rows.append(jnp.zeros((16 - len(rows), lanes), F32))
    return jnp.concatenate(rows, axis=0).astype(BF16)


def unpacked_masses(block, count):
    block = block.astype(F32)
    lanes = block.shape[1]
    if count < lanes:
        return block[0:1, :count] + block[1:2, :count]
    rows = count // lanes
    return jnp.concatenate(
        [block[i : i + 1, :] + block[rows + i : rows + i + 1, :] for i in range(rows)], axis=1
    )


def cents_kernel(own_ref, recv_ref, out_ref):
    half = own_ref.shape[0] // 2
    for at in (0, half):
        recv = recv_ref[half - at : 2 * half - at, :]
        sums = own_ref[at : at + half, :].astype(F32) + recv.astype(F32)
        out_ref[at : at + half, :] = to_unit(sums).astype(BF16)


def own_half_kernel(count, *refs):
    key_refs, (cent_ref, unit_ref, raised_ref, total_ref) = refs[:count], refs[count:]
    first = 0
    for key_ref in key_refs:
        unit_keys = to_unit(key_ref[...]).astype(BF16)
        tokens = unit_keys.shape[0]
        unit_ref[first : first + tokens, :] = unit_keys
        total = fill_raised(cent_ref, unit_keys, raised_ref, 0, first)
        total_ref[:, first : first + tokens] = jnp.broadcast_to(total, (8, tokens))
        first += tokens


def other_half_kernel(count, *refs):
    pair_refs, refs = refs[: 2 * count], refs[2 * count :]
    unit_ref, cent_ref, total_ref, send_ref, inverse_ref, early_ref = refs[:6]
    raised_ref, weight_ref, mass_ref = refs[6:]
    rows, lanes = early_ref.shape[0], send_ref.shape[1]
    first = 0
    for key_ref in pair_refs[:count]:
        tokens = key_ref.shape[0]
        chunk = slice(first, first + tokens)
        total = fill_raised(cent_ref, unit_ref[chunk, :], raised_ref, 0, 0)
        inverse = 1.0 / (total_ref[0:1, chunk] + total)
        inverse_ref[:, chunk] = jnp.broadcast_to(inverse, (8, tokens))
        fill_weights(raised_ref, inverse, weight_ref, rows, rows, first, 0, mass_ref)
        early_ref[:, chunk] = raised_ref[:rows, :tokens].astype(BF16)
        first += tokens
    masses = jnp.sum(mass_ref[...].T, axis=0, keepdims=True)
    send_ref[rows:, :] = packed_masses(masses, lanes)
    product(send_ref, weight_ref, joined_pairs(pair_refs[:count], pair_refs[count:]))


def part_kernel(count, row, to_send, *refs):
    pair_refs, refs = refs[: 2 * count], refs[2 * count :]
    raised_ref, inverse_ref, refs = refs[0], refs[1], refs[2:]
    out_ref, (weight_ref, mass_ref) = refs[0], refs[-2:]
    rows = weight_ref.shape[0]
    first = 0
    for key_ref in pair_refs[:count]:
        tokens = key_ref.shape[0]
        inverse = inverse_ref[0:1, first : first + tokens]
        fill_weights(raised_ref, inverse, weight_ref, rows, row, first, first, mass_ref)
        first += tokens
    masses = jnp.sum(mass_ref[...].T, axis=0, keepdims=True)
    if to_send:
        out_ref[rows:, :] = packed_masses(masses, out_ref.shape[1])
    else:
        refs[1][...] = jnp.broadcast_to(masses, refs[1].shape)
    product(out_ref, weight_ref, joined_pairs(pair_refs[:count], pair_refs[count:]))


def both_kernel(to_send, keep_ref, mass_ref, recv_ref, out_ref, *refs):
    count, lanes = keep_ref.shape
    masses = mass_ref[0:1, :] + unpacked_masses(recv_ref[count:, :], count)
    sums = keep_ref[...] + recv_ref[:count, :].astype(F32)
    out_ref[:count, :] = sums.astype(out_ref.dtype)
    if to_send:
        out_ref[count:, :] = packed_masses(masses, lanes)
    else:
        refs[0][...] = jnp.broadcast_to(masses, refs[0].shape)


def halve_kernel(keep_ref, mass_ref, recv_ref, keep_out_ref, mass_out_ref, send_ref):
    count, lanes = keep_ref.shape
    half = count // 2
    masses = mass_ref[0:1, :] + unpacked_masses(recv_ref[count:, :], count)
    keep_out_ref[...] = keep_ref[:half, :] + recv_ref[:half, :].astype(F32)
    mass_out_ref[...] = jnp.broadcast_to(masses[:, :half], mass_out_ref.shape)
    send_ref[:half, :] = (keep_ref[half:, :] + recv_ref[half:count, :].astype(F32)).astype(BF16)
    send_ref[half:, :] = packed_masses(masses[:, half:], lanes)


def packed_state(peak, weight_sum, weighted):
    rows, dim = weighted.shape
    lines = [
        jnp.concatenate(
            [jnp.broadcast_to(column, (rows, dim)), jnp.zeros((dim - rows, dim), F32)], axis=0
        ).T[0:1, :]
        for column in (peak, weight_sum)
    ]
    return jnp.concatenate([weighted, *lines, jnp.zeros((6, dim), F32)], axis=0)


def softmax_part(scores, usable, values):
    peak = jnp.max(jnp.where(usable, scores, NEGATIVE), axis=1, keepdims=True)
    probability = jnp.where(usable, jnp.exp(scores - peak), 0.0).astype(BF16)
    weight_sum = jnp.sum(probability.astype(F32), axis=1, keepdims=True)
    return peak, weight_sum, jnp.dot(probability, values, preferred_element_type=F32)


def joined(former, latter):
    peak = jnp.maximum(former[0], latter[0])
    left, right = jnp.exp(former[0] - peak), jnp.exp(latter[0] - peak)
    return (
        peak,
        former[1] * left + latter[1] * right,
        former[2] * left + latter[2] * right,
    )


def unpacked_state(state):
    dim = state.shape[1]
    rows = state.shape[0] - 8
    columns = [
        jnp.broadcast_to(state[rows + at : rows + at + 1, :], (dim, dim)).T[:rows, :]
        for at in range(2)
    ]
    return columns[0], columns[1], state[:rows, :]


def exact_kernel(count, head_masks, owned_by, per_owner, *refs):
    scalar_refs, key_refs, value_refs = (
        refs[:5],
        refs[5 : 5 + count],
        refs[5 + count : 5 + 2 * count],
    )
    head_ref, index_ref, base_ref, position_ref, cluster_ref = scalar_refs
    query_ref, chosen_ref, out_ref, own_query_ref, usable_ref = refs[5 + 2 * count :]
    head, index, base = head_ref[0], index_ref[0], base_ref[0]
    requests, _, group, dim = query_ref.shape
    rows = requests * group
    for r in range(requests):
        own_query_ref[r * group : (r + 1) * group, :] = query_ref[r, head].astype(F32)
    queries = own_query_ref[...].astype(BF16)
    ksel = chosen_ref.shape[2]
    chosen = jnp.concatenate(
        [
            jnp.broadcast_to(chosen_ref[r, pl.ds(head, 1), :], (group, ksel))
            for r in range(requests)
        ],
        axis=0,
    )
    positions = jnp.concatenate(
        [jnp.full((group, 1), position_ref[r], jnp.int32) for r in range(requests)], axis=0
    )
    lane = lax.broadcasted_iota(jnp.int32, (rows, BLOCK), 1)
    blocks = key_refs[0].shape[0] // BLOCK
    parts = []
    for mask in head_masks:
        for block in range(blocks):
            at = (index ^ mask) * blocks + block
            picked = jnp.max(
                jnp.where(chosen == cluster_ref[head, at], 1, 0).astype(F32), axis=1, keepdims=True
            )
            limit = jnp.where(picked > 0.5, positions - at * BLOCK, 0)
            parts.append(jnp.where(lane < limit, 1.0, 0.0))
    scores = dot_nt(queries, joined_rows(key_refs)) * dim ** (-0.5)
    usable = jnp.concatenate(parts, axis=1) > 0.5
    out_ref[...] = packed_state(*softmax_part(scores, usable, joined_rows(value_refs)))
    owned = usable_ref.shape[1]
    place = lax.broadcasted_iota(jnp.int32, (rows, owned), 1)
    ids = place
    for part, mask in enumerate(owned_by):
        shift = (base ^ mask) * per_owner - part * per_owner
        ids = jnp.where((place >= part * per_owner) & (place < (part + 1) * per_owner), place + shift, ids)
    free = jnp.ones((rows, owned), F32)
    for k in range(ksel):
        free = jnp.where(chosen[:, k : k + 1] == ids, 0.0, free)
    usable_ref[...] = free


def summary_kernel(
    keep_ref, mass_ref, recv_ref, query_ref, usable_ref, exact_ref, state_ref, cent_ref
):
    count, lanes = keep_ref.shape
    dim = lanes // 2
    masses = mass_ref[0:1, :] + unpacked_masses(recv_ref[count:, :], count)
    sums = keep_ref[...] + recv_ref[:count, :].astype(F32)
    cent_ref[...] = to_unit(sums[:, :dim])
    column = jnp.broadcast_to(masses, (dim, count)).T
    mean_keys = (sums[:, :dim] / column).astype(BF16)
    mean_values = (sums[:, dim:] / column).astype(BF16)
    queries = query_ref[...].astype(BF16)
    scores = dot_nt(queries, mean_keys) * dim ** (-0.5) + jnp.log(masses)
    state = softmax_part(scores, usable_ref[...] > 0.5, mean_values)
    state_ref[...] = packed_state(*joined(unpacked_state(exact_ref[...]), state))


def in_order(flip, own_ref, recv_ref):
    own, recv = own_ref[...], recv_ref[...]
    return jnp.where(flip, recv, own), jnp.where(flip, own, recv)


def merge_kernel(flip_ref, own_ref, recv_ref, out_ref):
    former, latter = in_order(flip_ref[0] != 0, own_ref, recv_ref)
    out_ref[...] = packed_state(*joined(unpacked_state(former), unpacked_state(latter)))


def last_merge_kernel(flip_ref, head_ref, own_ref, recv_ref, cent_ref, attended_ref, *pack_refs):
    former, latter = in_order(flip_ref[0] != 0, own_ref, recv_ref)
    _, weight_sum, weighted = joined(unpacked_state(former), unpacked_state(latter))
    attended = (weighted / weight_sum).astype(BF16)
    attended_ref[...] = attended
    rows = attended.shape[0]
    for step, pack_ref in enumerate(pack_refs, 1):
        pack_ref[:rows, :] = attended
        pack_ref[rows:, :] = cent_ref[head_ref[0] ^ step].astype(BF16)


def spread_kernel(head_ref, own_cent_ref, attended_ref, *refs):
    pack_refs, (cent_ref, out_ref) = refs[:-2], refs[-2:]
    own = head_ref[0]
    requests, _, group, _ = out_ref.shape
    rows = requests * group
    cent_ref[own] = own_cent_ref[own]
    for step, pack_ref in enumerate((attended_ref, *pack_refs)):
        attended = pack_ref[:rows, :].astype(F32)
        if step:
            cent_ref[own ^ step] = pack_ref[rows:, :].astype(F32)
        for r in range(requests):
            out_ref[r, own ^ step] = attended[r * group : (r + 1) * group, :].astype(BF16)


def body(
    key_cache,
    value_cache,
    init_centroids,
    block_clusters,
    chosen_clusters,
    request_positions,
    queries,
):
    devices = lax.axis_size("ctx")
    index = lax.axis_index("ctx").astype(jnp.int32)
    heads, tok_dev, dim = key_cache.shape
    clusters = init_centroids.shape[1]
    requests, _, group, _ = queries.shape
    per_owner = clusters // devices
    spread = devices // heads
    levels = spread.bit_length() - 1
    if heads * spread != devices or 1 << levels != spread or heads & (heads - 1) or levels < 2:
        raise ValueError("unsupported mesh")
    bits = devices.bit_length() - 1
    head_bits = heads.bit_length() - 1
    head_basis = [2 << bit for bit in range(head_bits)]
    rank_basis = [1] + [1 << bit for bit in range(head_bits + 1, bits)]
    rank_basis[1] |= heads
    head_masks = [spanned(head_basis, s) for s in range(heads)]
    rank_masks = [spanned(rank_basis, s) for s in range(spread)]
    head_duals, rank_duals = duals(head_basis, rank_basis, devices)
    head, rank = coordinates(index, head_duals), coordinates(index, rank_duals)
    base = coordinates(rank, [sum(1 << j for j in range(levels) if rank_basis[j] >> bit & 1) for bit in range(bits)])
    half = clusters // 2
    rows = requests * group
    owned = heads * per_owner

    def over(array, bit):
        return lax.ppermute(array, "ctx", [(i, i ^ bit) for i in range(devices)])

    def pick(array, at, axis=0):
        return lax.dynamic_index_in_dim(array, at, axis, keepdims=False)

    slices = [pick(cache, head ^ s) for cache in (key_cache, value_cache) for s in range(heads)]
    slices = lax.optimization_barrier(tuple(slices))
    keys = [slices[0]] + [over(slices[s], head_masks[s]) for s in range(1, heads)]

    blocks = pick(init_centroids, head).reshape(devices, per_owner, dim)
    turned = [int(format(r, f"0{levels}b")[::-1], 2) for r in range(spread)]
    order = [rank_masks[r] ^ mask for r in turned for mask in head_masks]
    scalar_base = base.reshape(1)

    pass_flops = 4 * tok_dev * clusters * dim
    chunk_scratch = [pltpu.VMEM((clusters, tok_dev), F32), pltpu.VMEM((half, tok_dev), BF16)]
    sums, keep_weights, unit_cents = call(
        lambda base_ref, *refs: first_kernel(base_ref, order, *refs),
        [
            shape((half, dim), F32),
            shape((half, tok_dev), BF16),
            shape((clusters, dim), BF16),
        ],
        [scalar_base, keys[0], blocks],
        [pltpu.VMEM((clusters, dim), F32), *chunk_scratch],
        pass_flops,
        scalars=1,
    )
    values = [slices[heads]] + [over(slices[heads + s], head_masks[s]) for s in range(1, heads)]

    keep_weights = [keep_weights]
    for step in range(1, heads):
        sums, kept = call(
            pass_chunk,
            [shape((half, dim), F32 if step < heads - 1 else BF16), shape((half, tok_dev), BF16)],
            [keys[step], unit_cents, sums],
            chunk_scratch,
            pass_flops,
        )
        keep_weights.append(kept)
    send = sums
    (keep,) = call(
        functools.partial(keep_kernel, heads),
        [shape((half, dim), F32)],
        [*keys, *keep_weights],
        (),
        pass_flops * heads // 4,
    )
    keep, values[3] = lax.optimization_barrier((keep, values[3]))
    for level in range(levels - 1):
        total = keep + over(send, rank_basis[level]).astype(F32)
        if level < levels - 2:
            cut = total.shape[0] // 2
            keep, send = total[:cut], total[cut:].astype(BF16)
    rounded = total.astype(BF16)
    recv = over(rounded, rank_basis[levels - 1])
    (own_cents,) = call(cents_kernel, [shape(rounded.shape, BF16)], [rounded, recv])
    for level in range(levels - 2, 0, -1):
        own_cents = jnp.concatenate([own_cents, over(own_cents, rank_basis[level])])
    other_cents = over(own_cents, 1)

    tokens = heads * tok_dev
    unit_keys, raised, total = call(
        functools.partial(own_half_kernel, heads),
        [shape((tokens, dim), BF16), shape((half, tokens), BF16), shape((8, tokens), F32)],
        [*keys, own_cents],
        (),
        pass_flops * heads // 4,
    )
    part = half // 2
    part_scratch = [pltpu.VMEM((part, tokens), BF16), pltpu.VMEM((part, 128), F32)]
    sent = shape((part + 16, 2 * dim), BF16)
    kept = [shape((part, 2 * dim), F32), shape((8, part), F32)]
    send, inverse, early = call(
        functools.partial(other_half_kernel, heads),
        [sent, shape((8, tokens), F32), shape((part, tokens), BF16)],
        [*keys, *values, unit_keys, other_cents, total],
        [pltpu.VMEM((half, tok_dev), F32), *part_scratch],
        pass_flops * heads // 2,
    )
    later = call(
        functools.partial(part_kernel, heads, part, False),
        kept,
        [*keys, *values, raised, inverse],
        part_scratch,
        pass_flops * heads // 4,
    )
    recv = over(send, 1)
    (send,) = call(functools.partial(both_kernel, True), [sent], [*later, recv])
    (early_send,) = call(
        functools.partial(part_kernel, heads, 0, True),
        [sent],
        [*keys, *values, early, inverse],
        part_scratch,
        pass_flops * heads // 4,
    )
    keep, keep_mass = call(
        functools.partial(part_kernel, heads, 0, False),
        kept,
        [*keys, *values, raised, inverse],
        part_scratch,
        pass_flops * heads // 4,
    )
    early_recv = over(early_send, 1)
    keep, keep_mass = call(functools.partial(both_kernel, False), kept, [keep, keep_mass, early_recv])

    exact, own_queries, usable = call(
        functools.partial(exact_kernel, heads, head_masks, head_masks, per_owner),
        [shape((rows + 8, dim), F32), shape((rows, dim), F32), shape((rows, owned), F32)],
        [
            head.reshape(1),
            index.reshape(1),
            scalar_base,
            request_positions,
            block_clusters,
            *keys,
            *values,
            queries,
            chosen_clusters,
        ],
        (),
        4 * rows * heads * tok_dev * dim,
        scalars=5,
    )

    for level in range(1, levels - 1):
        recv = over(send, rank_basis[level])
        count = keep.shape[0] // 2
        keep, keep_mass, send = call(
            halve_kernel,
            [
                shape((count, 2 * dim), F32),
                shape((8, count), F32),
                shape((count + 16, 2 * dim), BF16),
            ],
            [keep, keep_mass, recv],
        )
    recv = over(send, rank_basis[levels - 1])
    state, centroids = call(
        summary_kernel,
        [shape((rows + 8, dim), F32), shape((owned, dim), F32)],
        [keep, keep_mass, recv, own_queries, usable, exact],
        (),
        4 * rows * owned * dim,
    )
    for level in range(levels - 1):
        flip = ((rank >> level) & 1).reshape(1)
        (state,) = call(
            merge_kernel,
            [shape((rows + 8, dim), F32)],
            [flip, state, over(state, rank_basis[level])],
            scalars=1,
        )
    flip = ((rank >> (levels - 1)) & 1).reshape(1)
    centroids = centroids.reshape(heads, per_owner, dim)
    attended, *packs = call(
        last_merge_kernel,
        [shape((rows, dim), BF16)] + [shape((rows + per_owner, dim), BF16)] * (heads - 1),
        [flip, head.reshape(1), state, over(state, rank_basis[levels - 1]), centroids],
        scalars=2,
    )
    packs = [over(pack, head_masks[step]) for step, pack in enumerate(packs, 1)]
    return call(
        spread_kernel,
        [shape((heads, per_owner, dim), F32), shape(queries.shape, BF16)],
        [head.reshape(1), centroids, attended, *packs],
        scalars=1,
    )


def solution(mesh):
    placed = (
        P(None, ("groups", "ctx"), None),
        P(None, ("groups", "ctx"), None),
        P(),
        P(None, "groups"),
        P("groups", None, None),
        P("groups"),
        P("groups", None, None, None),
    )
    return jax.shard_map(
        body,
        mesh=mesh,
        in_specs=placed,
        out_specs=(P(None, ("groups", "ctx"), None), P("groups", None, None, None)),
        check_vma=False,
    )
```

```python
import functools
import math

import jax
import jax.numpy as jnp
from jax import lax
from jax.experimental import pallas as pl
from jax.experimental.pallas import tpu as pltpu
from jax.sharding import PartitionSpec as P

BLOCK = 128
SHARPNESS = 16.0
EPSILON = 1e-06
NEGATIVE = -1e30
F32 = jnp.float32
BF16 = jnp.bfloat16
VMEM_BYTES = 48 * 1024 * 1024
TILE = 256


def to_unit(vectors):
    vectors = vectors.astype(F32)
    return (
        vectors
        * lax.rsqrt(jnp.mean(vectors * vectors, axis=-1, keepdims=True) + EPSILON)
        * vectors.shape[-1] ** (-0.5)
    )


def dot_nt(left, right):
    return lax.dot_general(left, right, (((1,), (1,)), ((), ())), preferred_element_type=F32)


def spanned(basis, number):
    return functools.reduce(lambda a, b: a ^ b, [m for j, m in enumerate(basis) if number >> j & 1], 0)


def duals(head_basis, rank_basis, devices):
    basis = [*head_basis, *rank_basis]
    found = [
        next(
            f
            for f in range(devices)
            if all((f & m).bit_count() % 2 == (j == k) for j, m in enumerate(basis))
        )
        for k in range(len(basis))
    ]
    return found[: len(head_basis)], found[len(head_basis) :]


def coordinates(number, masks):
    result = 0
    for place, mask in enumerate(masks):
        for bit in range(mask.bit_length()):
            if mask >> bit & 1:
                result = result ^ ((number >> bit & 1) << place)
    return result


def call(kernel, outs, args, scratch=(), flops=0, scalars=0):
    in_specs = [pl.BlockSpec(memory_space=pltpu.SMEM)] * scalars
    in_specs += [pl.BlockSpec(memory_space=pltpu.VMEM)] * (len(args) - scalars)
    touched = sum(a.size * a.dtype.itemsize for a in (*args, *outs))
    return pl.pallas_call(
        kernel,
        out_shape=tuple(outs),
        in_specs=in_specs,
        out_specs=tuple(pl.BlockSpec(memory_space=pltpu.VMEM) for _ in outs),
        scratch_shapes=list(scratch),
        compiler_params=pltpu.CompilerParams(vmem_limit_bytes=VMEM_BYTES),
        cost_estimate=pl.CostEstimate(flops=flops, bytes_accessed=touched, transcendentals=0),
    )(*args)


def shape(dims, dtype):
    return jax.ShapeDtypeStruct(dims, dtype)


def fill_raised(piece, unit_keys, raised_ref, row, first):
    tokens = unit_keys.shape[0]
    factor = SHARPNESS * math.log2(math.e)
    total = jnp.zeros((1, tokens), F32)
    tile = min(TILE, piece.shape[0])
    for at in range(0, piece.shape[0], tile):
        raised = jnp.exp2(dot_nt(piece[at : at + tile, :], unit_keys) * factor)
        raised_ref[row + at : row + at + tile, first : first + tokens] = raised.astype(
            raised_ref.dtype
        )
        total = total + jnp.sum(raised, axis=0, keepdims=True)
    return total


def fill_weights(raised_ref, inverse, weight_ref, rows, from_row, first, raised_first, mass_ref):
    tokens = inverse.shape[1]
    tile = min(TILE, rows)
    for at in range(0, rows, tile):
        raised = raised_ref[
            from_row + at : from_row + at + tile, raised_first : raised_first + tokens
        ]
        weights = raised.astype(F32) * inverse
        weight_ref[at : at + tile, first : first + tokens] = weights.astype(BF16)
        if mass_ref is not None:
            part = weights[:, :128]
            for lane in range(128, tokens, 128):
                part = part + weights[:, lane : lane + 128]
            if first == 0:
                mass_ref[at : at + tile, :] = part
            else:
                mass_ref[at : at + tile, :] += part


def product(out_ref, weight_ref, values, sums_ref=None, row=0):
    rows = weight_ref.shape[0]
    tile = min(TILE, rows)
    for at in range(0, rows, tile):
        sums = jnp.dot(weight_ref[at : at + tile, :], values, preferred_element_type=F32)
        if sums_ref is not None:
            sums = sums + sums_ref[row + at : row + at + tile, :]
        out_ref[at : at + tile, :] = sums.astype(out_ref.dtype)


def first_kernel(
    base_ref,
    order,
    key_ref,
    cent_ref,
    sums_ref,
    keep_weight_ref,
    unit_ref,
    cents_ref,
    raised_ref,
    weight_ref,
):
    per_owner = cent_ref.shape[1]
    for at, mask in enumerate(order):
        cents_ref[at * per_owner : (at + 1) * per_owner, :] = cent_ref[base_ref[0] ^ mask].astype(
            F32
        )
    unit_ref[...] = to_unit(cents_ref[...]).astype(BF16)
    pass_chunk(key_ref, unit_ref, None, sums_ref, keep_weight_ref, raised_ref, weight_ref)


def pass_chunk(key_ref, unit_ref, before_ref, sums_ref, keep_weight_ref, raised_ref, weight_ref):
    keys = key_ref[...]
    half = sums_ref.shape[0]
    inverse = 1.0 / fill_raised(unit_ref, to_unit(keys).astype(BF16), raised_ref, 0, 0)
    fill_weights(raised_ref, inverse, weight_ref, half, half, 0, 0, None)
    fill_weights(raised_ref, inverse, keep_weight_ref, half, 0, 0, 0, None)
    product(sums_ref, weight_ref, keys, before_ref)


def keep_kernel(count, *refs):
    key_refs, weight_refs, keep_ref = refs[:count], refs[count : 2 * count], refs[-1]
    weights = jnp.concatenate([ref[...] for ref in weight_refs], axis=1)
    keep_ref[...] = jnp.dot(weights, joined_rows(key_refs), preferred_element_type=F32)


def joined_rows(refs):
    return jnp.concatenate([ref[...] for ref in refs], axis=0)


def joined_pairs(key_refs, value_refs):
    return jnp.concatenate(
        [jnp.concatenate([k[...], v[...]], axis=1) for k, v in zip(key_refs, value_refs)], axis=0
    )


def packed_masses(row, lanes):
    count = row.shape[1]
    high = row.astype(BF16).astype(F32)
    low = row - high
    rows = []
    for part in (high, low):
        if count < lanes:
            rows.append(jnp.concatenate([part, jnp.zeros((1, lanes - count), F32)], axis=1))
        else:
            rows += [part[:, at : at + lanes] for at in range(0, count, lanes)]
    rows.append(jnp.zeros((16 - len(rows), lanes), F32))
    return jnp.concatenate(rows, axis=0).astype(BF16)


def unpacked_masses(block, count):
    block = block.astype(F32)
    lanes = block.shape[1]
    if count < lanes:
        return block[0:1, :count] + block[1:2, :count]
    rows = count // lanes
    return jnp.concatenate(
        [block[i : i + 1, :] + block[rows + i : rows + i + 1, :] for i in range(rows)], axis=1
    )


def cents_kernel(own_ref, recv_ref, out_ref):
    half = own_ref.shape[0] // 2
    for at in (0, half):
        recv = recv_ref[half - at : 2 * half - at, :]
        sums = own_ref[at : at + half, :].astype(F32) + recv.astype(F32)
        out_ref[at : at + half, :] = to_unit(sums).astype(BF16)


def own_half_kernel(count, *refs):
    key_refs, (cent_ref, unit_ref, raised_ref, total_ref) = refs[:count], refs[count:]
    first = 0
    for key_ref in key_refs:
        unit_keys = to_unit(key_ref[...]).astype(BF16)
        tokens = unit_keys.shape[0]
        unit_ref[first : first + tokens, :] = unit_keys
        total = fill_raised(cent_ref, unit_keys, raised_ref, 0, first)
        total_ref[:, first : first + tokens] = jnp.broadcast_to(total, (8, tokens))
        first += tokens


def other_half_kernel(count, *refs):
    pair_refs, refs = refs[: 2 * count], refs[2 * count :]
    unit_ref, cent_ref, total_ref, send_ref, inverse_ref, early_ref = refs[:6]
    raised_ref, weight_ref, mass_ref = refs[6:]
    rows, lanes = early_ref.shape[0], send_ref.shape[1]
    first = 0
    for key_ref in pair_refs[:count]:
        tokens = key_ref.shape[0]
        chunk = slice(first, first + tokens)
        total = fill_raised(cent_ref, unit_ref[chunk, :], raised_ref, 0, 0)
        inverse = 1.0 / (total_ref[0:1, chunk] + total)
        inverse_ref[:, chunk] = jnp.broadcast_to(inverse, (8, tokens))
        fill_weights(raised_ref, inverse, weight_ref, rows, rows, first, 0, mass_ref)
        early_ref[:, chunk] = raised_ref[:rows, :tokens]
        first += tokens
    masses = jnp.sum(mass_ref[...].T, axis=0, keepdims=True)
    send_ref[rows:, :] = packed_masses(masses, lanes)
    product(send_ref, weight_ref, joined_pairs(pair_refs[:count], pair_refs[count:]))


def part_kernel(count, row, to_send, *refs):
    pair_refs, refs = refs[: 2 * count], refs[2 * count :]
    raised_ref, inverse_ref, refs = refs[0], refs[1], refs[2:]
    out_ref, (weight_ref, mass_ref) = refs[0], refs[-2:]
    rows = weight_ref.shape[0]
    first = 0
    for key_ref in pair_refs[:count]:
        tokens = key_ref.shape[0]
        inverse = inverse_ref[0:1, first : first + tokens]
        fill_weights(raised_ref, inverse, weight_ref, rows, row, first, first, mass_ref)
        first += tokens
    masses = jnp.sum(mass_ref[...].T, axis=0, keepdims=True)
    if to_send:
        out_ref[rows:, :] = packed_masses(masses, out_ref.shape[1])
    else:
        refs[1][...] = jnp.broadcast_to(masses, refs[1].shape)
    product(out_ref, weight_ref, joined_pairs(pair_refs[:count], pair_refs[count:]))


def both_kernel(to_send, keep_ref, mass_ref, recv_ref, out_ref, *refs):
    count, lanes = keep_ref.shape
    masses = mass_ref[0:1, :] + unpacked_masses(recv_ref[count:, :], count)
    sums = keep_ref[...] + recv_ref[:count, :].astype(F32)
    out_ref[:count, :] = sums.astype(out_ref.dtype)
    if to_send:
        out_ref[count:, :] = packed_masses(masses, lanes)
    else:
        refs[0][...] = jnp.broadcast_to(masses, refs[0].shape)


def halve_kernel(keep_ref, mass_ref, recv_ref, keep_out_ref, mass_out_ref, send_ref):
    count, lanes = keep_ref.shape
    half = count // 2
    masses = mass_ref[0:1, :] + unpacked_masses(recv_ref[count:, :], count)
    keep_out_ref[...] = keep_ref[:half, :] + recv_ref[:half, :].astype(F32)
    mass_out_ref[...] = jnp.broadcast_to(masses[:, :half], mass_out_ref.shape)
    send_ref[:half, :] = (keep_ref[half:, :] + recv_ref[half:count, :].astype(F32)).astype(BF16)
    send_ref[half:, :] = packed_masses(masses[:, half:], lanes)


def as_line(column, dim):
    rows = column.shape[0]
    square = [jnp.broadcast_to(column, (rows, dim)), jnp.zeros((dim - rows, dim), F32)]
    return jnp.concatenate(square, axis=0).T[0:1, :]


def packed_state(peak, weight_sum, weighted):
    dim = weighted.shape[1]
    lines = [as_line(peak, dim), as_line(weight_sum, dim), jnp.zeros((6, dim), F32)]
    return jnp.concatenate([weighted, *lines], axis=0)


def sent_state(peak, weight_sum, weighted):
    dim = weighted.shape[1]
    lines = []
    for column in (peak, weight_sum):
        rest = as_line(column, dim)
        for _ in range(3):
            lines.append(rest.astype(BF16).astype(F32))
            rest = rest - lines[-1]
    lines.append(jnp.zeros((10, dim), F32))
    return jnp.concatenate([weighted, *lines], axis=0).astype(BF16)


def softmax_part(scores, usable, values):
    peak = jnp.max(jnp.where(usable, scores, NEGATIVE), axis=1, keepdims=True)
    probability = jnp.where(usable, jnp.exp(scores - peak), 0.0).astype(BF16)
    weight_sum = jnp.sum(probability.astype(F32), axis=1, keepdims=True)
    return peak, weight_sum, jnp.dot(probability, values, preferred_element_type=F32)


def joined(former, latter):
    peak = jnp.maximum(former[0], latter[0])
    left, right = jnp.exp(former[0] - peak), jnp.exp(latter[0] - peak)
    return (
        peak,
        former[1] * left + latter[1] * right,
        former[2] * left + latter[2] * right,
    )


def unpacked_state(state):
    dim = state.shape[1]
    short = state.dtype == BF16
    rows = state.shape[0] - (16 if short else 8)
    state = state.astype(F32)
    lines = [state[at : at + 1, :] for at in range(rows, rows + (6 if short else 2))]
    if short:
        lines = [lines[at] + lines[at + 1] + lines[at + 2] for at in (0, 3)]
    columns = [jnp.broadcast_to(line, (dim, dim)).T[:rows, :] for line in lines]
    return columns[0], columns[1], state[:rows, :]


def exact_kernel(count, head_masks, owned_by, per_owner, *refs):
    scalar_refs, key_refs, value_refs = (
        refs[:5],
        refs[5 : 5 + count],
        refs[5 + count : 5 + 2 * count],
    )
    head_ref, index_ref, base_ref, position_ref, cluster_ref = scalar_refs
    query_ref, chosen_ref, out_ref, own_query_ref, usable_ref = refs[5 + 2 * count :]
    head, index, base = head_ref[0], index_ref[0], base_ref[0]
    requests, _, group, dim = query_ref.shape
    rows = requests * group
    for r in range(requests):
        own_query_ref[r * group : (r + 1) * group, :] = query_ref[r, head].astype(F32)
    queries = own_query_ref[...].astype(BF16)
    ksel = chosen_ref.shape[2]
    chosen = jnp.concatenate(
        [
            jnp.broadcast_to(chosen_ref[r, pl.ds(head, 1), :], (group, ksel))
            for r in range(requests)
        ],
        axis=0,
    )
    positions = jnp.concatenate(
        [jnp.full((group, 1), position_ref[r], jnp.int32) for r in range(requests)], axis=0
    )
    lane = lax.broadcasted_iota(jnp.int32, (rows, BLOCK), 1)
    blocks = key_refs[0].shape[0] // BLOCK
    parts = []
    for mask in head_masks:
        for block in range(blocks):
            at = (index ^ mask) * blocks + block
            picked = jnp.max(
                jnp.where(chosen == cluster_ref[head, at], 1, 0).astype(F32), axis=1, keepdims=True
            )
            limit = jnp.where(picked > 0.5, positions - at * BLOCK, 0)
            parts.append(jnp.where(lane < limit, 1.0, 0.0))
    scores = dot_nt(queries, joined_rows(key_refs)) * dim ** (-0.5)
    usable = jnp.concatenate(parts, axis=1) > 0.5
    out_ref[...] = packed_state(*softmax_part(scores, usable, joined_rows(value_refs)))
    owned = usable_ref.shape[1]
    place = lax.broadcasted_iota(jnp.int32, (rows, owned), 1)
    ids = place
    for part, mask in enumerate(owned_by):
        shift = (base ^ mask) * per_owner - part * per_owner
        ids = jnp.where((place >= part * per_owner) & (place < (part + 1) * per_owner), place + shift, ids)
    free = jnp.ones((rows, owned), F32)
    for k in range(ksel):
        free = jnp.where(chosen[:, k : k + 1] == ids, 0.0, free)
    usable_ref[...] = free


def summary_kernel(
    keep_ref, mass_ref, recv_ref, query_ref, usable_ref, exact_ref, state_ref, cent_ref
):
    count, lanes = keep_ref.shape
    dim = lanes // 2
    masses = mass_ref[0:1, :] + unpacked_masses(recv_ref[count:, :], count)
    sums = keep_ref[...] + recv_ref[:count, :].astype(F32)
    cent_ref[...] = to_unit(sums[:, :dim])
    column = jnp.broadcast_to(masses, (dim, count)).T
    mean_keys = (sums[:, :dim] / column).astype(BF16)
    mean_values = (sums[:, dim:] / column).astype(BF16)
    queries = query_ref[...].astype(BF16)
    scores = dot_nt(queries, mean_keys) * dim ** (-0.5) + jnp.log(masses)
    state = softmax_part(scores, usable_ref[...] > 0.5, mean_values)
    state_ref[...] = packed_state(*joined(unpacked_state(exact_ref[...]), state))


def in_order(flip, own_ref, recv_ref):
    own, recv = own_ref[...], recv_ref[...]
    return jnp.where(flip, recv, own), jnp.where(flip, own, recv)


def merge_kernel(flip_ref, own_ref, recv_ref, out_ref):
    former, latter = in_order(flip_ref[0] != 0, own_ref, recv_ref)
    out_ref[...] = sent_state(*joined(unpacked_state(former), unpacked_state(latter)))


def last_merge_kernel(flip_ref, head_ref, own_ref, recv_ref, cent_ref, attended_ref, *pack_refs):
    former, latter = in_order(flip_ref[0] != 0, own_ref, recv_ref)
    _, weight_sum, weighted = joined(unpacked_state(former), unpacked_state(latter))
    attended = (weighted / weight_sum).astype(BF16)
    attended_ref[...] = attended
    rows = attended.shape[0]
    for step, pack_ref in enumerate(pack_refs, 1):
        pack_ref[:rows, :] = attended
        pack_ref[rows:, :] = cent_ref[head_ref[0] ^ step].astype(BF16)


def spread_kernel(head_ref, own_cent_ref, attended_ref, *refs):
    pack_refs, (cent_ref, out_ref) = refs[:-2], refs[-2:]
    own = head_ref[0]
    requests, _, group, _ = out_ref.shape
    rows = requests * group
    cent_ref[own] = own_cent_ref[own]
    for step, pack_ref in enumerate((attended_ref, *pack_refs)):
        attended = pack_ref[:rows, :].astype(F32)
        if step:
            cent_ref[own ^ step] = pack_ref[rows:, :].astype(F32)
        for r in range(requests):
            out_ref[r, own ^ step] = attended[r * group : (r + 1) * group, :].astype(BF16)


def body(
    key_cache,
    value_cache,
    init_centroids,
    block_clusters,
    chosen_clusters,
    request_positions,
    queries,
):
    devices = lax.axis_size("ctx")
    index = lax.axis_index("ctx").astype(jnp.int32)
    heads, tok_dev, dim = key_cache.shape
    clusters = init_centroids.shape[1]
    requests, _, group, _ = queries.shape
    per_owner = clusters // devices
    spread = devices // heads
    levels = spread.bit_length() - 1
    if heads * spread != devices or 1 << levels != spread or heads & (heads - 1) or levels < 2:
        raise ValueError("unsupported mesh")
    bits = devices.bit_length() - 1
    head_bits = heads.bit_length() - 1
    head_basis = [2 << bit for bit in range(head_bits)]
    rank_basis = [1] + [1 << bit for bit in range(head_bits + 1, bits)]
    rank_basis[1] |= heads
    head_masks = [spanned(head_basis, s) for s in range(heads)]
    rank_masks = [spanned(rank_basis, s) for s in range(spread)]
    head_duals, rank_duals = duals(head_basis, rank_basis, devices)
    head, rank = coordinates(index, head_duals), coordinates(index, rank_duals)
    base = coordinates(rank, [sum(1 << j for j in range(levels) if rank_basis[j] >> bit & 1) for bit in range(bits)])
    half = clusters // 2
    rows = requests * group
    owned = heads * per_owner

    def over(array, bit):
        return lax.ppermute(array, "ctx", [(i, i ^ bit) for i in range(devices)])

    def pick(array, at, axis=0):
        return lax.dynamic_index_in_dim(array, at, axis, keepdims=False)

    slices = [pick(cache, head ^ s) for cache in (key_cache, value_cache) for s in range(heads)]
    slices = lax.optimization_barrier(tuple(slices))
    keys = [slices[0]] + [over(slices[s], head_masks[s]) for s in range(1, heads)]

    blocks = pick(init_centroids, head).reshape(devices, per_owner, dim)
    turned = [int(format(r, f"0{levels}b")[::-1], 2) for r in range(spread)]
    order = [rank_masks[r] ^ mask for r in turned for mask in head_masks]
    scalar_base = base.reshape(1)

    pass_flops = 4 * tok_dev * clusters * dim
    chunk_scratch = [pltpu.VMEM((clusters, tok_dev), F32), pltpu.VMEM((half, tok_dev), BF16)]
    sums, keep_weights, unit_cents = call(
        lambda base_ref, *refs: first_kernel(base_ref, order, *refs),
        [
            shape((half, dim), F32),
            shape((half, tok_dev), BF16),
            shape((clusters, dim), BF16),
        ],
        [scalar_base, keys[0], blocks],
        [pltpu.VMEM((clusters, dim), F32), *chunk_scratch],
        pass_flops,
        scalars=1,
    )
    values = [slices[heads]] + [over(slices[heads + s], head_masks[s]) for s in range(1, heads)]

    keep_weights = [keep_weights]
    for step in range(1, heads):
        sums, kept = call(
            pass_chunk,
            [shape((half, dim), F32 if step < heads - 1 else BF16), shape((half, tok_dev), BF16)],
            [keys[step], unit_cents, sums],
            chunk_scratch,
            pass_flops,
        )
        keep_weights.append(kept)
    send = sums
    (keep,) = call(
        functools.partial(keep_kernel, heads),
        [shape((half, dim), F32)],
        [*keys, *keep_weights],
        (),
        pass_flops * heads // 4,
    )
    keep, values[3] = lax.optimization_barrier((keep, values[3]))
    for level in range(levels - 1):
        total = keep + over(send, rank_basis[level]).astype(F32)
        if level < levels - 2:
            cut = total.shape[0] // 2
            keep, send = total[:cut], total[cut:].astype(BF16)
    rounded = total.astype(BF16)
    recv = over(rounded, rank_basis[levels - 1])
    (own_cents,) = call(cents_kernel, [shape(rounded.shape, BF16)], [rounded, recv])
    for level in range(levels - 2, 0, -1):
        own_cents = jnp.concatenate([own_cents, over(own_cents, rank_basis[level])])
    other_cents = over(own_cents, 1)

    tokens = heads * tok_dev
    unit_keys, raised, total = call(
        functools.partial(own_half_kernel, heads),
        [shape((tokens, dim), BF16), shape((half, tokens), F32), shape((8, tokens), F32)],
        [*keys, own_cents],
        (),
        pass_flops * heads // 4,
    )
    part = half // 2
    part_scratch = [pltpu.VMEM((part, tokens), BF16), pltpu.VMEM((part, 128), F32)]
    sent = shape((part + 16, 2 * dim), BF16)
    kept = [shape((part, 2 * dim), F32), shape((8, part), F32)]
    send, inverse, early = call(
        functools.partial(other_half_kernel, heads),
        [sent, shape((8, tokens), F32), shape((part, tokens), F32)],
        [*keys, *values, unit_keys, other_cents, total],
        [pltpu.VMEM((half, tok_dev), F32), *part_scratch],
        pass_flops * heads // 2,
    )
    later = call(
        functools.partial(part_kernel, heads, part, False),
        kept,
        [*keys, *values, raised, inverse],
        part_scratch,
        pass_flops * heads // 4,
    )
    recv = over(send, 1)
    (send,) = call(functools.partial(both_kernel, True), [sent], [*later, recv])
    (early_send,) = call(
        functools.partial(part_kernel, heads, 0, True),
        [sent],
        [*keys, *values, early, inverse],
        part_scratch,
        pass_flops * heads // 4,
    )
    keep, keep_mass = call(
        functools.partial(part_kernel, heads, 0, False),
        kept,
        [*keys, *values, raised, inverse],
        part_scratch,
        pass_flops * heads // 4,
    )
    early_recv = over(early_send, 1)
    keep, keep_mass = call(functools.partial(both_kernel, False), kept, [keep, keep_mass, early_recv])

    exact, own_queries, usable = call(
        functools.partial(exact_kernel, heads, head_masks, head_masks, per_owner),
        [shape((rows + 8, dim), F32), shape((rows, dim), F32), shape((rows, owned), F32)],
        [
            head.reshape(1),
            index.reshape(1),
            scalar_base,
            request_positions,
            block_clusters,
            *keys,
            *values,
            queries,
            chosen_clusters,
        ],
        (),
        4 * rows * heads * tok_dev * dim,
        scalars=5,
    )

    for level in range(1, levels - 1):
        recv = over(send, rank_basis[level])
        count = keep.shape[0] // 2
        keep, keep_mass, send = call(
            halve_kernel,
            [
                shape((count, 2 * dim), F32),
                shape((8, count), F32),
                shape((count + 16, 2 * dim), BF16),
            ],
            [keep, keep_mass, recv],
        )
    recv = over(send, rank_basis[levels - 1])
    state, centroids = call(
        summary_kernel,
        [shape((rows + 8, dim), F32), shape((owned, dim), F32)],
        [keep, keep_mass, recv, own_queries, usable, exact],
        (),
        4 * rows * owned * dim,
    )
    for level in range(levels - 1):
        flip = ((rank >> level) & 1).reshape(1)
        (state,) = call(
            merge_kernel,
            [shape((rows + 16, dim), BF16)],
            [flip, state, over(state, rank_basis[level])],
            scalars=1,
        )
    flip = ((rank >> (levels - 1)) & 1).reshape(1)
    centroids = centroids.reshape(heads, per_owner, dim)
    attended, *packs = call(
        last_merge_kernel,
        [shape((rows, dim), BF16)] + [shape((rows + per_owner, dim), BF16)] * (heads - 1),
        [flip, head.reshape(1), state, over(state, rank_basis[levels - 1]), centroids],
        scalars=2,
    )
    packs = [over(pack, head_masks[step]) for step, pack in enumerate(packs, 1)]
    return call(
        spread_kernel,
        [shape((heads, per_owner, dim), F32), shape(queries.shape, BF16)],
        [head.reshape(1), centroids, attended, *packs],
        scalars=1,
    )


def solution(mesh):
    placed = (
        P(None, ("groups", "ctx"), None),
        P(None, ("groups", "ctx"), None),
        P(),
        P(None, "groups"),
        P("groups", None, None),
        P("groups"),
        P("groups", None, None, None),
    )
    return jax.shard_map(
        body,
        mesh=mesh,
        in_specs=placed,
        out_specs=(P(None, ("groups", "ctx"), None), P("groups", None, None, None)),
        check_vma=False,
    )
```

```python
import functools
import math

import jax
import jax.numpy as jnp
from jax import lax
from jax.experimental import pallas as pl
from jax.experimental.pallas import tpu as pltpu
from jax.sharding import PartitionSpec as P

BLOCK = 128
SHARPNESS = 16.0
EPSILON = 1e-06
NEGATIVE = -1e30
F32 = jnp.float32
BF16 = jnp.bfloat16
VMEM_BYTES = 48 * 1024 * 1024
TILE = 256


def to_unit(vectors):
    vectors = vectors.astype(F32)
    return (
        vectors
        * lax.rsqrt(jnp.mean(vectors * vectors, axis=-1, keepdims=True) + EPSILON)
        * vectors.shape[-1] ** (-0.5)
    )


def dot_nt(left, right):
    return lax.dot_general(left, right, (((1,), (1,)), ((), ())), preferred_element_type=F32)


def spanned(basis, number):
    return functools.reduce(lambda a, b: a ^ b, [m for j, m in enumerate(basis) if number >> j & 1], 0)


def duals(head_basis, rank_basis, devices):
    basis = [*head_basis, *rank_basis]
    found = [
        next(
            f
            for f in range(devices)
            if all((f & m).bit_count() % 2 == (j == k) for j, m in enumerate(basis))
        )
        for k in range(len(basis))
    ]
    return found[: len(head_basis)], found[len(head_basis) :]


def coordinates(number, masks):
    result = 0
    for place, mask in enumerate(masks):
        for bit in range(mask.bit_length()):
            if mask >> bit & 1:
                result = result ^ ((number >> bit & 1) << place)
    return result


def call(kernel, outs, args, scratch=(), flops=0, scalars=0):
    in_specs = [pl.BlockSpec(memory_space=pltpu.SMEM)] * scalars
    in_specs += [pl.BlockSpec(memory_space=pltpu.VMEM)] * (len(args) - scalars)
    touched = sum(a.size * a.dtype.itemsize for a in (*args, *outs))
    return pl.pallas_call(
        kernel,
        out_shape=tuple(outs),
        in_specs=in_specs,
        out_specs=tuple(pl.BlockSpec(memory_space=pltpu.VMEM) for _ in outs),
        scratch_shapes=list(scratch),
        compiler_params=pltpu.CompilerParams(vmem_limit_bytes=VMEM_BYTES),
        cost_estimate=pl.CostEstimate(flops=flops, bytes_accessed=touched, transcendentals=0),
    )(*args)


def shape(dims, dtype):
    return jax.ShapeDtypeStruct(dims, dtype)


def fill_raised(piece, unit_keys, raised_ref, row, first):
    tokens = unit_keys.shape[0]
    factor = SHARPNESS * math.log2(math.e)
    total = jnp.zeros((1, tokens), F32)
    tile = min(TILE, piece.shape[0])
    for at in range(0, piece.shape[0], tile):
        raised = jnp.exp2(dot_nt(piece[at : at + tile, :], unit_keys) * factor)
        raised_ref[row + at : row + at + tile, first : first + tokens] = raised.astype(
            raised_ref.dtype
        )
        total = total + jnp.sum(raised, axis=0, keepdims=True)
    return total


def fill_weights(raised_ref, inverse, weight_ref, rows, from_row, first, raised_first, mass_ref):
    tokens = inverse.shape[1]
    tile = min(TILE, rows)
    for at in range(0, rows, tile):
        raised = raised_ref[
            from_row + at : from_row + at + tile, raised_first : raised_first + tokens
        ]
        weights = raised.astype(F32) * inverse
        weight_ref[at : at + tile, first : first + tokens] = weights.astype(BF16)
        if mass_ref is not None:
            part = weights[:, :128]
            for lane in range(128, tokens, 128):
                part = part + weights[:, lane : lane + 128]
            if first == 0:
                mass_ref[at : at + tile, :] = part
            else:
                mass_ref[at : at + tile, :] += part


def product(out_ref, weight_ref, values, sums_ref=None, row=0):
    rows = weight_ref.shape[0]
    tile = min(TILE, rows)
    for at in range(0, rows, tile):
        sums = jnp.dot(weight_ref[at : at + tile, :], values, preferred_element_type=F32)
        if sums_ref is not None:
            sums = sums + sums_ref[row + at : row + at + tile, :]
        out_ref[at : at + tile, :] = sums.astype(out_ref.dtype)


def first_kernel(
    base_ref,
    order,
    key_ref,
    cent_ref,
    sums_ref,
    keep_raised_ref,
    inverse_ref,
    unit_ref,
    cents_ref,
    raised_ref,
    weight_ref,
):
    per_owner = cent_ref.shape[1]
    for at, mask in enumerate(order):
        cents_ref[at * per_owner : (at + 1) * per_owner, :] = cent_ref[base_ref[0] ^ mask].astype(
            F32
        )
    unit_ref[...] = to_unit(cents_ref[...]).astype(BF16)
    pass_chunk(
        key_ref, unit_ref, None, sums_ref, keep_raised_ref, inverse_ref, raised_ref, weight_ref
    )


def pass_chunk(
    key_ref, unit_ref, before_ref, sums_ref, keep_raised_ref, inverse_ref, raised_ref, weight_ref
):
    keys = key_ref[...]
    half = sums_ref.shape[0]
    unit_keys = to_unit(keys).astype(BF16)
    total = fill_raised(unit_ref.at[pl.ds(0, half)], unit_keys, keep_raised_ref, 0, 0)
    total = total + fill_raised(unit_ref.at[pl.ds(half, half)], unit_keys, raised_ref, 0, 0)
    inverse = 1.0 / total
    inverse_ref[...] = jnp.broadcast_to(inverse, inverse_ref.shape)
    fill_weights(raised_ref, inverse, weight_ref, half, 0, 0, 0, None)
    product(sums_ref, weight_ref, keys, before_ref)


def keep_kernel(count, *refs):
    key_refs, raised_refs, inverse_refs = refs[:count], refs[count : 2 * count], refs[2 * count : 3 * count]
    keep_ref, weight_ref = refs[3 * count :]
    first = 0
    for raised_ref, inverse_ref in zip(raised_refs, inverse_refs):
        rows, tokens = raised_ref.shape
        fill_weights(raised_ref, inverse_ref[0:1, :], weight_ref, rows, 0, first, 0, None)
        first += tokens
    product(keep_ref, weight_ref, joined_rows(key_refs))


def joined_rows(refs):
    return jnp.concatenate([ref[...] for ref in refs], axis=0)


def joined_pairs(key_refs, value_refs):
    return jnp.concatenate(
        [jnp.concatenate([k[...], v[...]], axis=1) for k, v in zip(key_refs, value_refs)], axis=0
    )


def packed_masses(row, lanes):
    count = row.shape[1]
    high = row.astype(BF16).astype(F32)
    low = row - high
    rows = []
    for part in (high, low):
        if count < lanes:
            rows.append(jnp.concatenate([part, jnp.zeros((1, lanes - count), F32)], axis=1))
        else:
            rows += [part[:, at : at + lanes] for at in range(0, count, lanes)]
    rows.append(jnp.zeros((16 - len(rows), lanes), F32))
    return jnp.concatenate(rows, axis=0).astype(BF16)


def unpacked_masses(block, count):
    block = block.astype(F32)
    lanes = block.shape[1]
    if count < lanes:
        return block[0:1, :count] + block[1:2, :count]
    rows = count // lanes
    return jnp.concatenate(
        [block[i : i + 1, :] + block[rows + i : rows + i + 1, :] for i in range(rows)], axis=1
    )


def cents_kernel(own_ref, recv_ref, out_ref):
    half = own_ref.shape[0] // 2
    for at in (0, half):
        recv = recv_ref[half - at : 2 * half - at, :]
        sums = own_ref[at : at + half, :].astype(F32) + recv.astype(F32)
        out_ref[at : at + half, :] = to_unit(sums).astype(BF16)


def own_half_kernel(count, *refs):
    key_refs, (cent_ref, unit_ref, raised_ref, total_ref) = refs[:count], refs[count:]
    first = 0
    for key_ref in key_refs:
        unit_keys = to_unit(key_ref[...]).astype(BF16)
        tokens = unit_keys.shape[0]
        unit_ref[first : first + tokens, :] = unit_keys
        total = fill_raised(cent_ref, unit_keys, raised_ref, 0, first)
        total_ref[:, first : first + tokens] = jnp.broadcast_to(total, (8, tokens))
        first += tokens


def other_half_kernel(count, *refs):
    pair_refs, refs = refs[: 2 * count], refs[2 * count :]
    unit_ref, cent_ref, total_ref, send_ref, inverse_ref, early_ref = refs[:6]
    raised_ref, weight_ref, mass_ref = refs[6:]
    rows, lanes = early_ref.shape[0], send_ref.shape[1]
    first = 0
    for key_ref in pair_refs[:count]:
        tokens = key_ref.shape[0]
        chunk = slice(first, first + tokens)
        total = fill_raised(cent_ref, unit_ref[chunk, :], raised_ref, 0, 0)
        inverse = 1.0 / (total_ref[0:1, chunk] + total)
        inverse_ref[:, chunk] = jnp.broadcast_to(inverse, (8, tokens))
        fill_weights(raised_ref, inverse, weight_ref, rows, rows, first, 0, mass_ref)
        early_ref[:, chunk] = raised_ref[:rows, :tokens]
        first += tokens
    masses = jnp.sum(mass_ref[...].T, axis=0, keepdims=True)
    send_ref[rows:, :] = packed_masses(masses, lanes)
    product(send_ref, weight_ref, joined_pairs(pair_refs[:count], pair_refs[count:]))


def part_kernel(count, row, to_send, *refs):
    pair_refs, refs = refs[: 2 * count], refs[2 * count :]
    raised_ref, inverse_ref, refs = refs[0], refs[1], refs[2:]
    out_ref, (weight_ref, mass_ref) = refs[0], refs[-2:]
    rows = weight_ref.shape[0]
    first = 0
    for key_ref in pair_refs[:count]:
        tokens = key_ref.shape[0]
        inverse = inverse_ref[0:1, first : first + tokens]
        fill_weights(raised_ref, inverse, weight_ref, rows, row, first, first, mass_ref)
        first += tokens
    masses = jnp.sum(mass_ref[...].T, axis=0, keepdims=True)
    if to_send:
        out_ref[rows:, :] = packed_masses(masses, out_ref.shape[1])
    else:
        refs[1][...] = jnp.broadcast_to(masses, refs[1].shape)
    product(out_ref, weight_ref, joined_pairs(pair_refs[:count], pair_refs[count:]))


def both_kernel(to_send, keep_ref, mass_ref, recv_ref, out_ref, *refs):
    count, lanes = keep_ref.shape
    masses = mass_ref[0:1, :] + unpacked_masses(recv_ref[count:, :], count)
    sums = keep_ref[...] + recv_ref[:count, :].astype(F32)
    out_ref[:count, :] = sums.astype(out_ref.dtype)
    if to_send:
        out_ref[count:, :] = packed_masses(masses, lanes)
    else:
        refs[0][...] = jnp.broadcast_to(masses, refs[0].shape)


def halve_kernel(keep_ref, mass_ref, recv_ref, keep_out_ref, mass_out_ref, send_ref):
    count, lanes = keep_ref.shape
    half = count // 2
    masses = mass_ref[0:1, :] + unpacked_masses(recv_ref[count:, :], count)
    keep_out_ref[...] = keep_ref[:half, :] + recv_ref[:half, :].astype(F32)
    mass_out_ref[...] = jnp.broadcast_to(masses[:, :half], mass_out_ref.shape)
    send_ref[:half, :] = (keep_ref[half:, :] + recv_ref[half:count, :].astype(F32)).astype(BF16)
    send_ref[half:, :] = packed_masses(masses[:, half:], lanes)


def as_line(column, dim):
    rows = column.shape[0]
    square = [jnp.broadcast_to(column, (rows, dim)), jnp.zeros((dim - rows, dim), F32)]
    return jnp.concatenate(square, axis=0).T[0:1, :]


def packed_state(peak, weight_sum, weighted):
    dim = weighted.shape[1]
    lines = [as_line(peak, dim), as_line(weight_sum, dim), jnp.zeros((6, dim), F32)]
    return jnp.concatenate([weighted, *lines], axis=0)


def sent_state(peak, weight_sum, weighted):
    dim = weighted.shape[1]
    lines = []
    for column in (peak, weight_sum):
        rest = as_line(column, dim)
        for _ in range(3):
            lines.append(rest.astype(BF16).astype(F32))
            rest = rest - lines[-1]
    lines.append(jnp.zeros((10, dim), F32))
    return jnp.concatenate([weighted, *lines], axis=0).astype(BF16)


def softmax_part(scores, usable, values):
    peak = jnp.max(jnp.where(usable, scores, NEGATIVE), axis=1, keepdims=True)
    probability = jnp.where(usable, jnp.exp(scores - peak), 0.0).astype(BF16)
    weight_sum = jnp.sum(probability.astype(F32), axis=1, keepdims=True)
    return peak, weight_sum, jnp.dot(probability, values, preferred_element_type=F32)


def joined(former, latter):
    peak = jnp.maximum(former[0], latter[0])
    left, right = jnp.exp(former[0] - peak), jnp.exp(latter[0] - peak)
    return (
        peak,
        former[1] * left + latter[1] * right,
        former[2] * left + latter[2] * right,
    )


def unpacked_state(state):
    dim = state.shape[1]
    short = state.dtype == BF16
    rows = state.shape[0] - (16 if short else 8)
    state = state.astype(F32)
    lines = [state[at : at + 1, :] for at in range(rows, rows + (6 if short else 2))]
    if short:
        lines = [lines[at] + lines[at + 1] + lines[at + 2] for at in (0, 3)]
    columns = [jnp.broadcast_to(line, (dim, dim)).T[:rows, :] for line in lines]
    return columns[0], columns[1], state[:rows, :]


def exact_kernel(count, head_masks, owned_by, per_owner, *refs):
    scalar_refs, key_refs, value_refs = (
        refs[:5],
        refs[5 : 5 + count],
        refs[5 + count : 5 + 2 * count],
    )
    head_ref, index_ref, base_ref, position_ref, cluster_ref = scalar_refs
    query_ref, chosen_ref, out_ref, own_query_ref, usable_ref = refs[5 + 2 * count :]
    head, index, base = head_ref[0], index_ref[0], base_ref[0]
    requests, _, group, dim = query_ref.shape
    rows = requests * group
    for r in range(requests):
        own_query_ref[r * group : (r + 1) * group, :] = query_ref[r, head].astype(F32)
    queries = own_query_ref[...].astype(BF16)
    ksel = chosen_ref.shape[2]
    chosen = jnp.concatenate(
        [
            jnp.broadcast_to(chosen_ref[r, pl.ds(head, 1), :], (group, ksel))
            for r in range(requests)
        ],
        axis=0,
    )
    positions = jnp.concatenate(
        [jnp.full((group, 1), position_ref[r], jnp.int32) for r in range(requests)], axis=0
    )
    lane = lax.broadcasted_iota(jnp.int32, (rows, BLOCK), 1)
    blocks = key_refs[0].shape[0] // BLOCK
    parts = []
    for mask in head_masks:
        for block in range(blocks):
            at = (index ^ mask) * blocks + block
            picked = jnp.max(
                jnp.where(chosen == cluster_ref[head, at], 1, 0).astype(F32), axis=1, keepdims=True
            )
            limit = jnp.where(picked > 0.5, positions - at * BLOCK, 0)
            parts.append(jnp.where(lane < limit, 1.0, 0.0))
    scores = dot_nt(queries, joined_rows(key_refs)) * dim ** (-0.5)
    usable = jnp.concatenate(parts, axis=1) > 0.5
    out_ref[...] = packed_state(*softmax_part(scores, usable, joined_rows(value_refs)))
    owned = usable_ref.shape[1]
    place = lax.broadcasted_iota(jnp.int32, (rows, owned), 1)
    ids = place
    for part, mask in enumerate(owned_by):
        shift = (base ^ mask) * per_owner - part * per_owner
        ids = jnp.where((place >= part * per_owner) & (place < (part + 1) * per_owner), place + shift, ids)
    free = jnp.ones((rows, owned), F32)
    for k in range(ksel):
        free = jnp.where(chosen[:, k : k + 1] == ids, 0.0, free)
    usable_ref[...] = free


def summary_kernel(
    keep_ref, mass_ref, recv_ref, query_ref, usable_ref, exact_ref, state_ref, cent_ref
):
    count, lanes = keep_ref.shape
    dim = lanes // 2
    masses = mass_ref[0:1, :] + unpacked_masses(recv_ref[count:, :], count)
    sums = keep_ref[...] + recv_ref[:count, :].astype(F32)
    cent_ref[...] = to_unit(sums[:, :dim])
    column = jnp.broadcast_to(masses, (dim, count)).T
    mean_keys = (sums[:, :dim] / column).astype(BF16)
    mean_values = (sums[:, dim:] / column).astype(BF16)
    queries = query_ref[...].astype(BF16)
    scores = dot_nt(queries, mean_keys) * dim ** (-0.5) + jnp.log(masses)
    state = softmax_part(scores, usable_ref[...] > 0.5, mean_values)
    state_ref[...] = packed_state(*joined(unpacked_state(exact_ref[...]), state))


def in_order(flip, own_ref, recv_ref):
    own, recv = own_ref[...], recv_ref[...]
    return jnp.where(flip, recv, own), jnp.where(flip, own, recv)


def merge_kernel(flip_ref, own_ref, recv_ref, out_ref):
    former, latter = in_order(flip_ref[0] != 0, own_ref, recv_ref)
    out_ref[...] = sent_state(*joined(unpacked_state(former), unpacked_state(latter)))


def last_merge_kernel(flip_ref, head_ref, own_ref, recv_ref, cent_ref, attended_ref, *pack_refs):
    former, latter = in_order(flip_ref[0] != 0, own_ref, recv_ref)
    _, weight_sum, weighted = joined(unpacked_state(former), unpacked_state(latter))
    attended = (weighted / weight_sum).astype(BF16)
    attended_ref[...] = attended
    rows = attended.shape[0]
    for step, pack_ref in enumerate(pack_refs, 1):
        pack_ref[:rows, :] = attended
        pack_ref[rows:, :] = cent_ref[head_ref[0] ^ step].astype(BF16)


def spread_kernel(head_ref, own_cent_ref, attended_ref, *refs):
    pack_refs, (cent_ref, out_ref) = refs[:-2], refs[-2:]
    own = head_ref[0]
    requests, _, group, _ = out_ref.shape
    rows = requests * group
    cent_ref[own] = own_cent_ref[own]
    for step, pack_ref in enumerate((attended_ref, *pack_refs)):
        attended = pack_ref[:rows, :].astype(F32)
        if step:
            cent_ref[own ^ step] = pack_ref[rows:, :].astype(F32)
        for r in range(requests):
            out_ref[r, own ^ step] = attended[r * group : (r + 1) * group, :].astype(BF16)


def body(
    key_cache,
    value_cache,
    init_centroids,
    block_clusters,
    chosen_clusters,
    request_positions,
    queries,
):
    devices = lax.axis_size("ctx")
    index = lax.axis_index("ctx").astype(jnp.int32)
    heads, tok_dev, dim = key_cache.shape
    clusters = init_centroids.shape[1]
    requests, _, group, _ = queries.shape
    per_owner = clusters // devices
    spread = devices // heads
    levels = spread.bit_length() - 1
    if heads * spread != devices or 1 << levels != spread or heads & (heads - 1) or levels < 2:
        raise ValueError("unsupported mesh")
    bits = devices.bit_length() - 1
    head_bits = heads.bit_length() - 1
    head_basis = [2 << bit for bit in range(head_bits)]
    rank_basis = [1] + [1 << bit for bit in range(head_bits + 1, bits)]
    rank_basis[1] |= heads
    head_masks = [spanned(head_basis, s) for s in range(heads)]
    rank_masks = [spanned(rank_basis, s) for s in range(spread)]
    head_duals, rank_duals = duals(head_basis, rank_basis, devices)
    head, rank = coordinates(index, head_duals), coordinates(index, rank_duals)
    base = coordinates(rank, [sum(1 << j for j in range(levels) if rank_basis[j] >> bit & 1) for bit in range(bits)])
    half = clusters // 2
    rows = requests * group
    owned = heads * per_owner

    def over(array, bit):
        return lax.ppermute(array, "ctx", [(i, i ^ bit) for i in range(devices)])

    def pick(array, at, axis=0):
        return lax.dynamic_index_in_dim(array, at, axis, keepdims=False)

    slices = [pick(cache, head ^ s) for cache in (key_cache, value_cache) for s in range(heads)]
    slices = lax.optimization_barrier(tuple(slices))
    keys = [slices[0]] + [over(slices[s], head_masks[s]) for s in range(1, heads)]

    blocks = pick(init_centroids, head).reshape(devices, per_owner, dim)
    turned = [int(format(r, f"0{levels}b")[::-1], 2) for r in range(spread)]
    order = [rank_masks[r] ^ mask for r in turned for mask in head_masks]
    scalar_base = base.reshape(1)

    pass_flops = 4 * tok_dev * clusters * dim
    chunk_scratch = [pltpu.VMEM((half, tok_dev), F32), pltpu.VMEM((half, tok_dev), BF16)]
    sums, raised, inverse, unit_cents = call(
        lambda base_ref, *refs: first_kernel(base_ref, order, *refs),
        [
            shape((half, dim), F32),
            shape((half, tok_dev), F32),
            shape((8, tok_dev), F32),
            shape((clusters, dim), BF16),
        ],
        [scalar_base, keys[0], blocks],
        [pltpu.VMEM((clusters, dim), F32), *chunk_scratch],
        pass_flops,
        scalars=1,
    )
    values = [slices[heads]] + [over(slices[heads + s], head_masks[s]) for s in range(1, heads)]

    kept_raised, inverses = [raised], [inverse]
    for step in range(1, heads):
        sums, raised, inverse = call(
            pass_chunk,
            [
                shape((half, dim), F32 if step < heads - 1 else BF16),
                shape((half, tok_dev), F32),
                shape((8, tok_dev), F32),
            ],
            [keys[step], unit_cents, sums],
            chunk_scratch,
            pass_flops,
        )
        kept_raised.append(raised)
        inverses.append(inverse)
    send = sums
    (keep,) = call(
        functools.partial(keep_kernel, heads),
        [shape((half, dim), F32)],
        [*keys, *kept_raised, *inverses],
        [pltpu.VMEM((half, heads * tok_dev), BF16)],
        pass_flops * heads // 4,
    )
    keep, values[3] = lax.optimization_barrier((keep, values[3]))
    for level in range(levels - 1):
        total = keep + over(send, rank_basis[level]).astype(F32)
        if level < levels - 2:
            cut = total.shape[0] // 2
            keep, send = total[:cut], total[cut:].astype(BF16)
    rounded = total.astype(BF16)
    recv = over(rounded, rank_basis[levels - 1])
    (own_cents,) = call(cents_kernel, [shape(rounded.shape, BF16)], [rounded, recv])
    for level in range(levels - 2, 0, -1):
        own_cents = jnp.concatenate([own_cents, over(own_cents, rank_basis[level])])
    other_cents = over(own_cents, 1)

    tokens = heads * tok_dev
    unit_keys, raised, total = call(
        functools.partial(own_half_kernel, heads),
        [shape((tokens, dim), BF16), shape((half, tokens), F32), shape((8, tokens), F32)],
        [*keys, own_cents],
        (),
        pass_flops * heads // 4,
    )
    part = half // 2
    part_scratch = [pltpu.VMEM((part, tokens), BF16), pltpu.VMEM((part, 128), F32)]
    sent = shape((part + 16, 2 * dim), BF16)
    kept = [shape((part, 2 * dim), F32), shape((8, part), F32)]
    send, inverse, early = call(
        functools.partial(other_half_kernel, heads),
        [sent, shape((8, tokens), F32), shape((part, tokens), F32)],
        [*keys, *values, unit_keys, other_cents, total],
        [pltpu.VMEM((half, tok_dev), F32), *part_scratch],
        pass_flops * heads // 2,
    )
    later = call(
        functools.partial(part_kernel, heads, part, False),
        kept,
        [*keys, *values, raised, inverse],
        part_scratch,
        pass_flops * heads // 4,
    )
    recv = over(send, 1)
    (send,) = call(functools.partial(both_kernel, True), [sent], [*later, recv])
    (early_send,) = call(
        functools.partial(part_kernel, heads, 0, True),
        [sent],
        [*keys, *values, early, inverse],
        part_scratch,
        pass_flops * heads // 4,
    )
    keep, keep_mass = call(
        functools.partial(part_kernel, heads, 0, False),
        kept,
        [*keys, *values, raised, inverse],
        part_scratch,
        pass_flops * heads // 4,
    )
    early_recv = over(early_send, 1)
    keep, keep_mass = call(functools.partial(both_kernel, False), kept, [keep, keep_mass, early_recv])

    exact, own_queries, usable = call(
        functools.partial(exact_kernel, heads, head_masks, head_masks, per_owner),
        [shape((rows + 8, dim), F32), shape((rows, dim), F32), shape((rows, owned), F32)],
        [
            head.reshape(1),
            index.reshape(1),
            scalar_base,
            request_positions,
            block_clusters,
            *keys,
            *values,
            queries,
            chosen_clusters,
        ],
        (),
        4 * rows * heads * tok_dev * dim,
        scalars=5,
    )

    for level in range(1, levels - 1):
        recv = over(send, rank_basis[level])
        count = keep.shape[0] // 2
        keep, keep_mass, send = call(
            halve_kernel,
            [
                shape((count, 2 * dim), F32),
                shape((8, count), F32),
                shape((count + 16, 2 * dim), BF16),
            ],
            [keep, keep_mass, recv],
        )
    recv = over(send, rank_basis[levels - 1])
    state, centroids = call(
        summary_kernel,
        [shape((rows + 8, dim), F32), shape((owned, dim), F32)],
        [keep, keep_mass, recv, own_queries, usable, exact],
        (),
        4 * rows * owned * dim,
    )
    for level in range(levels - 1):
        flip = ((rank >> level) & 1).reshape(1)
        (state,) = call(
            merge_kernel,
            [shape((rows + 16, dim), BF16)],
            [flip, state, over(state, rank_basis[level])],
            scalars=1,
        )
    flip = ((rank >> (levels - 1)) & 1).reshape(1)
    centroids = centroids.reshape(heads, per_owner, dim)
    attended, *packs = call(
        last_merge_kernel,
        [shape((rows, dim), BF16)] + [shape((rows + per_owner, dim), BF16)] * (heads - 1),
        [flip, head.reshape(1), state, over(state, rank_basis[levels - 1]), centroids],
        scalars=2,
    )
    packs = [over(pack, head_masks[step]) for step, pack in enumerate(packs, 1)]
    return call(
        spread_kernel,
        [shape((heads, per_owner, dim), F32), shape(queries.shape, BF16)],
        [head.reshape(1), centroids, attended, *packs],
        scalars=1,
    )


def solution(mesh):
    placed = (
        P(None, ("groups", "ctx"), None),
        P(None, ("groups", "ctx"), None),
        P(),
        P(None, "groups"),
        P("groups", None, None),
        P("groups"),
        P("groups", None, None, None),
    )
    return jax.shard_map(
        body,
        mesh=mesh,
        in_specs=placed,
        out_specs=(P(None, ("groups", "ctx"), None), P("groups", None, None, None)),
        check_vma=False,
    )
```

```python
import functools
import math

import jax
import jax.numpy as jnp
from jax import lax
from jax.experimental import pallas as pl
from jax.experimental.pallas import tpu as pltpu
from jax.sharding import PartitionSpec as P

BLOCK = 128
SHARPNESS = 16.0
EPSILON = 1e-06
NEGATIVE = -1e30
F32 = jnp.float32
BF16 = jnp.bfloat16
VMEM_BYTES = 48 * 1024 * 1024
TILE = 256


def to_unit(vectors):
    vectors = vectors.astype(F32)
    return (
        vectors
        * lax.rsqrt(jnp.mean(vectors * vectors, axis=-1, keepdims=True) + EPSILON)
        * vectors.shape[-1] ** (-0.5)
    )


def dot_nt(left, right):
    return lax.dot_general(left, right, (((1,), (1,)), ((), ())), preferred_element_type=F32)


def spanned(basis, number):
    return functools.reduce(lambda a, b: a ^ b, [m for j, m in enumerate(basis) if number >> j & 1], 0)


def duals(head_basis, rank_basis, devices):
    basis = [*head_basis, *rank_basis]
    found = [
        next(
            f
            for f in range(devices)
            if all((f & m).bit_count() % 2 == (j == k) for j, m in enumerate(basis))
        )
        for k in range(len(basis))
    ]
    return found[: len(head_basis)], found[len(head_basis) :]


def coordinates(number, masks):
    result = 0
    for place, mask in enumerate(masks):
        for bit in range(mask.bit_length()):
            if mask >> bit & 1:
                result = result ^ ((number >> bit & 1) << place)
    return result


def call(kernel, outs, args, scratch=(), flops=0, scalars=0):
    in_specs = [pl.BlockSpec(memory_space=pltpu.SMEM)] * scalars
    in_specs += [pl.BlockSpec(memory_space=pltpu.VMEM)] * (len(args) - scalars)
    touched = sum(a.size * a.dtype.itemsize for a in (*args, *outs))
    return pl.pallas_call(
        kernel,
        out_shape=tuple(outs),
        in_specs=in_specs,
        out_specs=tuple(pl.BlockSpec(memory_space=pltpu.VMEM) for _ in outs),
        scratch_shapes=list(scratch),
        compiler_params=pltpu.CompilerParams(vmem_limit_bytes=VMEM_BYTES),
        cost_estimate=pl.CostEstimate(flops=flops, bytes_accessed=touched, transcendentals=0),
    )(*args)


def shape(dims, dtype):
    return jax.ShapeDtypeStruct(dims, dtype)


def fill_raised(piece, unit_keys, raised_ref, row, first):
    tokens = unit_keys.shape[0]
    factor = SHARPNESS * math.log2(math.e)
    total = jnp.zeros((1, tokens), F32)
    tile = min(TILE, piece.shape[0])
    for at in range(0, piece.shape[0], tile):
        raised = jnp.exp2(dot_nt(piece[at : at + tile, :], unit_keys) * factor)
        raised_ref[row + at : row + at + tile, first : first + tokens] = raised.astype(
            raised_ref.dtype
        )
        total = total + jnp.sum(raised, axis=0, keepdims=True)
    return total


def fill_weights(raised_ref, inverse, weight_ref, rows, from_row, first, raised_first, mass_ref):
    tokens = inverse.shape[1]
    tile = min(TILE, rows)
    for at in range(0, rows, tile):
        raised = raised_ref[
            from_row + at : from_row + at + tile, raised_first : raised_first + tokens
        ]
        weights = raised.astype(F32) * inverse
        weight_ref[at : at + tile, first : first + tokens] = weights.astype(BF16)
        if mass_ref is not None:
            part = weights[:, :128]
            for lane in range(128, tokens, 128):
                part = part + weights[:, lane : lane + 128]
            if first == 0:
                mass_ref[at : at + tile, :] = part
            else:
                mass_ref[at : at + tile, :] += part


def product(out_ref, weight_ref, values, sums_ref=None, row=0):
    rows = weight_ref.shape[0]
    tile = min(TILE, rows)
    for at in range(0, rows, tile):
        sums = jnp.dot(weight_ref[at : at + tile, :], values, preferred_element_type=F32)
        if sums_ref is not None:
            sums = sums + sums_ref[row + at : row + at + tile, :]
        out_ref[at : at + tile, :] = sums.astype(out_ref.dtype)


def first_kernel(
    base_ref,
    order,
    key_ref,
    cent_ref,
    sums_ref,
    keep_raised_ref,
    inverse_ref,
    unit_ref,
    cents_ref,
    raised_ref,
    weight_ref,
):
    per_owner = cent_ref.shape[1]
    for at, mask in enumerate(order):
        cents_ref[at * per_owner : (at + 1) * per_owner, :] = cent_ref[base_ref[0] ^ mask].astype(
            F32
        )
    unit_ref[...] = to_unit(cents_ref[...]).astype(BF16)
    pass_chunk(
        key_ref, unit_ref, None, sums_ref, keep_raised_ref, inverse_ref, raised_ref, weight_ref
    )


def pass_chunk(
    key_ref, unit_ref, before_ref, sums_ref, keep_raised_ref, inverse_ref, raised_ref, weight_ref
):
    keys = key_ref[...]
    half = sums_ref.shape[0]
    unit_keys = to_unit(keys).astype(BF16)
    total = fill_raised(unit_ref.at[pl.ds(0, half)], unit_keys, keep_raised_ref, 0, 0)
    total = total + fill_raised(unit_ref.at[pl.ds(half, half)], unit_keys, raised_ref, 0, 0)
    inverse = 1.0 / total
    inverse_ref[...] = jnp.broadcast_to(inverse, inverse_ref.shape)
    fill_weights(raised_ref, inverse, weight_ref, half, 0, 0, 0, None)
    product(sums_ref, weight_ref, keys, before_ref)


def keep_kernel(count, *refs):
    key_refs, raised_refs, inverse_refs = refs[:count], refs[count : 2 * count], refs[2 * count : 3 * count]
    keep_ref, weight_ref = refs[3 * count :]
    first = 0
    for raised_ref, inverse_ref in zip(raised_refs, inverse_refs):
        rows, tokens = raised_ref.shape
        fill_weights(raised_ref, inverse_ref[0:1, :], weight_ref, rows, 0, first, 0, None)
        first += tokens
    product(keep_ref, weight_ref, joined_rows(key_refs))


def joined_rows(refs):
    return jnp.concatenate([ref[...] for ref in refs], axis=0)


def joined_pairs(key_refs, value_refs):
    return jnp.concatenate(
        [jnp.concatenate([k[...], v[...]], axis=1) for k, v in zip(key_refs, value_refs)], axis=0
    )


def packed_masses(row, lanes):
    count = row.shape[1]
    high = row.astype(BF16).astype(F32)
    low = row - high
    rows = []
    for part in (high, low):
        if count < lanes:
            rows.append(jnp.concatenate([part, jnp.zeros((1, lanes - count), F32)], axis=1))
        else:
            rows += [part[:, at : at + lanes] for at in range(0, count, lanes)]
    rows.append(jnp.zeros((16 - len(rows), lanes), F32))
    return jnp.concatenate(rows, axis=0).astype(BF16)


def unpacked_masses(block, count):
    block = block.astype(F32)
    lanes = block.shape[1]
    if count < lanes:
        return block[0:1, :count] + block[1:2, :count]
    rows = count // lanes
    return jnp.concatenate(
        [block[i : i + 1, :] + block[rows + i : rows + i + 1, :] for i in range(rows)], axis=1
    )


def cents_kernel(own_ref, recv_ref, out_ref):
    half = own_ref.shape[0] // 2
    for at in (0, half):
        recv = recv_ref[half - at : 2 * half - at, :]
        sums = own_ref[at : at + half, :].astype(F32) + recv.astype(F32)
        out_ref[at : at + half, :] = to_unit(sums).astype(BF16)


def own_half_kernel(count, *refs):
    key_refs, (cent_ref, unit_ref, raised_ref, total_ref) = refs[:count], refs[count:]
    first = 0
    for key_ref in key_refs:
        unit_keys = to_unit(key_ref[...]).astype(BF16)
        tokens = unit_keys.shape[0]
        unit_ref[first : first + tokens, :] = unit_keys
        total = fill_raised(cent_ref, unit_keys, raised_ref, 0, first)
        total_ref[:, first : first + tokens] = jnp.broadcast_to(total, (8, tokens))
        first += tokens


def other_half_kernel(count, *refs):
    pair_refs, refs = refs[: 2 * count], refs[2 * count :]
    unit_ref, cent_ref, total_ref, send_ref, inverse_ref, early_ref = refs[:6]
    raised_ref, weight_ref, mass_ref = refs[6:]
    rows, lanes = early_ref.shape[0], send_ref.shape[1]
    first = 0
    for key_ref in pair_refs[:count]:
        tokens = key_ref.shape[0]
        chunk = slice(first, first + tokens)
        unit_keys = unit_ref[chunk, :]
        total = total_ref[0:1, chunk] + fill_raised(
            cent_ref.at[pl.ds(0, rows)], unit_keys, early_ref, 0, first
        )
        total = total + fill_raised(cent_ref.at[pl.ds(rows, rows)], unit_keys, raised_ref, 0, 0)
        inverse = 1.0 / total
        inverse_ref[:, chunk] = jnp.broadcast_to(inverse, (8, tokens))
        fill_weights(raised_ref, inverse, weight_ref, rows, 0, first, 0, mass_ref)
        first += tokens
    masses = jnp.sum(mass_ref[...].T, axis=0, keepdims=True)
    send_ref[rows:, :] = packed_masses(masses, lanes)
    product(send_ref, weight_ref, joined_pairs(pair_refs[:count], pair_refs[count:]))


def part_kernel(count, row, to_send, *refs):
    pair_refs, refs = refs[: 2 * count], refs[2 * count :]
    raised_ref, inverse_ref, refs = refs[0], refs[1], refs[2:]
    out_ref, (weight_ref, mass_ref) = refs[0], refs[-2:]
    rows = weight_ref.shape[0]
    first = 0
    for key_ref in pair_refs[:count]:
        tokens = key_ref.shape[0]
        inverse = inverse_ref[0:1, first : first + tokens]
        fill_weights(raised_ref, inverse, weight_ref, rows, row, first, first, mass_ref)
        first += tokens
    masses = jnp.sum(mass_ref[...].T, axis=0, keepdims=True)
    if to_send:
        out_ref[rows:, :] = packed_masses(masses, out_ref.shape[1])
    else:
        refs[1][...] = jnp.broadcast_to(masses, refs[1].shape)
    product(out_ref, weight_ref, joined_pairs(pair_refs[:count], pair_refs[count:]))


def both_kernel(to_send, keep_ref, mass_ref, recv_ref, out_ref, *refs):
    count, lanes = keep_ref.shape
    masses = mass_ref[0:1, :] + unpacked_masses(recv_ref[count:, :], count)
    sums = keep_ref[...] + recv_ref[:count, :].astype(F32)
    out_ref[:count, :] = sums.astype(out_ref.dtype)
    if to_send:
        out_ref[count:, :] = packed_masses(masses, lanes)
    else:
        refs[0][...] = jnp.broadcast_to(masses, refs[0].shape)


def halve_kernel(keep_ref, mass_ref, recv_ref, keep_out_ref, mass_out_ref, send_ref):
    count, lanes = keep_ref.shape
    half = count // 2
    masses = mass_ref[0:1, :] + unpacked_masses(recv_ref[count:, :], count)
    keep_out_ref[...] = keep_ref[:half, :] + recv_ref[:half, :].astype(F32)
    mass_out_ref[...] = jnp.broadcast_to(masses[:, :half], mass_out_ref.shape)
    send_ref[:half, :] = (keep_ref[half:, :] + recv_ref[half:count, :].astype(F32)).astype(BF16)
    send_ref[half:, :] = packed_masses(masses[:, half:], lanes)


def as_line(column, dim):
    rows = column.shape[0]
    square = [jnp.broadcast_to(column, (rows, dim)), jnp.zeros((dim - rows, dim), F32)]
    return jnp.concatenate(square, axis=0).T[0:1, :]


def packed_state(peak, weight_sum, weighted):
    dim = weighted.shape[1]
    lines = [as_line(peak, dim), as_line(weight_sum, dim), jnp.zeros((6, dim), F32)]
    return jnp.concatenate([weighted, *lines], axis=0)


def sent_state(peak, weight_sum, weighted):
    dim = weighted.shape[1]
    lines = []
    for column in (peak, weight_sum):
        rest = as_line(column, dim)
        for _ in range(3):
            lines.append(rest.astype(BF16).astype(F32))
            rest = rest - lines[-1]
    lines.append(jnp.zeros((10, dim), F32))
    return jnp.concatenate([weighted, *lines], axis=0).astype(BF16)


def softmax_part(scores, usable, values):
    peak = jnp.max(jnp.where(usable, scores, NEGATIVE), axis=1, keepdims=True)
    probability = jnp.where(usable, jnp.exp(scores - peak), 0.0).astype(BF16)
    weight_sum = jnp.sum(probability.astype(F32), axis=1, keepdims=True)
    return peak, weight_sum, jnp.dot(probability, values, preferred_element_type=F32)


def joined(former, latter):
    peak = jnp.maximum(former[0], latter[0])
    left, right = jnp.exp(former[0] - peak), jnp.exp(latter[0] - peak)
    return (
        peak,
        former[1] * left + latter[1] * right,
        former[2] * left + latter[2] * right,
    )


def unpacked_state(state):
    dim = state.shape[1]
    short = state.dtype == BF16
    rows = state.shape[0] - (16 if short else 8)
    state = state.astype(F32)
    lines = [state[at : at + 1, :] for at in range(rows, rows + (6 if short else 2))]
    if short:
        lines = [lines[at] + lines[at + 1] + lines[at + 2] for at in (0, 3)]
    columns = [jnp.broadcast_to(line, (dim, dim)).T[:rows, :] for line in lines]
    return columns[0], columns[1], state[:rows, :]


def exact_kernel(count, head_masks, owned_by, per_owner, *refs):
    scalar_refs, key_refs, value_refs = (
        refs[:5],
        refs[5 : 5 + count],
        refs[5 + count : 5 + 2 * count],
    )
    head_ref, index_ref, base_ref, position_ref, cluster_ref = scalar_refs
    query_ref, chosen_ref, out_ref, own_query_ref, usable_ref = refs[5 + 2 * count :]
    head, index, base = head_ref[0], index_ref[0], base_ref[0]
    requests, _, group, dim = query_ref.shape
    rows = requests * group
    for r in range(requests):
        own_query_ref[r * group : (r + 1) * group, :] = query_ref[r, head].astype(F32)
    queries = own_query_ref[...].astype(BF16)
    ksel = chosen_ref.shape[2]
    chosen = jnp.concatenate(
        [
            jnp.broadcast_to(chosen_ref[r, pl.ds(head, 1), :], (group, ksel))
            for r in range(requests)
        ],
        axis=0,
    )
    positions = jnp.concatenate(
        [jnp.full((group, 1), position_ref[r], jnp.int32) for r in range(requests)], axis=0
    )
    lane = lax.broadcasted_iota(jnp.int32, (rows, BLOCK), 1)
    blocks = key_refs[0].shape[0] // BLOCK
    parts = []
    for mask in head_masks:
        for block in range(blocks):
            at = (index ^ mask) * blocks + block
            picked = jnp.max(
                jnp.where(chosen == cluster_ref[head, at], 1, 0).astype(F32), axis=1, keepdims=True
            )
            limit = jnp.where(picked > 0.5, positions - at * BLOCK, 0)
            parts.append(jnp.where(lane < limit, 1.0, 0.0))
    scores = dot_nt(queries, joined_rows(key_refs)) * dim ** (-0.5)
    usable = jnp.concatenate(parts, axis=1) > 0.5
    out_ref[...] = packed_state(*softmax_part(scores, usable, joined_rows(value_refs)))
    owned = usable_ref.shape[1]
    place = lax.broadcasted_iota(jnp.int32, (rows, owned), 1)
    ids = place
    for part, mask in enumerate(owned_by):
        shift = (base ^ mask) * per_owner - part * per_owner
        ids = jnp.where((place >= part * per_owner) & (place < (part + 1) * per_owner), place + shift, ids)
    free = jnp.ones((rows, owned), F32)
    for k in range(ksel):
        free = jnp.where(chosen[:, k : k + 1] == ids, 0.0, free)
    usable_ref[...] = free


def summary_kernel(
    keep_ref, mass_ref, recv_ref, query_ref, usable_ref, exact_ref, state_ref, cent_ref
):
    count, lanes = keep_ref.shape
    dim = lanes // 2
    masses = mass_ref[0:1, :] + unpacked_masses(recv_ref[count:, :], count)
    sums = keep_ref[...] + recv_ref[:count, :].astype(F32)
    cent_ref[...] = to_unit(sums[:, :dim])
    column = jnp.broadcast_to(masses, (dim, count)).T
    mean_keys = (sums[:, :dim] / column).astype(BF16)
    mean_values = (sums[:, dim:] / column).astype(BF16)
    queries = query_ref[...].astype(BF16)
    scores = dot_nt(queries, mean_keys) * dim ** (-0.5) + jnp.log(masses)
    state = softmax_part(scores, usable_ref[...] > 0.5, mean_values)
    state_ref[...] = packed_state(*joined(unpacked_state(exact_ref[...]), state))


def in_order(flip, own_ref, recv_ref):
    own, recv = own_ref[...], recv_ref[...]
    return jnp.where(flip, recv, own), jnp.where(flip, own, recv)


def merge_kernel(flip_ref, own_ref, recv_ref, out_ref):
    former, latter = in_order(flip_ref[0] != 0, own_ref, recv_ref)
    out_ref[...] = sent_state(*joined(unpacked_state(former), unpacked_state(latter)))


def last_merge_kernel(flip_ref, head_ref, own_ref, recv_ref, cent_ref, attended_ref, *pack_refs):
    former, latter = in_order(flip_ref[0] != 0, own_ref, recv_ref)
    _, weight_sum, weighted = joined(unpacked_state(former), unpacked_state(latter))
    attended = (weighted / weight_sum).astype(BF16)
    attended_ref[...] = attended
    rows = attended.shape[0]
    for step, pack_ref in enumerate(pack_refs, 1):
        pack_ref[:rows, :] = attended
        pack_ref[rows:, :] = cent_ref[head_ref[0] ^ step].astype(BF16)


def spread_kernel(head_ref, own_cent_ref, attended_ref, *refs):
    pack_refs, (cent_ref, out_ref) = refs[:-2], refs[-2:]
    own = head_ref[0]
    requests, _, group, _ = out_ref.shape
    rows = requests * group
    cent_ref[own] = own_cent_ref[own]
    for step, pack_ref in enumerate((attended_ref, *pack_refs)):
        attended = pack_ref[:rows, :].astype(F32)
        if step:
            cent_ref[own ^ step] = pack_ref[rows:, :].astype(F32)
        for r in range(requests):
            out_ref[r, own ^ step] = attended[r * group : (r + 1) * group, :].astype(BF16)


def body(
    key_cache,
    value_cache,
    init_centroids,
    block_clusters,
    chosen_clusters,
    request_positions,
    queries,
):
    devices = lax.axis_size("ctx")
    index = lax.axis_index("ctx").astype(jnp.int32)
    heads, tok_dev, dim = key_cache.shape
    clusters = init_centroids.shape[1]
    requests, _, group, _ = queries.shape
    per_owner = clusters // devices
    spread = devices // heads
    levels = spread.bit_length() - 1
    if heads * spread != devices or 1 << levels != spread or heads & (heads - 1) or levels < 2:
        raise ValueError("unsupported mesh")
    bits = devices.bit_length() - 1
    head_bits = heads.bit_length() - 1
    head_basis = [2 << bit for bit in range(head_bits)]
    rank_basis = [1] + [1 << bit for bit in range(head_bits + 1, bits)]
    rank_basis[1] |= heads
    head_masks = [spanned(head_basis, s) for s in range(heads)]
    rank_masks = [spanned(rank_basis, s) for s in range(spread)]
    head_duals, rank_duals = duals(head_basis, rank_basis, devices)
    head, rank = coordinates(index, head_duals), coordinates(index, rank_duals)
    base = coordinates(rank, [sum(1 << j for j in range(levels) if rank_basis[j] >> bit & 1) for bit in range(bits)])
    half = clusters // 2
    rows = requests * group
    owned = heads * per_owner

    def over(array, bit):
        return lax.ppermute(array, "ctx", [(i, i ^ bit) for i in range(devices)])

    def pick(array, at, axis=0):
        return lax.dynamic_index_in_dim(array, at, axis, keepdims=False)

    slices = [pick(cache, head ^ s) for cache in (key_cache, value_cache) for s in range(heads)]
    slices = lax.optimization_barrier(tuple(slices))
    keys = [slices[0]] + [over(slices[s], head_masks[s]) for s in range(1, heads)]

    blocks = pick(init_centroids, head).reshape(devices, per_owner, dim)
    turned = [int(format(r, f"0{levels}b")[::-1], 2) for r in range(spread)]
    order = [rank_masks[r] ^ mask for r in turned for mask in head_masks]
    scalar_base = base.reshape(1)

    pass_flops = 4 * tok_dev * clusters * dim
    chunk_scratch = [pltpu.VMEM((half, tok_dev), F32), pltpu.VMEM((half, tok_dev), BF16)]
    sums, raised, inverse, unit_cents = call(
        lambda base_ref, *refs: first_kernel(base_ref, order, *refs),
        [
            shape((half, dim), F32),
            shape((half, tok_dev), F32),
            shape((8, tok_dev), F32),
            shape((clusters, dim), BF16),
        ],
        [scalar_base, keys[0], blocks],
        [pltpu.VMEM((clusters, dim), F32), *chunk_scratch],
        pass_flops,
        scalars=1,
    )
    values = [slices[heads]] + [over(slices[heads + s], head_masks[s]) for s in range(1, heads)]

    kept_raised, inverses = [raised], [inverse]
    for step in range(1, heads):
        sums, raised, inverse = call(
            pass_chunk,
            [
                shape((half, dim), F32 if step < heads - 1 else BF16),
                shape((half, tok_dev), F32),
                shape((8, tok_dev), F32),
            ],
            [keys[step], unit_cents, sums],
            chunk_scratch,
            pass_flops,
        )
        kept_raised.append(raised)
        inverses.append(inverse)
    send = sums
    (keep,) = call(
        functools.partial(keep_kernel, heads),
        [shape((half, dim), F32)],
        [*keys, *kept_raised, *inverses],
        [pltpu.VMEM((half, heads * tok_dev), BF16)],
        pass_flops * heads // 4,
    )
    keep, values[3] = lax.optimization_barrier((keep, values[3]))
    for level in range(levels - 1):
        total = keep + over(send, rank_basis[level]).astype(F32)
        if level < levels - 2:
            cut = total.shape[0] // 2
            keep, send = total[:cut], total[cut:].astype(BF16)
    rounded = total.astype(BF16)
    recv = over(rounded, rank_basis[levels - 1])
    (own_cents,) = call(cents_kernel, [shape(rounded.shape, BF16)], [rounded, recv])
    for level in range(levels - 2, 0, -1):
        own_cents = jnp.concatenate([own_cents, over(own_cents, rank_basis[level])])
    other_cents = over(own_cents, 1)

    tokens = heads * tok_dev
    unit_keys, raised, total = call(
        functools.partial(own_half_kernel, heads),
        [shape((tokens, dim), BF16), shape((half, tokens), F32), shape((8, tokens), F32)],
        [*keys, own_cents],
        (),
        pass_flops * heads // 4,
    )
    part = half // 2
    part_scratch = [pltpu.VMEM((part, tokens), BF16), pltpu.VMEM((part, 128), F32)]
    sent = shape((part + 16, 2 * dim), BF16)
    kept = [shape((part, 2 * dim), F32), shape((8, part), F32)]
    send, inverse, early = call(
        functools.partial(other_half_kernel, heads),
        [sent, shape((8, tokens), F32), shape((part, tokens), F32)],
        [*keys, *values, unit_keys, other_cents, total],
        [pltpu.VMEM((part, tok_dev), F32), *part_scratch],
        pass_flops * heads // 2,
    )
    later = call(
        functools.partial(part_kernel, heads, part, False),
        kept,
        [*keys, *values, raised, inverse],
        part_scratch,
        pass_flops * heads // 4,
    )
    recv = over(send, 1)
    (send,) = call(functools.partial(both_kernel, True), [sent], [*later, recv])
    (early_send,) = call(
        functools.partial(part_kernel, heads, 0, True),
        [sent],
        [*keys, *values, early, inverse],
        part_scratch,
        pass_flops * heads // 4,
    )
    keep, keep_mass = call(
        functools.partial(part_kernel, heads, 0, False),
        kept,
        [*keys, *values, raised, inverse],
        part_scratch,
        pass_flops * heads // 4,
    )
    early_recv = over(early_send, 1)
    keep, keep_mass = call(functools.partial(both_kernel, False), kept, [keep, keep_mass, early_recv])

    exact, own_queries, usable = call(
        functools.partial(exact_kernel, heads, head_masks, head_masks, per_owner),
        [shape((rows + 8, dim), F32), shape((rows, dim), F32), shape((rows, owned), F32)],
        [
            head.reshape(1),
            index.reshape(1),
            scalar_base,
            request_positions,
            block_clusters,
            *keys,
            *values,
            queries,
            chosen_clusters,
        ],
        (),
        4 * rows * heads * tok_dev * dim,
        scalars=5,
    )

    for level in range(1, levels - 1):
        recv = over(send, rank_basis[level])
        count = keep.shape[0] // 2
        keep, keep_mass, send = call(
            halve_kernel,
            [
                shape((count, 2 * dim), F32),
                shape((8, count), F32),
                shape((count + 16, 2 * dim), BF16),
            ],
            [keep, keep_mass, recv],
        )
    recv = over(send, rank_basis[levels - 1])
    state, centroids = call(
        summary_kernel,
        [shape((rows + 8, dim), F32), shape((owned, dim), F32)],
        [keep, keep_mass, recv, own_queries, usable, exact],
        (),
        4 * rows * owned * dim,
    )
    for level in range(levels - 1):
        flip = ((rank >> level) & 1).reshape(1)
        (state,) = call(
            merge_kernel,
            [shape((rows + 16, dim), BF16)],
            [flip, state, over(state, rank_basis[level])],
            scalars=1,
        )
    flip = ((rank >> (levels - 1)) & 1).reshape(1)
    centroids = centroids.reshape(heads, per_owner, dim)
    attended, *packs = call(
        last_merge_kernel,
        [shape((rows, dim), BF16)] + [shape((rows + per_owner, dim), BF16)] * (heads - 1),
        [flip, head.reshape(1), state, over(state, rank_basis[levels - 1]), centroids],
        scalars=2,
    )
    packs = [over(pack, head_masks[step]) for step, pack in enumerate(packs, 1)]
    return call(
        spread_kernel,
        [shape((heads, per_owner, dim), F32), shape(queries.shape, BF16)],
        [head.reshape(1), centroids, attended, *packs],
        scalars=1,
    )


def solution(mesh):
    placed = (
        P(None, ("groups", "ctx"), None),
        P(None, ("groups", "ctx"), None),
        P(),
        P(None, "groups"),
        P("groups", None, None),
        P("groups"),
        P("groups", None, None, None),
    )
    return jax.shard_map(
        body,
        mesh=mesh,
        in_specs=placed,
        out_specs=(P(None, ("groups", "ctx"), None), P("groups", None, None, None)),
        check_vma=False,
    )
```
